256 devices in a mesh: row: 16 (over y_hi, x, core), col: 16 (over y_lo, z).
Axes of the slice: x: 4, y: 4 (y_hi: 2, y_lo: 2; y = y_hi * 2 + y_lo), z: 8, core: 2. Of those that a mesh axis runs over, the one named last changes fastest.
Arguments:
- pair: bfloat16 [96, 1536, 128], P('row', 'col'), may hold values from -6 to 6
- w_qkvg: bfloat16 [128, 256], replicated, may hold values from -0.5 to 0.5
- w_out: bfloat16 [64, 128], replicated, may hold values from -0.75 to 0.75
- bias: bfloat16 [2, 1536, 1536], P(None, 'col', 'row'), may hold values from -25 to 300
- chain_lengths: int32 [8], replicated, may hold values from 1 to 192, 960 in all
- d_pair_out: bfloat16 [96, 1536, 128], P('row', 'col'), may hold values from -6 to 6
Outputs:
- d_pair: bfloat16 [96, 1536, 128], P('row', 'col')
- d_bias: float32 [2, 1536, 1536], P(None, 'col', 'row')
The draws below stay inside these ranges and needn't reach their ends.
Inputs may be any that keep to these rules, and one draw needn't show every extreme that they name: Chain c owns token slots c * 192 to (c + 1) * 192 - 1, of which the first chain_lengths[c] are valid; the lengths sum to 960, and some chain fills all its 192 slots.
All inputs are finite; a program needn't handle non-finite values.
Results may differ from the reference program's by a relative error of at most 0.023.
Values may be sent and summed in bfloat16 or wider, within the bound.
No kernel may reach another device: no remote copies, remote signals or barrier semaphores. Data moves between devices by JAX's collectives and lax.ppermute only.
A program may use at most 64 MiB of HBM per device.

```python
import math
import jax
import jax.numpy as jnp
import numpy as np
from jax import lax

C = 128
H = 2
DH = 32
CHAINS = 8
N = 1536
IB = 96
SLOT = 192
VALID = 960


def draw_bias(key, part):
    key = jax.random.fold_in(key, 7)
    base_key = jax.random.fold_in(key, 0)
    logits = 1.5 * jax.random.normal(base_key, (H, N, N), jnp.float32)
    logits = jnp.clip(logits, -9.0, 9.0)
    return logits.astype(jnp.bfloat16)


def block_scale(stream_key, shape, shards, low, top_value):
    def one(dim, blocks):
        draws = jax.random.uniform(jax.random.fold_in(jax.random.fold_in(stream_key, 6), dim), (blocks,), jnp.float32, low / len(shards), top_value / len(shards))
        return jnp.repeat(jnp.exp(draws), shape[dim] // blocks).reshape((-1,) + (1,) * (len(shape) - dim - 1))

    loudness = one(*shards[0])
    for cut in shards[1:]:
        loudness = loudness * one(*cut)
    return loudness


def length_profile(count, total, limit, slope):
    loads = [(1 << 20) // math.isqrt(grade ** slope) + 1 for grade in range(2, count + 1)]
    spare, holding = total - limit - (count - 1), [1] * (count - 1)
    while spare > 0:
        free = [i for i in range(count - 1) if holding[i] < limit]
        mass, budget = sum([loads[i] for i in free]), spare
        for i in free:
            addition = min(limit - holding[i], max(1, budget * loads[i] // mass), spare)
            holding[i] = holding[i] + addition
            spare = spare - addition
    return np.array([limit] + holding)


def ragged(key, amount, total, most, lean):
    if amount == 2:
        one = jax.random.randint(key, (), max(1, total - most), min(most, total - 1) + 1)
        return jnp.stack([one, total - one])
    tallies = jnp.asarray(length_profile(amount, total, most, lean), jnp.int32)
    couples = (amount - 1) // 2
    donor, taker = tallies[1:1 + 2 * couples:2], tallies[2:2 + 2 * couples:2]
    slack = jnp.minimum(donor - 1, most - taker)
    passed = jax.random.randint(jax.random.fold_in(key, 1), (couples,), 0, 1 << 20) % (slack + 1)
    tallies = tallies.at[1:1 + 2 * couples:2].set(donor - passed).at[2:2 + 2 * couples:2].set(taker + passed)
    return tallies[jax.random.permutation(jax.random.fold_in(key, 2), amount)]


def noise(key, extent, deviation, reach, cuts=(), kind=jnp.bfloat16):
    gain = block_scale(key, extent, cuts, -0.22, 0.18) if cuts else 1.0
    array = jax.random.normal(key, extent, jnp.float32) * deviation * gain
    return jnp.minimum(jnp.maximum(array, -reach), reach).astype(kind)


def setup_inputs(seed: int = 0) -> dict:
    key_list = jax.random.split(jax.random.key(seed), 7)
    pair = noise(key_list[0], (IB, N, C), 1.0, 6.0, ((0, 16), (1, 16)))
    w_qkvg = noise(key_list[1], (C, 4 * H * DH), C ** -0.5, 0.5)
    w_out = noise(key_list[2], (H * DH, C), (H * DH) ** -0.5, 0.75)
    bias = draw_bias(jax.random.fold_in(key_list[6], 71), 0)
    chain_lengths = ragged(key_list[4], CHAINS, VALID, SLOT, 1).astype(jnp.int32)
    d_pair_out = noise(key_list[5], (IB, N, C), 1.0, 6.0, ((0, 16), (1, 16)))
    return dict(pair=pair, w_qkvg=w_qkvg, w_out=w_out, bias=bias, chain_lengths=chain_lengths, d_pair_out=d_pair_out)


MASKED_SCORE = -1e+30

def rounded_wide(values):
    return lax.optimization_barrier(values.astype(jnp.bfloat16)).astype(jnp.float32)

def key_mask(chain_lengths):
    position = jnp.arange(N, dtype=jnp.int32)
    chain_index = position // SLOT
    chosen = chain_index[:, None] == jnp.arange(CHAINS, dtype=jnp.int32)[None, :]
    chain_size = lax.optimization_barrier(jnp.sum(jnp.where(chosen, chain_lengths[None, :], 0), axis=1))
    return position % SLOT < chain_size

def reference(pair, w_qkvg, w_out, bias, chain_lengths, d_pair_out):
    head_span = H * DH
    score_scale = 1.0 / math.sqrt(DH)
    key_valid = key_mask(chain_lengths)
    bias_wide = bias.astype(jnp.float32)

    def row_step(d_bias, inputs):
        pair_row, grad_row = inputs
        projected = jnp.dot(pair_row, w_qkvg, preferred_element_type=jnp.float32)
        queries = rounded_wide(projected[:, :head_span] * score_scale).reshape(N, H, DH)
        keys = rounded_wide(projected[:, head_span:2 * head_span]).reshape(N, H, DH)
        values = rounded_wide(projected[:, 2 * head_span:3 * head_span]).reshape(N, H, DH)
        gates = jax.nn.sigmoid(projected[:, 3 * head_span:])
        scores = jnp.einsum('jhd,khd->hjk', queries, keys) + bias_wide
        scores = jnp.where(key_valid[None, None, :], scores, MASKED_SCORE)
        highest = lax.optimization_barrier(jnp.max(scores, axis=2, keepdims=True))
        exponent = jnp.exp(scores - highest)
        weights = exponent / lax.optimization_barrier(jnp.sum(exponent, axis=2, keepdims=True))
        attention = jnp.einsum('hjk,khd->jhd', weights, values, precision=lax.Precision.HIGHEST).reshape(N, head_span)
        d_output = jnp.dot(grad_row, w_out.T, preferred_element_type=jnp.float32)
        d_attention = rounded_wide(d_output * gates)
        row_dot = lax.optimization_barrier(jnp.sum((d_attention * attention).reshape(N, H, DH), axis=2)).T
        d_weights = jnp.einsum('jhd,khd->hjk', d_attention.reshape(N, H, DH), values)
        d_scores = weights * (d_weights - row_dot[:, :, None])
        d_scores_low = rounded_wide(d_scores)
        weights_low = rounded_wide(weights)
        d_queries = jnp.einsum('hjk,khd->jhd', d_scores_low, keys) * score_scale
        d_keys = jnp.einsum('hjk,jhd->khd', d_scores_low, queries)
        d_values = jnp.einsum('hjk,jhd->khd', weights_low, d_attention.reshape(N, H, DH))
        d_gates = d_output * attention * gates * (1.0 - gates)
        d_projected = jnp.concatenate([d_queries.reshape(N, head_span), d_keys.reshape(N, head_span), d_values.reshape(N, head_span), d_gates], axis=1).astype(jnp.bfloat16)
        d_pair_row = jnp.dot(d_projected, w_qkvg.T, preferred_element_type=jnp.float32).astype(jnp.bfloat16)
        return (d_bias + d_scores, d_pair_row)
    d_bias, d_pair = lax.scan(row_step, jnp.zeros((H, N, N), jnp.float32), (pair, d_pair_out))
    return (d_pair, d_bias)
```

```python
import functools
import math

import jax
import jax.numpy as jnp
from jax import lax
from jax.experimental import pallas as pl
from jax.experimental.pallas import tpu as pltpu
from jax.sharding import Mesh, PartitionSpec as P

H = 2
DH = 32
CHAINS = 8
SCALE = 1.0 / math.sqrt(DH)
MASKED_SCORE = -1e30
F32 = jnp.float32
BF16 = jnp.bfloat16

ROWS = 6
COLS = 96
RING = 8
HALF = RING * COLS
KEYS = 2 * HALF
WIDE = 128
SLOT = KEYS // CHAINS

NT = (((1,), (1,)), ((), ()))
NN = (((1,), (0,)), ((), ()))
TN = (((0,), (0,)), ((), ()))


def mm(a, b, dims):
    return lax.dot_general(a, b, dims, preferred_element_type=F32)


def params(limit=48 << 20):
    return pltpu.CompilerParams(vmem_limit_bytes=limit)


def cost(flops, size):
    return pl.CostEstimate(flops=flops, bytes_accessed=size, transcendentals=0)


def lanes(shape):
    return lax.broadcasted_iota(jnp.int32, shape, len(shape) - 1)


def head_weight(w, h):
    parts = [w[:, (part * H + h) * DH : (part * H + h + 1) * DH] for part in (1, 2, 0, 3)]
    return jnp.concatenate(parts, axis=1)


def project_kernel(pair_ref, grad_ref, w_ref, wout_ref, mine_ref, other_ref, gmine_ref, gother_ref):
    yl = lax.axis_index("yl")
    pair = pair_ref[...].reshape(ROWS * COLS, WIDE)
    grad = grad_ref[...].reshape(ROWS * COLS, WIDE)
    w = w_ref[...]
    wout = wout_ref[...]
    lane = lanes((ROWS * COLS, WIDE))
    for h in range(H):
        proj = mm(pair, head_weight(w, h), NN)
        rows = jnp.concatenate(
            [jnp.zeros((WIDE - DH, WIDE), BF16), wout[h * DH : (h + 1) * DH]], axis=0
        )
        d_out = mm(grad, rows, NT)
        gate = jax.nn.sigmoid(proj)
        payload = jnp.where(
            lane < 2 * DH, proj, jnp.where(lane < 3 * DH, proj * SCALE, d_out * gate)
        )
        payload = payload.astype(BF16).reshape(ROWS, COLS, WIDE)
        g = (d_out * gate * (1.0 - gate)).reshape(ROWS, COLS, WIDE)

        @pl.when(yl == h)
        def _():
            mine_ref[...] = payload
            gmine_ref[...] = g

        @pl.when(yl != h)
        def _():
            other_ref[...] = payload
            gother_ref[...] = g


def project(pair, grad, w, wout):
    shape = (ROWS, COLS, WIDE)
    return pl.pallas_call(
        project_kernel,
        out_shape=[
            jax.ShapeDtypeStruct(shape, BF16),
            jax.ShapeDtypeStruct(shape, BF16),
            jax.ShapeDtypeStruct(shape, F32),
            jax.ShapeDtypeStruct(shape, F32),
        ],
        compiler_params=params(),
        name="project",
    )(pair, grad, w, wout)


def pack_kernel(mine_ref, recv_ref, kv_ref, x0_ref, x1_ref):
    yl = lax.axis_index("yl")
    lane = lanes((COLS, WIDE))

    def write(i, a, b):
        x0_ref[i] = a
        x1_ref[i] = b
        moved = pltpu.roll(b.astype(F32), 2 * DH, 1)
        kv_ref[i] = jnp.where(lane < 2 * DH, a.astype(F32), moved).astype(BF16)

    for i in range(ROWS):

        @pl.when(yl == 0)
        def _():
            write(i, mine_ref[i], recv_ref[i])

        @pl.when(yl != 0)
        def _():
            write(i, recv_ref[i], mine_ref[i])


def pack(mine, recv):
    shape = jax.ShapeDtypeStruct((ROWS, COLS, WIDE), BF16)
    return pl.pallas_call(
        pack_kernel, out_shape=[shape] * 3, compiler_params=params(), name="pack"
    )(mine, recv)


def bias_kernel(len_ref, own_ref, oth_ref, out_ref):
    core = lax.axis_index("core")
    lane = lanes((1, SLOT))

    def write(even, odd):
        for yh in range(2):
            for x in range(4):
                valid = lane < len_ref[yh * 4 + x]
                lift = jnp.where(valid, 0.0, MASKED_SCORE)
                for yl in range(2):
                    both = jnp.concatenate(
                        [even[yh, x, yl].astype(F32), odd[yh, x, yl].astype(F32)], axis=1
                    )
                    start = yh * HALF + x * SLOT
                    out_ref[yl * COLS : (yl + 1) * COLS, start : start + SLOT] = both + lift

    @pl.when(core == 0)
    def _():
        write(own_ref, oth_ref)

    @pl.when(core != 0)
    def _():
        write(oth_ref, own_ref)


def bias_table(chain_lengths, own, oth):
    return pl.pallas_call(
        bias_kernel,
        out_shape=jax.ShapeDtypeStruct((2 * COLS, KEYS), F32),
        in_specs=[
            pl.BlockSpec(memory_space=pltpu.SMEM),
            pl.BlockSpec(memory_space=pltpu.VMEM),
            pl.BlockSpec(memory_space=pltpu.VMEM),
        ],
        compiler_params=params(),
        name="bias_table",
    )(chain_lengths, own, oth)


def masked(value, lane, part):
    keep = (lane >= part * DH) & (lane < (part + 1) * DH)
    return jnp.where(keep, value, jnp.zeros_like(value))


def main_kernel(x0_ref, x1_ref, bias_ref, *refs):
    kv_refs = refs[:RING]
    u_ref, dkv_refs, dbias_ref = refs[RING], refs[RING + 1 : 2 * RING + 1], refs[2 * RING + 1]
    kv_s, left, right, dkv_s = refs[2 * RING + 2 :]
    z = lax.axis_index("z")
    i = pl.program_id(0)
    for r in range(RING):
        start = pl.multiple_of(lax.rem(z + r, RING) * COLS, COLS)
        kv_s[pl.ds(start, COLS), :] = kv_refs[r][0]
    kv = kv_s[...]
    lane = lanes((COLS, WIDE))

    @pl.when(i == 0)
    def _():
        dbias_ref[...] = jnp.zeros_like(dbias_ref)

    for part, x_ref in enumerate((x0_ref, x1_ref)):
        x = x_ref[0]
        y = pltpu.roll(x.astype(F32), 2 * DH, 1).astype(BF16)
        q0, da0 = masked(y, lane, 0), masked(y, lane, 1)
        q1, da1 = masked(x, lane, 2), masked(x, lane, 3)
        rows = slice(part * COLS, (part + 1) * COLS)
        s0 = mm(q0, kv, NT) + bias_ref[rows, :HALF]
        s1 = mm(q1, kv, NT) + bias_ref[rows, HALF:]
        top = jnp.maximum(
            jnp.max(s0, axis=1, keepdims=True), jnp.max(s1, axis=1, keepdims=True)
        )
        e0 = jnp.exp(s0 - top)
        e1 = jnp.exp(s1 - top)
        total = jnp.sum(e0, axis=1, keepdims=True) + jnp.sum(e1, axis=1, keepdims=True)
        inverse = 1.0 / total
        p0 = e0 * inverse
        p1 = e1 * inverse
        p0b = p0.astype(BF16)
        p1b = p1.astype(BF16)
        pv0 = mm(p0b, kv, NN)
        pv1 = mm(p1b, kv, NN)
        dot = jnp.sum(pv0 * da0.astype(F32) + pv1 * da1.astype(F32), axis=1, keepdims=True)
        d0 = p0 * (mm(da0, kv, NT) - dot)
        d1 = p1 * (mm(da1, kv, NT) - dot)
        dbias_ref[rows, :HALF] += d0
        dbias_ref[rows, HALF:] += d1
        d0b = d0.astype(BF16)
        d1b = d1.astype(BF16)
        dk0 = mm(d0b, kv, NN)
        dk1 = mm(d1b, kv, NN)
        t0 = jnp.where(lane < DH, dk0, pv0)
        t1 = jnp.where(lane < 3 * DH, dk1, pv1)
        u = t0 + pltpu.roll(t1, 2 * DH, 1)
        u_ref[part, 0] = jnp.where(lane < DH, u * SCALE, u)
        base = part * COLS
        for slot, (l_val, r_val) in enumerate(((d0b, q0), (p0b, da0), (d1b, q1), (p1b, da1))):
            left[slot * 2 * COLS + base : slot * 2 * COLS + base + COLS, :] = l_val
            right[slot * 2 * COLS + base : slot * 2 * COLS + base + COLS, :] = r_val
    dkv_s[...] = mm(left[...], right[...], TN)
    for r in range(RING):
        start = pl.multiple_of(lax.rem(z + r, RING) * COLS, COLS)
        dkv_refs[r][0] = dkv_s[pl.ds(start, COLS), :].astype(BF16)


def main(x0, x1, bias, kvs):
    row = pl.BlockSpec((1, COLS, WIDE), lambda i: (i, 0, 0))
    table = pl.BlockSpec((2 * COLS, KEYS), lambda i: (0, 0))
    block = jax.ShapeDtypeStruct((ROWS, COLS, WIDE), BF16)
    out = pl.pallas_call(
        main_kernel,
        grid=(ROWS,),
        in_specs=[row, row, table] + [row] * RING,
        out_specs=[pl.BlockSpec((2, 1, COLS, WIDE), lambda i: (0, i, 0, 0))]
        + [row] * RING
        + [table],
        out_shape=[jax.ShapeDtypeStruct((2, ROWS, COLS, WIDE), F32)]
        + [block] * RING
        + [jax.ShapeDtypeStruct((2 * COLS, KEYS), F32)],
        scratch_shapes=[
            pltpu.VMEM((HALF, WIDE), BF16),
            pltpu.VMEM((8 * COLS, HALF), BF16),
            pltpu.VMEM((8 * COLS, WIDE), BF16),
            pltpu.VMEM((HALF, WIDE), F32),
        ],
        compiler_params=params(),
        name="main",
    )(x0, x1, bias, *kvs)
    return out[0], out[1 : RING + 1], out[RING + 1]


def split_kernel(table_ref, keep_ref, send_ref):
    core = lax.axis_index("core")
    for yh in range(2):
        for x in range(4):
            for b in range(2):
                start = yh * HALF + x * SLOT + b * COLS
                for yl in range(2):

                    @pl.when(core == b)
                    def _():
                        keep_ref[yh, x, yl] = table_ref[
                            yl * COLS : (yl + 1) * COLS, start : start + COLS
                        ]

                    @pl.when(core != b)
                    def _():
                        send_ref[yh, x, yl] = table_ref[
                            yl * COLS : (yl + 1) * COLS, start : start + COLS
                        ].astype(BF16)


def split_table(table):
    shape = (2, 4, 2, COLS, COLS)
    return pl.pallas_call(
        split_kernel,
        out_shape=[jax.ShapeDtypeStruct(shape, F32), jax.ShapeDtypeStruct(shape, BF16)],
        compiler_params=params(),
        name="split_table",
    )(table)


def finish_kernel(u_ref, a_ref, b_ref, c_ref, keep_ref, send_ref):
    yl = lax.axis_index("yl")
    lane = lanes((COLS, WIDE))
    for i in range(ROWS):
        dkv = a_ref[i].astype(F32) + b_ref[i].astype(F32) + c_ref[i].astype(F32)
        first = jnp.where(lane < 2 * DH, dkv, pltpu.roll(u_ref[0, i], 2 * DH, 1))
        second = jnp.where(
            lane < 2 * DH, pltpu.roll(dkv, 2 * DH, 1), pltpu.roll(u_ref[1, i], 2 * DH, 1)
        )

        @pl.when(yl == 0)
        def _():
            keep_ref[i] = first
            send_ref[i] = second.astype(BF16)

        @pl.when(yl != 0)
        def _():
            keep_ref[i] = second
            send_ref[i] = first.astype(BF16)


def finish(u, a, b, c):
    shape = (ROWS, COLS, WIDE)
    return pl.pallas_call(
        finish_kernel,
        out_shape=[jax.ShapeDtypeStruct(shape, F32), jax.ShapeDtypeStruct(shape, BF16)],
        compiler_params=params(),
        name="finish",
    )(u, a, b, c)


def output_kernel(keep_ref, recv_ref, gmine_ref, gother_ref, w_ref, out_ref):
    yl = lax.axis_index("yl")
    flat = (ROWS * COLS, WIDE)
    lane = lanes(flat)
    keep = keep_ref[...].reshape(flat)
    recv = recv_ref[...].reshape(flat).astype(F32)
    mine = jnp.where(lane < 3 * DH, keep, keep * gmine_ref[...].reshape(flat)).astype(BF16)
    other = jnp.where(lane < 3 * DH, recv, recv * gother_ref[...].reshape(flat)).astype(BF16)
    w = w_ref[...]
    w0, w1 = head_weight(w, 0), head_weight(w, 1)

    def write(a, b):
        out_ref[...] = (mm(a, w0, NT) + mm(b, w1, NT)).astype(BF16).reshape(ROWS, COLS, WIDE)

    @pl.when(yl == 0)
    def _():
        write(mine, other)

    @pl.when(yl != 0)
    def _():
        write(other, mine)


def output(keep, recv, gmine, gother, w):
    return pl.pallas_call(
        output_kernel,
        out_shape=jax.ShapeDtypeStruct((ROWS, COLS, WIDE), BF16),
        compiler_params=params(),
        name="output",
    )(keep, recv, gmine, gother, w)


def shift(value, step):
    return lax.ppermute(value, "z", [(z, (z + step) % RING) for z in range(RING)])


def swap(value, axis):
    return lax.ppermute(value, axis, [(0, 1), (1, 0)])


def added(a, b):
    return (a.astype(F32) + b.astype(F32)).astype(BF16)


def body(pair, w_qkvg, w_out, bias, chain_lengths, d_pair_out):
    peers = ("yh", "x", "yl")
    mine, other, gmine, gother = project(pair, d_pair_out, w_qkvg, w_out)
    recv = swap(other, "yl")
    wanted = jnp.broadcast_to(bias[None], (8,) + bias.shape).reshape(16, COLS, COLS)
    own = lax.all_to_all(wanted, peers, 0, 0, tiled=True)
    oth = swap(own, "core")
    blocks = (2, 4, 2, COLS, COLS)
    table = bias_table(chain_lengths, own.reshape(blocks), oth.reshape(blocks))
    kv, x0, x1 = pack(mine, recv)
    kvs = [kv] + [None] * (RING - 1)
    up = down = kv
    for r in range(1, 5):
        down = shift(down, -1)
        kvs[r] = down
        if r < 4:
            up = shift(up, 1)
            kvs[RING - r] = up
    u, dkvs, d_table = main(x0, x1, table, kvs)
    up = shift(dkvs[4], 1)
    up = shift(added(up, dkvs[3]), 1)
    down = shift(dkvs[5], -1)
    up = shift(added(up, dkvs[2]), 1)
    down = shift(added(down, dkvs[6]), -1)
    up = shift(added(up, dkvs[1]), 1)
    down = shift(added(down, dkvs[7]), -1)
    keep_table, send_table = split_table(d_table)
    summed = (keep_table + swap(send_table, "core").astype(F32)).astype(BF16)
    parts = lax.all_to_all(summed.reshape(16, COLS, COLS), peers, 0, 0, tiled=True)
    d_bias = jnp.sum(parts.reshape(8, H, COLS, COLS).astype(F32), axis=0)
    keep, send = finish(u, dkvs[0], up, down)
    d_pair = output(keep, swap(send, "yl"), gmine, gother, w_qkvg)
    return (d_pair, d_bias)


def solution(mesh):
    split = Mesh(mesh.devices.reshape(2, 4, 2, 2, RING), ("yh", "x", "core", "yl", "z"))
    row, col = ("yh", "x", "core"), ("yl", "z")
    in_specs = (P(row, col, None), P(), P(), P(None, col, row), P(), P(row, col, None))
    out_specs = (P(row, col, None), P(None, col, row))
    return jax.shard_map(body, mesh=split, in_specs=in_specs, out_specs=out_specs, check_vma=False)
```

```python
import functools
import math

import jax
import jax.numpy as jnp
from jax import lax
from jax.experimental import pallas as pl
from jax.experimental.pallas import tpu as pltpu
from jax.sharding import Mesh, PartitionSpec as P

H = 2
DH = 32
CHAINS = 8
SCALE = 1.0 / math.sqrt(DH)
MASKED_SCORE = -1e30
F32 = jnp.float32
BF16 = jnp.bfloat16

ROWS = 6
COLS = 96
RING = 8
HALF = RING * COLS
KEYS = 2 * HALF
WIDE = 128
CHUNK = 4 * COLS
CHUNKS = ((0, 1), (2, 7), (3, 6), (4, 5))
LAST = len(CHUNKS) - 1
M_LANE = 64
SLOT = KEYS // CHAINS

NT = (((1,), (1,)), ((), ()))
NN = (((1,), (0,)), ((), ()))
TN = (((0,), (0,)), ((), ()))


def mm(a, b, dims):
    return lax.dot_general(a, b, dims, preferred_element_type=F32)


def params(limit=48 << 20):
    return pltpu.CompilerParams(vmem_limit_bytes=limit)


def cost(us):
    return pl.CostEstimate(flops=0, bytes_accessed=int(us * 3e6), transcendentals=0)


def lanes(shape):
    return lax.broadcasted_iota(jnp.int32, shape, len(shape) - 1)


def head_weight(w, h):
    parts = [w[:, (part * H + h) * DH : (part * H + h + 1) * DH] for part in (1, 2, 0, 3)]
    return jnp.concatenate(parts, axis=1)


def project_kernel(
    pair_hbm, grad_hbm, w_hbm, wout_hbm, mine_ref, other_ref, gmine_ref, gother_ref,
    pair_s, grad_s, w_s, wout_s, sem,
):
    yl = lax.axis_index("yl")
    pairs = ((w_hbm, w_s), (wout_hbm, wout_s), (pair_hbm, pair_s), (grad_hbm, grad_s))
    copies = [pltpu.make_async_copy(a, b, sem.at[n]) for n, (a, b) in enumerate(pairs)]
    for copy in copies:
        copy.start()
    for copy in copies:
        copy.wait()
    pair = pair_s[...].reshape(ROWS * COLS, WIDE)
    grad = grad_s[...].reshape(ROWS * COLS, WIDE)
    w = w_s[...]
    wout = wout_s[...]
    lane = lanes((ROWS * COLS, WIDE))
    for h in range(H):
        proj = mm(pair, head_weight(w, h), NN)
        rows = jnp.concatenate(
            [jnp.zeros((WIDE - DH, WIDE), BF16), wout[h * DH : (h + 1) * DH]], axis=0
        )
        d_out = mm(grad, rows, NT)
        gate = jax.nn.sigmoid(proj)
        payload = jnp.where(
            lane < 2 * DH, proj, jnp.where(lane < 3 * DH, proj * SCALE, d_out * gate)
        )
        payload = payload.astype(BF16).reshape(ROWS, COLS, WIDE)
        g = (d_out * gate * (1.0 - gate)).reshape(ROWS, COLS, WIDE)

        @pl.when(yl == h)
        def _():
            mine_ref[...] = payload
            gmine_ref[...] = g

        @pl.when(yl != h)
        def _():
            other_ref[...] = payload
            gother_ref[...] = g


def project(pair, grad, w, wout):
    shape = (ROWS, COLS, WIDE)
    return pl.pallas_call(
        project_kernel,
        in_specs=[pl.BlockSpec(memory_space=pl.ANY)] * 4,
        out_shape=[
            jax.ShapeDtypeStruct(shape, BF16),
            jax.ShapeDtypeStruct(shape, BF16),
            jax.ShapeDtypeStruct(shape, F32),
            jax.ShapeDtypeStruct(shape, F32),
        ],
        scratch_shapes=[
            pltpu.VMEM(shape, BF16),
            pltpu.VMEM(shape, BF16),
            pltpu.VMEM(w.shape, BF16),
            pltpu.VMEM(wout.shape, BF16),
            pltpu.SemaphoreType.DMA((4,)),
        ],
        compiler_params=params(),
        cost_estimate=cost(2.0),
        name="project",
    )(pair, grad, w, wout)


def pack_kernel(mine_ref, recv_ref, kv_ref, q_ref, da_ref):
    yl = lax.axis_index("yl")
    lane = lanes((COLS, WIDE))

    def write(i, a, b):
        a, b = a.astype(F32), b.astype(F32)
        kv_ref[i] = jnp.where(lane < 2 * DH, a, pltpu.roll(b, 2 * DH, 1)).astype(BF16)
        for part, x in enumerate((a, b)):
            y = pltpu.roll(x, 2 * DH, 1)
            rows = slice(part * COLS, (part + 1) * COLS)
            q_ref[i, rows] = jnp.where(lane < DH, y, 0.0).astype(BF16)
            da_ref[i, rows] = jnp.where((lane >= DH) & (lane < 2 * DH), y, 0.0).astype(BF16)

    for i in range(ROWS):

        @pl.when(yl == 0)
        def _():
            write(i, mine_ref[i], recv_ref[i])

        @pl.when(yl != 0)
        def _():
            write(i, recv_ref[i], mine_ref[i])


def pack(mine, recv):
    block = jax.ShapeDtypeStruct((ROWS, COLS, WIDE), BF16)
    both = jax.ShapeDtypeStruct((ROWS, 2 * COLS, WIDE), BF16)
    return pl.pallas_call(
        pack_kernel,
        out_shape=[block, both, both],
        compiler_params=params(),
        cost_estimate=cost(0.6),
        name="pack",
    )(mine, recv)


def bias_kernel(len_ref, own_ref, oth_ref, out_ref):
    core = lax.axis_index("core")
    z = lax.axis_index("z")
    lane = lanes((1, COLS))
    for c, pair in enumerate(CHUNKS):
        for n, r in enumerate(pair):
            at = lax.rem(z + r, RING)
            x, odd = at // 2, lax.rem(at, 2)
            for yh in range(2):
                start = (yh * 2 + n) * COLS
                valid = lane + odd * COLS < len_ref[yh * 4 + x]
                lift = jnp.where(valid, 0.0, MASKED_SCORE)
                for yl in range(2):
                    rows = slice(yl * COLS, (yl + 1) * COLS)
                    both = jnp.where(odd == core, own_ref[yh, x, yl], oth_ref[yh, x, yl])
                    out_ref[c, rows, start : start + COLS] = both.astype(F32) + lift


def bias_table(chain_lengths, own, oth):
    return pl.pallas_call(
        bias_kernel,
        out_shape=jax.ShapeDtypeStruct((len(CHUNKS), 2 * COLS, CHUNK), F32),
        in_specs=[
            pl.BlockSpec(memory_space=pltpu.SMEM),
            pl.BlockSpec(memory_space=pltpu.VMEM),
            pl.BlockSpec(memory_space=pltpu.VMEM),
        ],
        compiler_params=params(),
        cost_estimate=cost(1.5),
        name="bias_table",
    )(chain_lengths, own, oth)


def stack(a, b):
    two = jnp.concatenate([a, b], axis=0)
    moved = pltpu.roll(two.astype(F32), 2 * DH, 1).astype(BF16)
    return jnp.concatenate([two, moved], axis=0)


def unstack(value):
    moved = pltpu.roll(value[2 * COLS :], 2 * DH, 1)
    both = (value[: 2 * COLS] + moved).astype(BF16)
    return both[:COLS], both[COLS:]


def column(state, n):
    return state[:, M_LANE + n : M_LANE + n + 1]


def score_step(c, q, kv, bias, state):
    lane = lanes((2 * COLS, WIDE))
    s = mm(q, kv, NT) + bias
    top = jnp.max(s, axis=1, keepdims=True)
    if c > 0:
        old = column(state, c)
        top = jnp.maximum(top, old)
        fade = jnp.exp(old - top)
    e = jnp.exp(s - top)
    total = jnp.sum(e, axis=1, keepdims=True)
    acc = mm(e.astype(BF16), kv, NN)
    if c > 0:
        total = total + column(state, 0) * fade
        acc = acc + state * fade
    acc = jnp.where(lane < M_LANE, acc, jnp.where(lane == M_LANE, total, 0.0))
    for n in range(c):
        acc = jnp.where(lane == M_LANE + 1 + n, column(state, 1 + n), acc)
    acc = jnp.where(lane == M_LANE + 1 + c, top, acc)
    return e, acc, top, total


def forward_kernel(c, q_ref, a_ref, b_ref, bias_ref, *refs):
    state = refs[0][0] if c > 0 else None
    e_ref, state_ref = refs[-2:]
    e, acc, _, _ = score_step(c, q_ref[0], stack(a_ref[0], b_ref[0]), bias_ref[0], state)
    e_ref[0] = e
    state_ref[0] = acc


ROW = pl.BlockSpec((1, COLS, WIDE), lambda i: (i, 0, 0))
ROW2 = pl.BlockSpec((1, 2 * COLS, WIDE), lambda i: (i, 0, 0))
ROWE = pl.BlockSpec((1, 2 * COLS, CHUNK), lambda i: (i, 0, 0))
TABLE = pl.BlockSpec((2 * COLS, CHUNK), lambda i: (0, 0))
BLOCK = jax.ShapeDtypeStruct((ROWS, COLS, WIDE), BF16)
STATE = jax.ShapeDtypeStruct((ROWS, 2 * COLS, WIDE), F32)


def table_of(c):
    return pl.BlockSpec((1, 2 * COLS, CHUNK), lambda i: (c, 0, 0))


def forward(c, q, kvs, bias, state):
    a, b = CHUNKS[c]
    more = [] if c == 0 else [state]
    return pl.pallas_call(
        functools.partial(forward_kernel, c),
        grid=(ROWS,),
        in_specs=[ROW2, ROW, ROW, table_of(c)] + [ROW2] * len(more),
        out_specs=[ROWE, ROW2],
        out_shape=[jax.ShapeDtypeStruct((ROWS, 2 * COLS, CHUNK), F32), STATE],
        compiler_params=params(),
        cost_estimate=cost(2.0),
        name=f"forward_{c}",
    )(q, kvs[a], kvs[b], bias, *more)


def gradient_step(p, q, da, kv, dot, left, right):
    d = p * (mm(da, kv, NT) - dot)
    low = d.astype(BF16)
    left[: 2 * COLS, :] = low
    left[2 * COLS :, :] = p.astype(BF16)
    dq = mm(low, kv, NN)
    return d, dq, mm(left[...], right[...], TN)


def turn_kernel(q_ref, da_ref, a_ref, b_ref, bias_ref, state_ref, *refs):
    out_ref, da_out, db_out, table_ref, left, right = refs
    i = pl.program_id(0)
    q, da = q_ref[0], da_ref[0]
    kv = stack(a_ref[0], b_ref[0])
    e, acc, top, total = score_step(LAST, q, kv, bias_ref[0], state_ref[0])
    inverse = 1.0 / total
    acc = acc * inverse
    dot = jnp.sum(acc * da.astype(F32), axis=1, keepdims=True)
    right[: 2 * COLS, :] = q
    right[2 * COLS :, :] = da
    d, dq, dkv = gradient_step(e * inverse, q, da, kv, dot, left, right)

    @pl.when(i == 0)
    def _():
        table_ref[...] = d

    @pl.when(i != 0)
    def _():
        table_ref[...] += d

    da_out[0], db_out[0] = unstack(dkv)
    lane = lanes((2 * COLS, WIDE))
    out = jnp.where(lane < DH, dq, acc)
    out = jnp.where(lane == M_LANE, dot, out)
    for c in range(LAST):
        factor = jnp.exp(column(state_ref[0], 1 + c) - top) * inverse
        out = jnp.where(lane == M_LANE + 1 + c, factor, out)
    out_ref[0] = out


def turn(q, da, kvs, bias, state):
    a, b = CHUNKS[LAST]
    return pl.pallas_call(
        turn_kernel,
        grid=(ROWS,),
        in_specs=[ROW2, ROW2, ROW, ROW, table_of(LAST), ROW2],
        out_specs=[ROW2, ROW, ROW, TABLE],
        out_shape=[STATE, BLOCK, BLOCK, jax.ShapeDtypeStruct((2 * COLS, CHUNK), F32)],
        scratch_shapes=[pltpu.VMEM((CHUNK, CHUNK), BF16), pltpu.VMEM((CHUNK, WIDE), BF16)],
        compiler_params=params(),
        cost_estimate=cost(4.0),
        name="turn",
    )(q, da, kvs[a], kvs[b], bias, state)


def backward_kernel(q_ref, da_ref, state_ref, table_ref, *refs):
    n = LAST
    kv_refs, e_refs = refs[: 2 * n], refs[2 * n : 3 * n]
    u_ref, dkv_refs = refs[3 * n], refs[3 * n + 1 : 5 * n + 1]
    keep_ref, send_ref = refs[5 * n + 1 : 5 * n + 3]
    left, right, sums = refs[5 * n + 3 :]
    i = pl.program_id(0)
    q, da, state = q_ref[0], da_ref[0], state_ref[0]
    dot = column(state, 0)
    right[: 2 * COLS, :] = q
    right[2 * COLS :, :] = da

    @pl.when(i == 0)
    def _():
        sums[...] = jnp.zeros_like(sums)

    u = state
    lane = lanes((2 * COLS, WIDE))
    for c in range(n):
        kv = stack(kv_refs[2 * c][0], kv_refs[2 * c + 1][0])
        p = e_refs[c][0] * column(state, 1 + c)
        d, dq, dkv = gradient_step(p, q, da, kv, dot, left.at[c], right)
        sums[c] += d
        u = jnp.where(lane < DH, u + dq, u)
        dkv_refs[2 * c][0], dkv_refs[2 * c + 1][0] = unstack(dkv)
    u = jnp.where(lane < DH, u * SCALE, u)
    u_ref[0, 0] = u[:COLS]
    u_ref[1, 0] = u[COLS:]

    @pl.when(i == ROWS - 1)
    def _():
        core = lax.axis_index("core")
        z = lax.axis_index("z")
        for c, pair in enumerate(CHUNKS):
            table = table_ref if c == LAST else sums.at[c]
            for m, r in enumerate(pair):
                at = lax.rem(z + r, RING)
                x, odd = at // 2, lax.rem(at, 2)
                for yh in range(2):
                    start = (yh * 2 + m) * COLS
                    for yl in range(2):
                        rows = slice(yl * COLS, (yl + 1) * COLS)
                        piece = table[rows, start : start + COLS]

                        @pl.when(odd == core)
                        def _():
                            keep_ref[yh, x, yl] = piece

                        @pl.when(odd != core)
                        def _():
                            send_ref[yh, x, yl] = piece.astype(BF16)


def backward(q, da, state, table, kvs, es):
    order = [r for pair in CHUNKS[:LAST] for r in pair]
    blocks = (2, 4, 2, COLS, COLS)
    whole = pl.BlockSpec(blocks, lambda i: (0, 0, 0, 0, 0))
    out = pl.pallas_call(
        backward_kernel,
        grid=(ROWS,),
        in_specs=[ROW2, ROW2, ROW2, TABLE] + [ROW] * len(order) + [ROWE] * LAST,
        out_specs=[pl.BlockSpec((2, 1, COLS, WIDE), lambda i: (0, i, 0, 0))]
        + [ROW] * len(order)
        + [whole, whole],
        out_shape=[jax.ShapeDtypeStruct((2, ROWS, COLS, WIDE), F32)]
        + [BLOCK] * len(order)
        + [jax.ShapeDtypeStruct(blocks, F32), jax.ShapeDtypeStruct(blocks, BF16)],
        scratch_shapes=[
            pltpu.VMEM((LAST, CHUNK, CHUNK), BF16),
            pltpu.VMEM((CHUNK, WIDE), BF16),
            pltpu.VMEM((LAST, 2 * COLS, CHUNK), F32),
        ],
        compiler_params=params(),
        cost_estimate=cost(6.0),
        name="backward",
    )(q, da, state, table, *[kvs[r] for r in order], *es)
    return out[0], dict(zip(order, out[1 : len(order) + 1])), out[-2], out[-1]


def finish_kernel(u_ref, a_ref, b_ref, c_ref, keep_ref, send_ref):
    yl = lax.axis_index("yl")
    lane = lanes((COLS, WIDE))
    for i in range(ROWS):
        dkv = a_ref[i].astype(F32) + b_ref[i].astype(F32) + c_ref[i].astype(F32)
        first = jnp.where(lane < 2 * DH, dkv, pltpu.roll(u_ref[0, i], 2 * DH, 1))
        second = jnp.where(
            lane < 2 * DH, pltpu.roll(dkv, 2 * DH, 1), pltpu.roll(u_ref[1, i], 2 * DH, 1)
        )

        @pl.when(yl == 0)
        def _():
            keep_ref[i] = first
            send_ref[i] = second.astype(BF16)

        @pl.when(yl != 0)
        def _():
            keep_ref[i] = second
            send_ref[i] = first.astype(BF16)


def finish(u, a, b, c):
    shape = (ROWS, COLS, WIDE)
    return pl.pallas_call(
        finish_kernel,
        out_shape=[jax.ShapeDtypeStruct(shape, F32), jax.ShapeDtypeStruct(shape, BF16)],
        compiler_params=params(),
        name="finish",
    )(u, a, b, c)


def output_kernel(keep_ref, recv_ref, gmine_ref, gother_ref, w_ref, out_ref):
    yl = lax.axis_index("yl")
    flat = (ROWS * COLS, WIDE)
    lane = lanes(flat)
    keep = keep_ref[...].reshape(flat)
    recv = recv_ref[...].reshape(flat).astype(F32)
    mine = jnp.where(lane < 3 * DH, keep, keep * gmine_ref[...].reshape(flat)).astype(BF16)
    other = jnp.where(lane < 3 * DH, recv, recv * gother_ref[...].reshape(flat)).astype(BF16)
    w = w_ref[...]
    w0, w1 = head_weight(w, 0), head_weight(w, 1)

    def write(a, b):
        out_ref[...] = (mm(a, w0, NT) + mm(b, w1, NT)).astype(BF16).reshape(ROWS, COLS, WIDE)

    @pl.when(yl == 0)
    def _():
        write(mine, other)

    @pl.when(yl != 0)
    def _():
        write(other, mine)


def output(keep, recv, gmine, gother, w):
    return pl.pallas_call(
        output_kernel,
        out_shape=jax.ShapeDtypeStruct((ROWS, COLS, WIDE), BF16),
        compiler_params=params(),
        name="output",
    )(keep, recv, gmine, gother, w)


def shift(value, step):
    return lax.ppermute(value, "z", [(z, (z + step) % RING) for z in range(RING)])


def swap(value, axis):
    return lax.ppermute(value, axis, [(0, 1), (1, 0)])


def added(a, b):
    return (a.astype(F32) + b.astype(F32)).astype(BF16)


def body(pair, w_qkvg, w_out, bias, chain_lengths, d_pair_out):
    peers = ("yh", "x", "yl")
    wanted = jnp.broadcast_to(bias[None], (8,) + bias.shape).reshape(16, COLS, COLS)
    mine, other, gmine, gother = project(pair, d_pair_out, w_qkvg, w_out)
    recv = swap(other, "yl")
    own = lax.all_to_all(wanted, peers, 0, 0, tiled=True)
    kv, q, da = pack(mine, recv)
    oth = swap(own, "core")
    blocks = (2, 4, 2, COLS, COLS)
    table = bias_table(chain_lengths, own.reshape(blocks), oth.reshape(blocks))
    kvs = [kv] + [None] * (RING - 1)
    up = down = kv
    for r in range(1, 5):
        down = shift(down, -1)
        kvs[r] = down
        if r < 4:
            up = shift(up, 1)
            kvs[RING - r] = up
    es, state = [], None
    for c in range(LAST):
        e, state = forward(c, q, kvs, table, state)
        es.append(e)
    state, d4, d5, d_last = turn(q, da, kvs, table, state)
    up = shift(d4, 1)
    down = shift(d5, -1)
    u, dkvs, keep_table, send_table = backward(q, da, state, d_last, kvs, es)
    up = shift(added(up, dkvs[3]), 1)
    down = shift(added(down, dkvs[6]), -1)
    up = shift(added(up, dkvs[2]), 1)
    down = shift(added(down, dkvs[7]), -1)
    up = shift(added(up, dkvs[1]), 1)
    summed = (keep_table + swap(send_table, "core").astype(F32)).astype(BF16)
    parts = lax.all_to_all(summed.reshape(16, COLS, COLS), peers, 0, 0, tiled=True)
    d_bias = jnp.sum(parts.reshape(8, H, COLS, COLS).astype(F32), axis=0)
    keep, send = finish(u, dkvs[0], up, down)
    d_pair = output(keep, swap(send, "yl"), gmine, gother, w_qkvg)
    return (d_pair, d_bias)


def solution(mesh):
    split = Mesh(mesh.devices.reshape(2, 4, 2, 2, RING), ("yh", "x", "core", "yl", "z"))
    row, col = ("yh", "x", "core"), ("yl", "z")
    in_specs = (P(row, col, None), P(), P(), P(None, col, row), P(), P(row, col, None))
    out_specs = (P(row, col, None), P(None, col, row))
    return jax.shard_map(body, mesh=split, in_specs=in_specs, out_specs=out_specs, check_vma=False)
```

```python
import functools
import math

import jax
import jax.numpy as jnp
from jax import lax
from jax.experimental import pallas as pl
from jax.experimental.pallas import tpu as pltpu
from jax.sharding import Mesh, PartitionSpec as P

H = 2
DH = 32
CHAINS = 8
SCALE = 1.0 / math.sqrt(DH)
MASKED_SCORE = -1e30
F32 = jnp.float32
BF16 = jnp.bfloat16

ROWS = 6
COLS = 96
RING = 8
HALF = RING * COLS
KEYS = 2 * HALF
WIDE = 128
EARLY = (0, 1, 7, 2, 6, 3)
LATE = (4, 5)
NE, NL = len(EARLY) * COLS, len(LATE) * COLS
SLOT = KEYS // CHAINS

NT = (((1,), (1,)), ((), ()))
NN = (((1,), (0,)), ((), ()))
TN = (((0,), (0,)), ((), ()))


def mm(a, b, dims):
    return lax.dot_general(a, b, dims, preferred_element_type=F32)


def params(limit=32 << 20):
    return pltpu.CompilerParams(vmem_limit_bytes=limit)


def cost(us):
    return pl.CostEstimate(flops=0, bytes_accessed=int(us * 3e6), transcendentals=0)


def lanes(shape):
    return lax.broadcasted_iota(jnp.int32, shape, len(shape) - 1)


def head_weight(w, h):
    parts = [w[:, (part * H + h) * DH : (part * H + h + 1) * DH] for part in (1, 2, 0, 3)]
    return jnp.concatenate(parts, axis=1)


def project_kernel(
    pair_hbm, grad_hbm, w_hbm, wout_hbm, mine_ref, other_ref, gmine_ref, gother_ref,
    pair_s, grad_s, w_s, wout_s, sem,
):
    yl = lax.axis_index("yl")
    pairs = ((w_hbm, w_s), (wout_hbm, wout_s), (pair_hbm, pair_s), (grad_hbm, grad_s))
    copies = [pltpu.make_async_copy(a, b, sem.at[n]) for n, (a, b) in enumerate(pairs)]
    for copy in copies:
        copy.start()
    for copy in copies:
        copy.wait()
    pair = pair_s[...].reshape(ROWS * COLS, WIDE)
    grad = grad_s[...].reshape(ROWS * COLS, WIDE)
    w = w_s[...]
    wout = wout_s[...]
    lane = lanes((ROWS * COLS, WIDE))
    for h in range(H):
        proj = mm(pair, head_weight(w, h), NN)
        rows = jnp.concatenate(
            [jnp.zeros((WIDE - DH, WIDE), BF16), wout[h * DH : (h + 1) * DH]], axis=0
        )
        d_out = mm(grad, rows, NT)
        gate = jax.nn.sigmoid(proj)
        payload = jnp.where(
            lane < 2 * DH, proj, jnp.where(lane < 3 * DH, proj * SCALE, d_out * gate)
        )
        payload = payload.astype(BF16).reshape(ROWS, COLS, WIDE)
        g = (d_out * gate * (1.0 - gate)).reshape(ROWS, COLS, WIDE)

        @pl.when(yl == h)
        def _():
            mine_ref[...] = payload
            gmine_ref[...] = g

        @pl.when(yl != h)
        def _():
            other_ref[...] = payload
            gother_ref[...] = g


def project(pair, grad, w, wout):
    shape = (ROWS, COLS, WIDE)
    return pl.pallas_call(
        project_kernel,
        in_specs=[pl.BlockSpec(memory_space=pltpu.HBM)] * 4,
        out_shape=[
            jax.ShapeDtypeStruct(shape, BF16),
            jax.ShapeDtypeStruct(shape, BF16),
            jax.ShapeDtypeStruct(shape, F32),
            jax.ShapeDtypeStruct(shape, F32),
        ],
        scratch_shapes=[
            pltpu.VMEM(shape, BF16),
            pltpu.VMEM(shape, BF16),
            pltpu.VMEM(w.shape, BF16),
            pltpu.VMEM(wout.shape, BF16),
            pltpu.SemaphoreType.DMA((4,)),
        ],
        compiler_params=params(60 << 20),
        cost_estimate=cost(2.0),
        name="project",
    )(pair, grad, w, wout)


def pack_kernel(mine_ref, recv_ref, kv_ref, q_ref, da_ref, qt_ref, dat_ref):
    yl = lax.axis_index("yl")
    lane = lanes((COLS, WIDE))

    def write(i, a, b):
        a, b = a.astype(F32), b.astype(F32)
        kv_ref[i] = jnp.where(lane < 2 * DH, a, pltpu.roll(b, 2 * DH, 1)).astype(BF16)
        for part, x in enumerate((a, b)):
            y = pltpu.roll(x, 2 * DH, 1)
            rows = slice(part * COLS, (part + 1) * COLS)
            q_ref[i, rows] = jnp.where(lane < DH, y, 0.0).astype(BF16)
            da_ref[i, rows] = jnp.where((lane >= DH) & (lane < 2 * DH), y, 0.0).astype(BF16)
        turned = jnp.concatenate([a, b], axis=0).T
        qt_ref[i] = turned[2 * DH : 3 * DH].astype(BF16)
        dat_ref[i] = turned[3 * DH :].astype(BF16)

    for i in range(ROWS):

        @pl.when(yl == 0)
        def _():
            write(i, mine_ref[i], recv_ref[i])

        @pl.when(yl != 0)
        def _():
            write(i, recv_ref[i], mine_ref[i])


BLOCK = jax.ShapeDtypeStruct((ROWS, COLS, WIDE), BF16)
STATE = jax.ShapeDtypeStruct((ROWS, 2 * COLS, WIDE), F32)


def pack(mine, recv):
    both = jax.ShapeDtypeStruct((ROWS, 2 * COLS, WIDE), BF16)
    turned = jax.ShapeDtypeStruct((ROWS, DH, 2 * COLS), BF16)
    return pl.pallas_call(
        pack_kernel,
        out_shape=[BLOCK, both, both, turned, turned],
        compiler_params=params(),
        cost_estimate=cost(0.6),
        name="pack",
    )(mine, recv)


def bias_kernel(len_ref, own_ref, oth_ref, early_ref, late_ref):
    core = lax.axis_index("core")
    z = lax.axis_index("z")
    lane = lanes((1, COLS))
    for order, out_ref in ((EARLY, early_ref), (LATE, late_ref)):
        for n, r in enumerate(order):
            at = lax.rem(z + r, RING)
            x, odd = at // 2, lax.rem(at, 2)
            for yh in range(2):
                start = (yh * len(order) + n) * COLS
                valid = lane + odd * COLS < len_ref[yh * 4 + x]
                lift = jnp.where(valid, 0.0, MASKED_SCORE)
                for yl in range(2):
                    rows = slice(yl * COLS, (yl + 1) * COLS)
                    both = jnp.where(odd == core, own_ref[yh, x, yl], oth_ref[yh, x, yl])
                    out_ref[rows, start : start + COLS] = both.astype(F32) + lift


def bias_tables(chain_lengths, own, oth):
    return pl.pallas_call(
        bias_kernel,
        out_shape=[
            jax.ShapeDtypeStruct((2 * COLS, 2 * NE), F32),
            jax.ShapeDtypeStruct((2 * COLS, 2 * NL), F32),
        ],
        in_specs=[
            pl.BlockSpec(memory_space=pltpu.SMEM),
            pl.BlockSpec(memory_space=pltpu.VMEM),
            pl.BlockSpec(memory_space=pltpu.VMEM),
        ],
        compiler_params=params(),
        cost_estimate=cost(1.5),
        name="bias_tables",
    )(chain_lengths, own, oth)


def stack(refs, i):
    one = jnp.concatenate([ref[i] for ref in refs], axis=0)
    moved = pltpu.roll(one.astype(F32), 2 * DH, 1).astype(BF16)
    return jnp.concatenate([one, moved], axis=0)


def key_gradients(qt, dat, low, p_low, dkv_refs, i):
    dk = mm(qt, low, NN)
    dv = mm(dat, p_low, NN)
    half = dk.shape[1] // 2
    dkv = jnp.concatenate([dk[:, :half], dv[:, :half], dk[:, half:], dv[:, half:]], axis=0).T
    for n, ref in enumerate(dkv_refs):
        ref[i] = dkv[n * COLS : (n + 1) * COLS].astype(BF16)


def early_kernel(q_ref, bias_ref, *refs):
    n = len(EARLY)
    kv_refs, (e_ref, state_ref) = refs[:n], refs[n:]
    lane = lanes((2 * COLS, WIDE))
    for i in range(ROWS):
        kv = stack(kv_refs, i)
        s = mm(q_ref[i], kv, NT) + bias_ref[...]
        top = jnp.max(s, axis=1, keepdims=True)
        e = jnp.exp(s - top)
        total = jnp.sum(e, axis=1, keepdims=True)
        low = e.astype(BF16)
        e_ref[i] = low
        acc = mm(low, kv, NN)
        acc = jnp.where(lane < 2 * DH, acc, jnp.where(lane == 2 * DH, total, top))
        state_ref[i] = acc


def early(q, bias, kvs):
    return pl.pallas_call(
        early_kernel,
        out_shape=[jax.ShapeDtypeStruct((ROWS, 2 * COLS, 2 * NE), BF16), STATE],
        compiler_params=params(),
        cost_estimate=cost(4.0),
        name="early",
    )(q, bias, *[kvs[r] for r in EARLY])


def turn_kernel(q_ref, da_ref, qt_ref, dat_ref, bias_ref, state_ref, *refs):
    n = len(LATE)
    kv_refs, out_ref, dkv_refs, table_ref = refs[:n], refs[n], refs[n + 1 : 2 * n + 1], refs[-1]
    lane = lanes((2 * COLS, WIDE))
    for i in range(ROWS):
        q, da, state = q_ref[i], da_ref[i], state_ref[i]
        kv = stack(kv_refs, i)
        s = mm(q, kv, NT) + bias_ref[...]
        old = state[:, 2 * DH + 1 : 2 * DH + 2]
        top = jnp.maximum(jnp.max(s, axis=1, keepdims=True), old)
        fade = jnp.exp(old - top)
        e = jnp.exp(s - top)
        total = jnp.sum(e, axis=1, keepdims=True) + state[:, 2 * DH : 2 * DH + 1] * fade
        inverse = 1.0 / total
        factor = fade * inverse
        p = e * inverse
        p_low = p.astype(BF16)
        acc = mm(p_low, kv, NN) + state * factor
        dot = jnp.sum(jnp.where(lane < 2 * DH, acc * da.astype(F32), 0.0), axis=1, keepdims=True)
        d = p * (mm(da, kv, NT) - dot)
        if i == 0:
            table_ref[...] = d
        else:
            table_ref[...] += d
        low = d.astype(BF16)
        dq = mm(low, kv, NN)
        key_gradients(qt_ref[i], dat_ref[i], low, p_low, dkv_refs, i)
        out = jnp.where(lane < DH, dq, acc)
        out_ref[i] = jnp.where(
            lane < 2 * DH, out, jnp.where(lane == 2 * DH, dot, factor)
        )


def turn(q, da, qt, dat, bias, state, kvs):
    return pl.pallas_call(
        turn_kernel,
        out_shape=[STATE]
        + [BLOCK] * len(LATE)
        + [jax.ShapeDtypeStruct((2 * COLS, 2 * NL), F32)],
        compiler_params=params(),
        cost_estimate=cost(4.0),
        name="turn",
    )(q, da, qt, dat, bias, state, *[kvs[r] for r in LATE])


def backward_kernel(q_ref, da_ref, qt_ref, dat_ref, state_ref, e_ref, late_ref, *refs):
    n = len(EARLY)
    kv_refs, u_ref, dkv_refs = refs[:n], refs[n], refs[n + 1 : 2 * n + 1]
    keep_ref, send_ref, table_ref = refs[2 * n + 1 :]
    lane = lanes((2 * COLS, WIDE))
    for i in range(ROWS):
        da, state = da_ref[i], state_ref[i]
        dot = state[:, 2 * DH : 2 * DH + 1]
        factor = state[:, 2 * DH + 1 : 2 * DH + 2]
        kv = stack(kv_refs, i)
        p = e_ref[i].astype(F32) * factor
        d = p * (mm(da, kv, NT) - dot)
        if i == 0:
            table_ref[...] = d
        else:
            table_ref[...] += d
        low = d.astype(BF16)
        u = jnp.where(lane < DH, (state + mm(low, kv, NN)) * SCALE, state)
        u_ref[0, i] = u[:COLS]
        u_ref[1, i] = u[COLS:]
        key_gradients(qt_ref[i], dat_ref[i], low, p.astype(BF16), dkv_refs, i)
    core = lax.axis_index("core")
    z = lax.axis_index("z")
    for order, table in ((EARLY, table_ref), (LATE, late_ref)):
        for m, r in enumerate(order):
            at = lax.rem(z + r, RING)
            x, odd = at // 2, lax.rem(at, 2)
            for yh in range(2):
                start = (yh * len(order) + m) * COLS
                for yl in range(2):
                    piece = table[yl * COLS : (yl + 1) * COLS, start : start + COLS]

                    @pl.when(odd == core)
                    def _():
                        keep_ref[yh, x, yl] = piece

                    @pl.when(odd != core)
                    def _():
                        send_ref[yh, x, yl] = piece.astype(BF16)


def backward(q, da, qt, dat, state, e, late, kvs):
    n = len(EARLY)
    blocks = (2, 4, 2, COLS, COLS)
    out = pl.pallas_call(
        backward_kernel,
        out_shape=[jax.ShapeDtypeStruct((2, ROWS, COLS, WIDE), F32)]
        + [BLOCK] * n
        + [jax.ShapeDtypeStruct(blocks, F32), jax.ShapeDtypeStruct(blocks, BF16)],
        scratch_shapes=[pltpu.VMEM((2 * COLS, 2 * NE), F32)],
        compiler_params=params(),
        cost_estimate=cost(5.0),
        name="backward",
    )(q, da, qt, dat, state, e, late, *[kvs[r] for r in EARLY])
    return out[0], dict(zip(EARLY, out[1 : n + 1])), out[-2], out[-1]


def finish_kernel(u_ref, a_ref, b_ref, c_ref, keep_ref, send_ref):
    yl = lax.axis_index("yl")
    lane = lanes((COLS, WIDE))
    for i in range(ROWS):
        dkv = a_ref[i].astype(F32) + b_ref[i].astype(F32) + c_ref[i].astype(F32)
        first = jnp.where(lane < 2 * DH, dkv, pltpu.roll(u_ref[0, i], 2 * DH, 1))
        second = jnp.where(
            lane < 2 * DH, pltpu.roll(dkv, 2 * DH, 1), pltpu.roll(u_ref[1, i], 2 * DH, 1)
        )

        @pl.when(yl == 0)
        def _():
            keep_ref[i] = first
            send_ref[i] = second.astype(BF16)

        @pl.when(yl != 0)
        def _():
            keep_ref[i] = second
            send_ref[i] = first.astype(BF16)


def finish(u, a, b, c):
    shape = (ROWS, COLS, WIDE)
    return pl.pallas_call(
        finish_kernel,
        out_shape=[jax.ShapeDtypeStruct(shape, F32), jax.ShapeDtypeStruct(shape, BF16)],
        compiler_params=params(),
        name="finish",
    )(u, a, b, c)


def output_kernel(keep_ref, recv_ref, gmine_ref, gother_ref, w_ref, out_ref):
    yl = lax.axis_index("yl")
    flat = (ROWS * COLS, WIDE)
    lane = lanes(flat)
    keep = keep_ref[...].reshape(flat)
    recv = recv_ref[...].reshape(flat).astype(F32)
    mine = jnp.where(lane < 3 * DH, keep, keep * gmine_ref[...].reshape(flat)).astype(BF16)
    other = jnp.where(lane < 3 * DH, recv, recv * gother_ref[...].reshape(flat)).astype(BF16)
    w = w_ref[...]
    w0, w1 = head_weight(w, 0), head_weight(w, 1)

    def write(a, b):
        out_ref[...] = (mm(a, w0, NT) + mm(b, w1, NT)).astype(BF16).reshape(ROWS, COLS, WIDE)

    @pl.when(yl == 0)
    def _():
        write(mine, other)

    @pl.when(yl != 0)
    def _():
        write(other, mine)


def output(keep, recv, gmine, gother, w):
    return pl.pallas_call(
        output_kernel,
        out_shape=jax.ShapeDtypeStruct((ROWS, COLS, WIDE), BF16),
        compiler_params=params(),
        name="output",
    )(keep, recv, gmine, gother, w)


def shift(value, step):
    return lax.ppermute(value, "z", [(z, (z + step) % RING) for z in range(RING)])


def swap(value, axis):
    return lax.ppermute(value, axis, [(0, 1), (1, 0)])


def added(a, b):
    return (a.astype(F32) + b.astype(F32)).astype(BF16)


def body(pair, w_qkvg, w_out, bias, chain_lengths, d_pair_out):
    peers = ("yh", "x", "yl")
    wanted = jnp.broadcast_to(bias[None], (8,) + bias.shape).reshape(16, COLS, COLS)
    mine, other, gmine, gother = project(pair, d_pair_out, w_qkvg, w_out)
    recv = swap(other, "yl")
    own = lax.all_to_all(wanted, peers, 0, 0, tiled=True)
    kv, q, da, qt, dat = pack(mine, recv)
    oth = swap(own, "core")
    blocks = (2, 4, 2, COLS, COLS)
    bias_early, bias_late = bias_tables(
        chain_lengths, own.reshape(blocks), oth.reshape(blocks)
    )
    kvs = [kv] + [None] * (RING - 1)
    up = down = kv
    for r in range(1, 5):
        down = shift(down, -1)
        kvs[r] = down
        if r < 4:
            up = shift(up, 1)
            kvs[RING - r] = up
    e, state = early(q, bias_early, kvs)
    state, d4, d5, d_late = turn(q, da, qt, dat, bias_late, state, kvs)
    up = shift(d4, 1)
    down = shift(d5, -1)
    u, dkvs, keep_table, send_table = backward(q, da, qt, dat, state, e, d_late, kvs)
    up = shift(added(up, dkvs[3]), 1)
    down = shift(added(down, dkvs[6]), -1)
    up = shift(added(up, dkvs[2]), 1)
    down = shift(added(down, dkvs[7]), -1)
    up = shift(added(up, dkvs[1]), 1)
    summed = (keep_table + swap(send_table, "core").astype(F32)).astype(BF16)
    parts = lax.all_to_all(summed.reshape(16, COLS, COLS), peers, 0, 0, tiled=True)
    d_bias = jnp.sum(parts.reshape(8, H, COLS, COLS).astype(F32), axis=0)
    keep, send = finish(u, dkvs[0], up, down)
    d_pair = output(keep, swap(send, "yl"), gmine, gother, w_qkvg)
    return (d_pair, d_bias)


def solution(mesh):
    split = Mesh(mesh.devices.reshape(2, 4, 2, 2, RING), ("yh", "x", "core", "yl", "z"))
    row, col = ("yh", "x", "core"), ("yl", "z")
    in_specs = (P(row, col, None), P(), P(), P(None, col, row), P(), P(row, col, None))
    out_specs = (P(row, col, None), P(None, col, row))
    return jax.shard_map(body, mesh=split, in_specs=in_specs, out_specs=out_specs, check_vma=False)
```

```python
import functools
import math

import jax
import jax.numpy as jnp
from jax import lax
from jax.experimental import pallas as pl
from jax.experimental.pallas import tpu as pltpu
from jax.sharding import Mesh, PartitionSpec as P

H = 2
DH = 32
CHAINS = 8
SCALE = 1.0 / math.sqrt(DH)
MASKED_SCORE = -1e30
F32 = jnp.float32
BF16 = jnp.bfloat16

ROWS = 6
COLS = 96
RING = 8
HALF = RING * COLS
KEYS = 2 * HALF
WIDE = 128
NEAR = (0, 1, 7, 2)
FAR = (3, 6)
LATE = (4, 5)
NC, NF, NL = (2 * len(group) * COLS for group in (NEAR, FAR, LATE))


NT = (((1,), (1,)), ((), ()))
NN = (((1,), (0,)), ((), ()))
TN = (((0,), (0,)), ((), ()))


def mm(a, b, dims):
    return lax.dot_general(a, b, dims, preferred_element_type=F32)


def params(limit=32 << 20):
    return pltpu.CompilerParams(vmem_limit_bytes=limit)


def cost(us):
    return pl.CostEstimate(flops=0, bytes_accessed=int(us * 3e6), transcendentals=0)


def lanes(shape):
    return lax.broadcasted_iota(jnp.int32, shape, len(shape) - 1)


def head_weight(w, h):
    parts = [w[:, (part * H + h) * DH : (part * H + h + 1) * DH] for part in (1, 2, 0, 3)]
    return jnp.concatenate(parts, axis=1)


def project_kernel(
    len_hbm, bias_hbm, pair_hbm, grad_hbm, w_hbm, wout_hbm,
    mine_ref, other_ref, gmine_ref, gother_ref, wanted_ref, lift_ref,
    len_s, bias_s, pair_s, grad_s, w_s, wout_s, sem,
):
    yl = lax.axis_index("yl")
    pairs = (
        (len_hbm, len_s), (bias_hbm, bias_s), (w_hbm, w_s),
        (wout_hbm, wout_s), (pair_hbm, pair_s), (grad_hbm, grad_s),
    )
    copies = [pltpu.make_async_copy(a, b, sem.at[n]) for n, (a, b) in enumerate(pairs)]
    for copy in copies:
        copy.start()
    for copy in copies[:2]:
        copy.wait()
    for h in range(H):
        for n in range(8):
            wanted_ref[n * H + h] = bias_s[h]
    for c in range(CHAINS):
        for half in range(2):
            position = lanes((1, COLS)) + half * COLS
            lift_ref[2 * c + half] = jnp.where(position < len_s[c], 0.0, MASKED_SCORE)
    for copy in copies[2:]:
        copy.wait()
    pair = pair_s[...].reshape(ROWS * COLS, WIDE)
    grad = grad_s[...].reshape(ROWS * COLS, WIDE)
    w = w_s[...]
    wout = wout_s[...]
    lane = lanes((ROWS * COLS, WIDE))
    for h in range(H):
        proj = mm(pair, head_weight(w, h), NN)
        rows = jnp.concatenate(
            [jnp.zeros((WIDE - DH, WIDE), BF16), wout[h * DH : (h + 1) * DH]], axis=0
        )
        d_out = mm(grad, rows, NT)
        gate = jax.nn.sigmoid(proj)
        payload = jnp.where(
            lane < 2 * DH, proj, jnp.where(lane < 3 * DH, proj * SCALE, d_out * gate)
        )
        payload = payload.astype(BF16).reshape(ROWS, COLS, WIDE)
        g = (d_out * gate * (1.0 - gate)).reshape(ROWS, COLS, WIDE)

        @pl.when(yl == h)
        def _():
            mine_ref[...] = payload
            gmine_ref[...] = g

        @pl.when(yl != h)
        def _():
            other_ref[...] = payload
            gother_ref[...] = g


def project(chain_lengths, bias, pair, grad, w, wout):
    shape = (ROWS, COLS, WIDE)
    arrays = (chain_lengths, bias, pair, grad, w, wout)
    arrays = [pltpu.with_memory_space_constraint(array, pltpu.HBM) for array in arrays]
    return pl.pallas_call(
        project_kernel,
        in_specs=[pl.BlockSpec(memory_space=pltpu.HBM)] * 6,
        out_shape=[
            jax.ShapeDtypeStruct(shape, BF16),
            jax.ShapeDtypeStruct(shape, BF16),
            jax.ShapeDtypeStruct(shape, F32),
            jax.ShapeDtypeStruct(shape, F32),
            jax.ShapeDtypeStruct((16, COLS, COLS), BF16),
            jax.ShapeDtypeStruct((2 * CHAINS, 1, COLS), F32),
        ],
        scratch_shapes=[
            pltpu.SMEM((CHAINS,), jnp.int32),
            pltpu.VMEM(bias.shape, BF16),
            pltpu.VMEM(shape, BF16),
            pltpu.VMEM(shape, BF16),
            pltpu.VMEM(w.shape, BF16),
            pltpu.VMEM(wout.shape, BF16),
            pltpu.SemaphoreType.DMA((6,)),
        ],
        compiler_params=params(),
        cost_estimate=cost(2.0),
        name="project",
    )(*arrays)


def pack_kernel(mine_ref, recv_ref, kv_ref, q_ref, da_ref, qt_ref, dat_ref):
    yl = lax.axis_index("yl")
    lane = lanes((COLS, WIDE))

    def write(i, a, b):
        a, b = a.astype(F32), b.astype(F32)
        kv_ref[i] = jnp.where(lane < 2 * DH, a, pltpu.roll(b, 2 * DH, 1)).astype(BF16)
        for part, x in enumerate((a, b)):
            y = pltpu.roll(x, 2 * DH, 1)
            rows = slice(part * COLS, (part + 1) * COLS)
            q_ref[i, rows] = jnp.where(lane < DH, y, 0.0).astype(BF16)
            da_ref[i, rows] = jnp.where((lane >= DH) & (lane < 2 * DH), y, 0.0).astype(BF16)
        turned = jnp.concatenate([a, b], axis=0).T
        qt_ref[i] = turned[2 * DH : 3 * DH].astype(BF16)
        dat_ref[i] = turned[3 * DH :].astype(BF16)

    for i in range(ROWS):

        @pl.when(yl == 0)
        def _():
            write(i, mine_ref[i], recv_ref[i])

        @pl.when(yl != 0)
        def _():
            write(i, recv_ref[i], mine_ref[i])


BLOCK = jax.ShapeDtypeStruct((ROWS, COLS, WIDE), BF16)
STATE = jax.ShapeDtypeStruct((ROWS, 2 * COLS, WIDE), F32)


def pack(mine, recv):
    both = jax.ShapeDtypeStruct((ROWS, 2 * COLS, WIDE), BF16)
    turned = jax.ShapeDtypeStruct((ROWS, DH, 2 * COLS), BF16)
    return pl.pallas_call(
        pack_kernel,
        out_shape=[BLOCK, both, both, turned, turned],
        compiler_params=params(),
        cost_estimate=cost(0.6),
        name="pack",
    )(mine, recv)


def bias_kernel(lift_ref, own_ref, oth_ref, early_ref, late_ref):
    core = lax.axis_index("core")
    z = lax.axis_index("z")
    for group, out_ref, first in (
        (FAR, early_ref, 0), (NEAR, early_ref, NF), (LATE, late_ref, 0),
    ):
        for n, r in enumerate(group):
            at = lax.rem(z + r, RING)
            x, odd = at // 2, lax.rem(at, 2)
            for yh in range(2):
                start = first + (yh * len(group) + n) * COLS
                lift = lift_ref[yh * CHAINS + at]
                for yl in range(2):
                    rows = slice(yl * COLS, (yl + 1) * COLS)
                    both = jnp.where(odd == core, own_ref[yh, x, yl], oth_ref[yh, x, yl])
                    out_ref[rows, start : start + COLS] = both.astype(F32) + lift


def bias_tables(lift, own, oth):
    return pl.pallas_call(
        bias_kernel,
        out_shape=[
            jax.ShapeDtypeStruct((2 * COLS, NF + NC), F32),
            jax.ShapeDtypeStruct((2 * COLS, NL), F32),
        ],
        compiler_params=params(),
        cost_estimate=cost(1.5),
        name="bias_tables",
    )(lift, own, oth)


def stack(refs, i):
    one = jnp.concatenate([ref[i] for ref in refs], axis=0)
    moved = pltpu.roll(one.astype(F32), 2 * DH, 1).astype(BF16)
    return jnp.concatenate([one, moved], axis=0)


def key_gradients(qt, dat, low, p_low, dkv_refs, i):
    dk = mm(qt, low, NN)
    dv = mm(dat, p_low, NN)
    half = dk.shape[1] // 2
    dkv = jnp.concatenate([dk[:, :half], dv[:, :half], dk[:, half:], dv[:, half:]], axis=0).T
    for n, ref in enumerate(dkv_refs):
        ref[i] = dkv[n * COLS : (n + 1) * COLS].astype(BF16)


def wide(value):
    return jnp.broadcast_to(value, (2 * COLS, WIDE))


def across(value, like):
    return jnp.concatenate([value] * (like.shape[1] // WIDE), axis=1)


def add_row(table_ref, i, value):
    if i == 0:
        table_ref[...] = value
    else:
        table_ref[...] += value


def staged(first, second, third):
    held = first(0)
    for i in range(ROWS):
        done = second(i, *held)
        if i + 1 < ROWS:
            following = first(i + 1)
        third(i, *done)
        held = following


def early_kernel(q_ref, da_ref, bias_ref, *refs):
    n = len(FAR) + len(NEAR)
    far_refs, near_refs = refs[: len(FAR)], refs[len(FAR) : n]
    far_e_ref, near_e_ref, acc_ref, total_ref, mass_ref, top_ref = refs[n:]

    def scores(i):
        kv = jnp.concatenate([stack(far_refs, i), stack(near_refs, i)], axis=0)
        return kv, mm(q_ref[i], kv, NT) + bias_ref[...], mm(da_ref[i], kv, NT)

    def weigh(i, kv, s, w):
        top = jnp.max(s, axis=1, keepdims=True)
        e = jnp.exp(s - top)
        low = e.astype(BF16)
        far_e_ref[i] = low[:, :NF]
        near_e_ref[i] = low[:, NF:]
        total_ref[i] = wide(jnp.sum(e, axis=1, keepdims=True))
        mass_ref[i] = wide(jnp.sum(e * w, axis=1, keepdims=True))
        top_ref[i] = wide(top)
        return kv, low

    def gather(i, kv, low):
        acc_ref[i] = mm(low, kv, NN)

    staged(scores, weigh, gather)


def early(q, da, bias, kvs):
    return pl.pallas_call(
        early_kernel,
        out_shape=[
            jax.ShapeDtypeStruct((ROWS, 2 * COLS, NF), BF16),
            jax.ShapeDtypeStruct((ROWS, 2 * COLS, NC), BF16),
        ]
        + [STATE] * 4,
        compiler_params=params(),
        cost_estimate=cost(4.0),
        name="early",
    )(q, da, bias, *[kvs[r] for r in FAR + NEAR])


def turn_kernel(
    q_ref, da_ref, qt_ref, dat_ref, bias_ref, acc_ref, total_ref, mass_ref, top_ref, *refs
):
    n = len(LATE)
    kv_refs, (u_ref, dot_ref, factor_ref) = refs[:n], refs[n : n + 3]
    dkv_refs, table_ref = refs[n + 3 : 2 * n + 3], refs[-1]
    lane = lanes((2 * COLS, WIDE))

    def scores(i):
        kv = stack(kv_refs, i)
        return kv, mm(q_ref[i], kv, NT) + bias_ref[...], mm(da_ref[i], kv, NT)

    def weigh(i, kv, s, w):
        old = top_ref[i]
        top = jnp.maximum(jnp.max(s, axis=1, keepdims=True), old)
        fade = jnp.exp(old - top)
        e = jnp.exp(s - across(top, s))
        inverse = 1.0 / (jnp.sum(e, axis=1, keepdims=True) + total_ref[i] * fade)
        factor = fade * inverse
        dot = (jnp.sum(e * w, axis=1, keepdims=True) + mass_ref[i] * fade) * inverse
        factor_ref[i] = factor
        dot_ref[i] = dot
        p = e * across(inverse, e)
        d = p * (w - across(dot, p))
        add_row(table_ref, i, d)
        return kv, p.astype(BF16), d.astype(BF16), factor

    def gather(i, kv, p_low, low, factor):
        key_gradients(qt_ref[i], dat_ref[i], low, p_low, dkv_refs, i)
        acc = mm(p_low, kv, NN) + acc_ref[i] * factor
        u_ref[i] = jnp.where(lane < DH, mm(low, kv, NN), acc)

    staged(scores, weigh, gather)


def turn(q, da, qt, dat, bias, state, kvs):
    return pl.pallas_call(
        turn_kernel,
        out_shape=[STATE] * 3
        + [BLOCK] * len(LATE)
        + [jax.ShapeDtypeStruct((2 * COLS, NL), F32)],
        compiler_params=params(),
        cost_estimate=cost(3.0),
        name="turn",
    )(q, da, qt, dat, bias, *state, *[kvs[r] for r in LATE])


def backward_kernel(
    group, da_ref, qt_ref, dat_ref, part_ref, dot_ref, factor_ref, e_ref, *refs
):
    n = len(group)
    kv_refs, u_ref, dkv_refs, table_ref = refs[:n], refs[n], refs[n + 1 : 2 * n + 1], refs[2 * n + 1]
    lane = lanes((2 * COLS, WIDE))

    def scores(i):
        kv = stack(kv_refs, i)
        return kv, mm(da_ref[i], kv, NT)

    def weigh(i, kv, w):
        p = e_ref[i].astype(F32)
        p = p * across(factor_ref[i], p)
        d = p * (w - across(dot_ref[i], p))
        add_row(table_ref, i, d)
        return kv, p.astype(BF16), d.astype(BF16)

    def gather(i, kv, p_low, low):
        u = part_ref[i]
        u_ref[i] = jnp.where(lane < DH, u + mm(low, kv, NN), u)
        key_gradients(qt_ref[i], dat_ref[i], low, p_low, dkv_refs, i)

    staged(scores, weigh, gather)


def backward(group, da, qt, dat, state, e, kvs, time):
    n = len(group)
    out = pl.pallas_call(
        functools.partial(backward_kernel, group),
        out_shape=[STATE]
        + [BLOCK] * n
        + [jax.ShapeDtypeStruct((2 * COLS, 2 * n * COLS), F32)],
        compiler_params=params(),
        cost_estimate=cost(time),
        name="backward",
    )(da, qt, dat, *state, e, *[kvs[r] for r in group])
    return out[0], dict(zip(group, out[1 : n + 1])), out[-1]


def split_kernel(near_ref, far_ref, late_ref, keep_ref, send_ref):
    core = lax.axis_index("core")
    z = lax.axis_index("z")
    for group, table in ((NEAR, near_ref), (FAR, far_ref), (LATE, late_ref)):
        for m, r in enumerate(group):
            at = lax.rem(z + r, RING)
            x, odd = at // 2, lax.rem(at, 2)
            for yh in range(2):
                start = (yh * len(group) + m) * COLS
                for yl in range(2):
                    piece = table[yl * COLS : (yl + 1) * COLS, start : start + COLS]

                    @pl.when(odd == core)
                    def _():
                        keep_ref[yh, x, yl] = piece

                    @pl.when(odd != core)
                    def _():
                        send_ref[yh, x, yl] = piece.astype(BF16)


def split_tables(near, far, late):
    blocks = (2, 4, 2, COLS, COLS)
    return pl.pallas_call(
        split_kernel,
        out_shape=[jax.ShapeDtypeStruct(blocks, F32), jax.ShapeDtypeStruct(blocks, BF16)],
        compiler_params=params(),
        cost_estimate=cost(1.0),
        name="split_tables",
    )(near, far, late)


def relay_kernel(up_ref, part_ref, keep_ref, recv_ref, sent_ref, summed_ref):
    sent_ref[...] = (up_ref[...].astype(F32) + part_ref[...].astype(F32)).astype(BF16)
    summed_ref[...] = (keep_ref[...] + recv_ref[...].astype(F32)).astype(BF16)


def relay(up, part, keep, recv):
    return pl.pallas_call(
        relay_kernel,
        out_shape=[BLOCK, jax.ShapeDtypeStruct(keep.shape, BF16)],
        compiler_params=params(),
        cost_estimate=cost(0.8),
        name="relay",
    )(up, part, keep, recv)


def finish_kernel(u_ref, a_ref, b_ref, c_ref, keep_ref, send_ref):
    yl = lax.axis_index("yl")
    lane = lanes((COLS, WIDE))
    lane2 = lanes((2 * COLS, WIDE))
    for i in range(ROWS):
        dkv = a_ref[i].astype(F32) + b_ref[i].astype(F32) + c_ref[i].astype(F32)
        u = jnp.where(lane2 < DH, u_ref[i] * SCALE, u_ref[i])
        u = pltpu.roll(u, 2 * DH, 1)
        first = jnp.where(lane < 2 * DH, dkv, u[:COLS])
        second = jnp.where(lane < 2 * DH, pltpu.roll(dkv, 2 * DH, 1), u[COLS:])

        @pl.when(yl == 0)
        def _():
            keep_ref[i] = first
            send_ref[i] = second.astype(BF16)

        @pl.when(yl != 0)
        def _():
            keep_ref[i] = second
            send_ref[i] = first.astype(BF16)


def finish(u, a, b, c):
    shape = (ROWS, COLS, WIDE)
    return pl.pallas_call(
        finish_kernel,
        out_shape=[jax.ShapeDtypeStruct(shape, F32), jax.ShapeDtypeStruct(shape, BF16)],
        compiler_params=params(),
        name="finish",
    )(u, a, b, c)


def output_kernel(keep_ref, recv_ref, gmine_ref, gother_ref, w_ref, out_ref):
    yl = lax.axis_index("yl")
    flat = (ROWS * COLS, WIDE)
    lane = lanes(flat)
    keep = keep_ref[...].reshape(flat)
    recv = recv_ref[...].reshape(flat).astype(F32)
    mine = jnp.where(lane < 3 * DH, keep, keep * gmine_ref[...].reshape(flat)).astype(BF16)
    other = jnp.where(lane < 3 * DH, recv, recv * gother_ref[...].reshape(flat)).astype(BF16)
    w = w_ref[...]
    w0, w1 = head_weight(w, 0), head_weight(w, 1)

    def write(a, b):
        out_ref[...] = (mm(a, w0, NT) + mm(b, w1, NT)).astype(BF16).reshape(ROWS, COLS, WIDE)

    @pl.when(yl == 0)
    def _():
        write(mine, other)

    @pl.when(yl != 0)
    def _():
        write(other, mine)


def output(keep, recv, gmine, gother, w):
    return pl.pallas_call(
        output_kernel,
        out_shape=jax.ShapeDtypeStruct((ROWS, COLS, WIDE), BF16),
        compiler_params=params(),
        name="output",
    )(keep, recv, gmine, gother, w)


def shift(value, step):
    return lax.ppermute(value, "z", [(z, (z + step) % RING) for z in range(RING)])


def swap(value, axis):
    return lax.ppermute(value, axis, [(0, 1), (1, 0)])


def added(a, b):
    return (a.astype(F32) + b.astype(F32)).astype(BF16)


def body(pair, w_qkvg, w_out, bias, chain_lengths, d_pair_out):
    peers = ("yh", "x", "yl")
    mine, other, gmine, gother, wanted, lift = project(
        chain_lengths, bias, pair, d_pair_out, w_qkvg, w_out
    )
    recv = swap(other, "yl")
    own = lax.all_to_all(wanted, peers, 0, 0, tiled=True)
    kv, q, da, qt, dat = pack(mine, recv)
    oth = swap(own, "core")
    blocks = (2, 4, 2, COLS, COLS)
    bias_early, bias_late = bias_tables(lift, own.reshape(blocks), oth.reshape(blocks))
    kvs = [kv] + [None] * (RING - 1)
    up = down = kv
    for r in range(1, 5):
        down = shift(down, -1)
        kvs[r] = down
        if r < 4:
            up = shift(up, 1)
            kvs[RING - r] = up
    e_far, e_near, *state = early(q, da, bias_early, kvs)
    u, dot, factor, d4, d5, t_late = turn(q, da, qt, dat, bias_late, state, kvs)
    up = shift(d4, 1)
    down = shift(d5, -1)
    u, far, t_far = backward(FAR, da, qt, dat, (u, dot, factor), e_far, kvs, 2.5)
    up = shift(added(up, far[3]), 1)
    down = shift(added(down, far[6]), -1)
    u, near, t_near = backward(NEAR, da, qt, dat, (u, dot, factor), e_near, kvs, 3.0)
    keep_table, send_table = split_tables(t_near, t_far, t_late)
    recv_table = swap(send_table, "core")
    up = shift(added(up, near[2]), 1)
    down = shift(added(down, near[7]), -1)
    up, summed = relay(up, near[1], keep_table, recv_table)
    up = shift(up, 1)
    parts = lax.all_to_all(summed.reshape(16, COLS, COLS), peers, 0, 0, tiled=True)
    keep, send = finish(u, near[0], up, down)
    d_bias = jnp.sum(parts.reshape(8, H, COLS, COLS).astype(F32), axis=0)
    d_pair = output(keep, swap(send, "yl"), gmine, gother, w_qkvg)
    return (d_pair, d_bias)


def solution(mesh):
    split = Mesh(mesh.devices.reshape(2, 4, 2, 2, RING), ("yh", "x", "core", "yl", "z"))
    row, col = ("yh", "x", "core"), ("yl", "z")
    in_specs = (P(row, col, None), P(), P(), P(None, col, row), P(), P(row, col, None))
    out_specs = (P(row, col, None), P(None, col, row))
    return jax.shard_map(body, mesh=split, in_specs=in_specs, out_specs=out_specs, check_vma=False)
```

```python
import functools
import math

import jax
import jax.numpy as jnp
from jax import lax
from jax.experimental import pallas as pl
from jax.experimental.pallas import tpu as pltpu
from jax.sharding import Mesh, PartitionSpec as P

H = 2
DH = 32
CHAINS = 8
SCALE = 1.0 / math.sqrt(DH)
MASKED_SCORE = -1e30
F32 = jnp.float32
BF16 = jnp.bfloat16

ROWS = 6
COLS = 96
RING = 8
HALF = RING * COLS
KEYS = 2 * HALF
WIDE = 128
NEAR = (0, 1, 7, 2)
FAR = (3, 6)
LATE = (4, 5)
NC, NF, NL = (2 * len(group) * COLS for group in (NEAR, FAR, LATE))


NT = (((1,), (1,)), ((), ()))
NN = (((1,), (0,)), ((), ()))
TN = (((0,), (0,)), ((), ()))


def mm(a, b, dims):
    return lax.dot_general(a, b, dims, preferred_element_type=F32)


def params(limit=32 << 20):
    return pltpu.CompilerParams(vmem_limit_bytes=limit)


def cost(us):
    return pl.CostEstimate(flops=0, bytes_accessed=int(us * 1e5), transcendentals=0)


def lanes(shape):
    return lax.broadcasted_iota(jnp.int32, shape, len(shape) - 1)


def head_weight(w, h):
    parts = [w[:, (part * H + h) * DH : (part * H + h + 1) * DH] for part in (1, 2, 0, 3)]
    return jnp.concatenate(parts, axis=1)


def project_kernel(
    len_hbm, pair_hbm, grad_hbm, w_hbm, wout_hbm,
    mine_ref, other_ref, lift_ref,
    len_s, pair_s, grad_s, w_s, wout_s, sem,
):
    yl = lax.axis_index("yl")
    pairs = (
        (len_hbm, len_s), (w_hbm, w_s), (wout_hbm, wout_s),
        (pair_hbm, pair_s), (grad_hbm, grad_s),
    )
    copies = [pltpu.make_async_copy(a, b, sem.at[n]) for n, (a, b) in enumerate(pairs)]
    for copy in copies:
        copy.start()
    copies[0].wait()
    for c in range(CHAINS):
        for half in range(2):
            position = lanes((1, COLS)) + half * COLS
            lift_ref[2 * c + half] = jnp.where(position < len_s[c], 0.0, MASKED_SCORE)
    for copy in copies[1:]:
        copy.wait()
    pair = pair_s[...].reshape(ROWS * COLS, WIDE)
    grad = grad_s[...].reshape(ROWS * COLS, WIDE)
    w = w_s[...]
    wout = wout_s[...]
    lane = lanes((ROWS * COLS, WIDE))
    for h in range(H):
        proj = mm(pair, head_weight(w, h), NN)
        rows = jnp.concatenate(
            [jnp.zeros((WIDE - DH, WIDE), BF16), wout[h * DH : (h + 1) * DH]], axis=0
        )
        d_out = mm(grad, rows, NT)
        gate = jax.nn.sigmoid(proj)
        payload = jnp.where(
            lane < 2 * DH, proj, jnp.where(lane < 3 * DH, proj * SCALE, d_out * gate)
        )
        payload = payload.astype(BF16).reshape(ROWS, COLS, WIDE)

        @pl.when(yl == h)
        def _():
            mine_ref[...] = payload

        @pl.when(yl != h)
        def _():
            other_ref[...] = payload


def project(chain_lengths, pair, grad, w, wout):
    shape = (ROWS, COLS, WIDE)
    arrays = (chain_lengths, pair, grad, w, wout)
    arrays = [pltpu.with_memory_space_constraint(array, pltpu.HBM) for array in arrays]
    return pl.pallas_call(
        project_kernel,
        in_specs=[pl.BlockSpec(memory_space=pltpu.HBM)] * 5,
        out_shape=[
            jax.ShapeDtypeStruct(shape, BF16),
            jax.ShapeDtypeStruct(shape, BF16),
            jax.ShapeDtypeStruct((2 * CHAINS, 1, COLS), F32),
        ],
        scratch_shapes=[
            pltpu.SMEM((CHAINS,), jnp.int32),
            pltpu.VMEM(shape, BF16),
            pltpu.VMEM(shape, BF16),
            pltpu.VMEM(w.shape, BF16),
            pltpu.VMEM(wout.shape, BF16),
            pltpu.SemaphoreType.DMA((5,)),
        ],
        compiler_params=params(),
        cost_estimate=cost(2.0),
        name="project",
    )(*arrays)


def slope_kernel(
    _, pair_hbm, grad_hbm, w_hbm, wout_hbm, gmine_ref, gother_ref, pair_s, grad_s, w_s, wout_s, sem
):
    yl = lax.axis_index("yl")
    pairs = ((w_hbm, w_s), (wout_hbm, wout_s), (pair_hbm, pair_s), (grad_hbm, grad_s))
    copies = [pltpu.make_async_copy(a, b, sem.at[n]) for n, (a, b) in enumerate(pairs)]
    for copy in copies:
        copy.start()
    for copy in copies:
        copy.wait()
    pair = pair_s[...].reshape(ROWS * COLS, WIDE)
    grad = grad_s[...].reshape(ROWS * COLS, WIDE)
    zeros = jnp.zeros((WIDE - DH, WIDE), BF16)
    for h in range(H):
        gate = jax.nn.sigmoid(mm(pair, head_weight(w_s[...], h), NN))
        rows = jnp.concatenate([zeros, wout_s[h * DH : (h + 1) * DH]], axis=0)
        g = mm(grad, rows, NT) * gate * (1.0 - gate)

        @pl.when(yl == h)
        def _():
            gmine_ref[...] = g.reshape(ROWS, COLS, WIDE)

        @pl.when(yl != h)
        def _():
            gother_ref[...] = g.reshape(ROWS, COLS, WIDE)


def slopes(after, pair, grad, w, wout):
    shape = (ROWS, COLS, WIDE)
    arrays = [pltpu.with_memory_space_constraint(array, pltpu.HBM) for array in (pair, grad, w, wout)]
    return pl.pallas_call(
        slope_kernel,
        in_specs=[pl.BlockSpec(memory_space=pl.ANY)] + [pl.BlockSpec(memory_space=pltpu.HBM)] * 4,
        out_shape=[jax.ShapeDtypeStruct(shape, F32)] * 2,
        scratch_shapes=[
            pltpu.VMEM(shape, BF16),
            pltpu.VMEM(shape, BF16),
            pltpu.VMEM(w.shape, BF16),
            pltpu.VMEM(wout.shape, BF16),
            pltpu.SemaphoreType.DMA((4,)),
        ],
        compiler_params=params(),
        cost_estimate=cost(2.0),
        name="slopes",
    )(after, *arrays)


def pack_kernel(mine_ref, recv_ref, _, kv_ref, q_ref, da_ref, qt_ref, dat_ref):
    yl = lax.axis_index("yl")
    lane = lanes((COLS, WIDE))

    def write(i, a, b):
        a, b = a.astype(F32), b.astype(F32)
        kv_ref[i] = jnp.where(lane < 2 * DH, a, pltpu.roll(b, 2 * DH, 1)).astype(BF16)
        for part, x in enumerate((a, b)):
            y = pltpu.roll(x, 2 * DH, 1)
            rows = slice(part * COLS, (part + 1) * COLS)
            q_ref[i, rows] = jnp.where(lane < DH, y, 0.0).astype(BF16)
            da_ref[i, rows] = jnp.where((lane >= DH) & (lane < 2 * DH), y, 0.0).astype(BF16)
        turned = jnp.concatenate([a, b], axis=0).T
        qt_ref[i] = turned[2 * DH : 3 * DH].astype(BF16)
        dat_ref[i] = turned[3 * DH :].astype(BF16)

    for i in range(ROWS):

        @pl.when(yl == 0)
        def _():
            write(i, mine_ref[i], recv_ref[i])

        @pl.when(yl != 0)
        def _():
            write(i, recv_ref[i], mine_ref[i])


BLOCK = jax.ShapeDtypeStruct((ROWS, COLS, WIDE), BF16)
STATE = jax.ShapeDtypeStruct((ROWS, 2 * COLS, WIDE), F32)


def pack(mine, recv, after):
    both = jax.ShapeDtypeStruct((ROWS, 2 * COLS, WIDE), BF16)
    turned = jax.ShapeDtypeStruct((ROWS, DH, 2 * COLS), BF16)
    return pl.pallas_call(
        pack_kernel,
        in_specs=[pl.BlockSpec(memory_space=pltpu.VMEM)] * 2 + [pl.BlockSpec(memory_space=pl.ANY)],
        out_shape=[BLOCK, both, both, turned, turned],
        compiler_params=params(),
        cost_estimate=cost(0.6),
        name="pack",
    )(mine, recv, after)


EXCHANGE = jax.ShapeDtypeStruct((16, 2, COLS, COLS), BF16)


def want_kernel(own_ref, oth_ref, out_ref):
    core = lax.axis_index("core")
    for h in range(H):
        for n in range(8):
            out_ref[n * H + h, core] = own_ref[h]
            out_ref[n * H + h, 1 - core] = oth_ref[h]


def want(own, oth):
    return pl.pallas_call(
        want_kernel,
        out_shape=EXCHANGE,
        compiler_params=params(),
        cost_estimate=cost(0.4),
        name="want",
    )(own, oth)


def bias_kernel(lift_ref, all_ref, near_ref, far_ref, late_ref):
    z = lax.axis_index("z")
    for group, out_ref in ((NEAR, near_ref), (FAR, far_ref), (LATE, late_ref)):
        for n, r in enumerate(group):
            at = lax.rem(z + r, RING)
            x, odd = at // 2, lax.rem(at, 2)
            for yh in range(2):
                start = (yh * len(group) + n) * COLS
                lift = lift_ref[yh * CHAINS + at]
                for yl in range(2):
                    rows = slice(yl * COLS, (yl + 1) * COLS)
                    block = all_ref[(yh * 4 + x) * 2 + yl, odd].astype(F32)
                    out_ref[rows, start : start + COLS] = block + lift


def bias_tables(lift, everything):
    return pl.pallas_call(
        bias_kernel,
        out_shape=[
            jax.ShapeDtypeStruct((2 * COLS, NC), F32),
            jax.ShapeDtypeStruct((2 * COLS, NF), F32),
            jax.ShapeDtypeStruct((2 * COLS, NL), F32),
        ],
        compiler_params=params(),
        cost_estimate=cost(0.5),
        name="bias_tables",
    )(lift, everything)


def join_kernel(block_ref, _, out_ref):
    out_ref[...] = block_ref[...]


def join(block, after):
    return pl.pallas_call(
        join_kernel,
        in_specs=[pl.BlockSpec(memory_space=pltpu.VMEM), pl.BlockSpec(memory_space=pl.ANY)],
        out_shape=BLOCK,
        compiler_params=params(),
        cost_estimate=cost(0.2),
        name="join",
    )(block, after)


def stack(refs, i):
    one = jnp.concatenate([ref[i] for ref in refs], axis=0)
    moved = pltpu.roll(one.astype(F32), 2 * DH, 1).astype(BF16)
    return jnp.concatenate([one, moved], axis=0)


def key_gradients(qt, dat, low, p_low, dkv_refs, i):
    dk = mm(qt, low, NN)
    dv = mm(dat, p_low, NN)
    half = dk.shape[1] // 2
    dkv = jnp.concatenate([dk[:, :half], dv[:, :half], dk[:, half:], dv[:, half:]], axis=0).T
    for n, ref in enumerate(dkv_refs):
        ref[i] = dkv[n * COLS : (n + 1) * COLS].astype(BF16)


def wide(value):
    return jnp.broadcast_to(value, (2 * COLS, WIDE))


def across(value, like):
    return jnp.concatenate([value] * (like.shape[1] // WIDE), axis=1)


def add_row(table_ref, i, value):
    if i == 0:
        table_ref[...] = value
    else:
        table_ref[...] += value


def staged(first, second, third):
    held = first(0)
    for i in range(ROWS):
        done = second(i, *held)
        if i + 1 < ROWS:
            following = first(i + 1)
        third(i, *done)
        held = following


def early_kernel(group, q_ref, da_ref, bias_ref, *refs):
    n = len(group)
    kv_refs, old_refs, (e_ref, *new_refs) = refs[:n], refs[n:-5], refs[-5:]
    acc_ref, total_ref, mass_ref, top_ref = new_refs

    def scores(i):
        kv = stack(kv_refs, i)
        return kv, mm(q_ref[i], kv, NT) + bias_ref[...], mm(da_ref[i], kv, NT)

    def weigh(i, kv, s, w):
        top = jnp.max(s, axis=1, keepdims=True)
        if old_refs:
            old = old_refs[3][i]
            top = jnp.maximum(top, old)
            fade = jnp.exp(old - top)
            e = jnp.exp(s - across(top, s))
        else:
            fade = None
            e = jnp.exp(s - top)
            top = wide(top)
        low = e.astype(BF16)
        e_ref[i] = low
        total = jnp.sum(e, axis=1, keepdims=True)
        mass = jnp.sum(e * w, axis=1, keepdims=True)
        if old_refs:
            total = total + old_refs[1][i] * fade
            mass = mass + old_refs[2][i] * fade
        total_ref[i] = wide(total)
        mass_ref[i] = wide(mass)
        top_ref[i] = top
        return kv, low, fade

    def gather(i, kv, low, fade):
        acc = mm(low, kv, NN)
        acc_ref[i] = acc + old_refs[0][i] * fade if old_refs else acc

    staged(scores, weigh, gather)


def early(group, q, da, bias, kvs, state):
    return pl.pallas_call(
        functools.partial(early_kernel, group),
        out_shape=[jax.ShapeDtypeStruct((ROWS, 2 * COLS, 2 * len(group) * COLS), BF16)]
        + [STATE] * 4,
        compiler_params=params(),
        cost_estimate=cost(4.0),
        name="early",
    )(q, da, bias, *[kvs[r] for r in group], *state)


def turn_kernel(
    q_ref, da_ref, qt_ref, dat_ref, bias_ref, near_top_ref,
    acc_ref, total_ref, mass_ref, top_ref, *refs,
):
    n = len(LATE)
    kv_refs, (u_ref, dot_ref, factor_ref, near_factor_ref) = refs[:n], refs[n : n + 4]
    dkv_refs, table_ref = refs[n + 4 : 2 * n + 4], refs[-1]
    lane = lanes((2 * COLS, WIDE))

    def scores(i):
        kv = stack(kv_refs, i)
        return kv, mm(q_ref[i], kv, NT) + bias_ref[...], mm(da_ref[i], kv, NT)

    def weigh(i, kv, s, w):
        old = top_ref[i]
        top = jnp.maximum(jnp.max(s, axis=1, keepdims=True), old)
        fade = jnp.exp(old - top)
        e = jnp.exp(s - across(top, s))
        inverse = 1.0 / (jnp.sum(e, axis=1, keepdims=True) + total_ref[i] * fade)
        factor = fade * inverse
        dot = (jnp.sum(e * w, axis=1, keepdims=True) + mass_ref[i] * fade) * inverse
        factor_ref[i] = factor
        near_factor_ref[i] = jnp.exp(near_top_ref[i] - top) * inverse
        dot_ref[i] = dot
        p = e * across(inverse, e)
        d = p * (w - across(dot, p))
        add_row(table_ref, i, d)
        return kv, p.astype(BF16), d.astype(BF16), factor

    def gather(i, kv, p_low, low, factor):
        key_gradients(qt_ref[i], dat_ref[i], low, p_low, dkv_refs, i)
        acc = mm(p_low, kv, NN) + acc_ref[i] * factor
        u_ref[i] = jnp.where(lane < DH, mm(low, kv, NN), acc)

    staged(scores, weigh, gather)


def turn(q, da, qt, dat, bias, near_top, state, kvs):
    return pl.pallas_call(
        turn_kernel,
        out_shape=[STATE] * 4
        + [BLOCK] * len(LATE)
        + [jax.ShapeDtypeStruct((2 * COLS, NL), F32)],
        compiler_params=params(),
        cost_estimate=cost(3.0),
        name="turn",
    )(q, da, qt, dat, bias, near_top, *state, *[kvs[r] for r in LATE])


def backward_kernel(
    group, _, da_ref, qt_ref, dat_ref, part_ref, dot_ref, factor_ref, e_ref, *refs
):
    n = len(group)
    kv_refs, u_ref, dkv_refs, table_ref = refs[:n], refs[n], refs[n + 1 : 2 * n + 1], refs[2 * n + 1]
    lane = lanes((2 * COLS, WIDE))

    def scores(i):
        kv = stack(kv_refs, i)
        return kv, mm(da_ref[i], kv, NT)

    def weigh(i, kv, w):
        p = e_ref[i].astype(F32)
        p = p * across(factor_ref[i], p)
        d = p * (w - across(dot_ref[i], p))
        add_row(table_ref, i, d)
        return kv, p.astype(BF16), d.astype(BF16)

    def gather(i, kv, p_low, low):
        u = part_ref[i]
        u_ref[i] = jnp.where(lane < DH, u + mm(low, kv, NN), u)
        key_gradients(qt_ref[i], dat_ref[i], low, p_low, dkv_refs, i)

    staged(scores, weigh, gather)


def backward(group, after, da, qt, dat, state, e, kvs, time):
    n = len(group)
    out = pl.pallas_call(
        functools.partial(backward_kernel, group),
        in_specs=[pl.BlockSpec(memory_space=pl.ANY)]
        + [pl.BlockSpec(memory_space=pltpu.VMEM)] * (7 + n),
        out_shape=[STATE]
        + [BLOCK] * n
        + [jax.ShapeDtypeStruct((2 * COLS, 2 * n * COLS), F32)],
        compiler_params=params(),
        cost_estimate=cost(time),
        name="backward",
    )(after, da, qt, dat, *state, e, *[kvs[r] for r in group])
    return out[0], dict(zip(group, out[1 : n + 1])), out[-1]


def split_kernel(near_ref, far_ref, late_ref, keep_ref, send_ref):
    core = lax.axis_index("core")
    z = lax.axis_index("z")

    def write(even_ref, odd_ref):
        for group, table in ((NEAR, near_ref), (FAR, far_ref), (LATE, late_ref)):
            for m, r in enumerate(group):
                ref = odd_ref if r % 2 else even_ref
                x = lax.rem(z + r, RING) // 2
                for yh in range(2):
                    start = (yh * len(group) + m) * COLS
                    for yl in range(2):
                        piece = table[yl * COLS : (yl + 1) * COLS, start : start + COLS]
                        ref[yh, x, yl] = piece.astype(ref.dtype)

    @pl.when(lax.rem(z + core, 2) == 0)
    def _():
        write(keep_ref, send_ref)

    @pl.when(lax.rem(z + core, 2) != 0)
    def _():
        write(send_ref, keep_ref)


def split_tables(near, far, late):
    blocks = (2, 4, 2, COLS, COLS)
    return pl.pallas_call(
        split_kernel,
        out_shape=[jax.ShapeDtypeStruct(blocks, F32), jax.ShapeDtypeStruct(blocks, BF16)],
        compiler_params=params(),
        cost_estimate=cost(1.0),
        name="split_tables",
    )(near, far, late)


def relay_kernel(up_ref, part_ref, keep_ref, recv_ref, sent_ref, summed_ref):
    sent_ref[...] = (up_ref[...].astype(F32) + part_ref[...].astype(F32)).astype(BF16)
    summed_ref[...] = (keep_ref[...] + recv_ref[...].astype(F32)).astype(BF16)


def relay(up, part, keep, recv):
    return pl.pallas_call(
        relay_kernel,
        out_shape=[BLOCK, jax.ShapeDtypeStruct(keep.shape, BF16)],
        compiler_params=params(),
        cost_estimate=cost(0.8),
        name="relay",
    )(up, part, keep, recv)


def gather_kernel(u_ref, a_ref, b_ref, near_ref, far_ref):
    lane = lanes((COLS, WIDE))
    lane2 = lanes((2 * COLS, WIDE))
    for i in range(ROWS):
        dkv = a_ref[i].astype(F32) + b_ref[i].astype(F32)
        u = jnp.where(lane2 < DH, u_ref[i] * SCALE, u_ref[i])
        u = pltpu.roll(u, 2 * DH, 1)
        near_ref[i] = jnp.where(lane < 2 * DH, dkv, u[:COLS])
        far_ref[i] = jnp.where(lane < 2 * DH, pltpu.roll(dkv, 2 * DH, 1), u[COLS:])


def gather_parts(u, a, b):
    shape = jax.ShapeDtypeStruct((ROWS, COLS, WIDE), F32)
    return pl.pallas_call(
        gather_kernel,
        out_shape=[shape, shape],
        compiler_params=params(),
        cost_estimate=cost(0.5),
        name="gather_parts",
    )(u, a, b)


def finish_kernel(first_ref, second_ref, last_ref, keep_ref, send_ref):
    yl = lax.axis_index("yl")
    lane = lanes((COLS, WIDE))

    def write(first_out, second_out):
        for i in range(ROWS):
            last = last_ref[i].astype(F32)
            first = first_ref[i] + jnp.where(lane < 2 * DH, last, 0.0)
            second = second_ref[i] + jnp.where(lane < 2 * DH, pltpu.roll(last, 2 * DH, 1), 0.0)
            first_out[i] = first.astype(first_out.dtype)
            second_out[i] = second.astype(second_out.dtype)

    @pl.when(yl == 0)
    def _():
        write(keep_ref, send_ref)

    @pl.when(yl != 0)
    def _():
        write(send_ref, keep_ref)


def finish(first, second, last):
    shape = (ROWS, COLS, WIDE)
    return pl.pallas_call(
        finish_kernel,
        out_shape=[jax.ShapeDtypeStruct(shape, F32), jax.ShapeDtypeStruct(shape, BF16)],
        compiler_params=params(),
        cost_estimate=cost(0.8),
        name="finish",
    )(first, second, last)


def product(value, gate, w, h):
    flat = (ROWS * COLS, WIDE)
    value = value.reshape(flat).astype(F32)
    value = jnp.where(lanes(flat) < 3 * DH, value, value * gate.reshape(flat)).astype(BF16)
    weight = jnp.where(h == 0, head_weight(w, 0).astype(F32), head_weight(w, 1).astype(F32))
    return mm(value, weight.astype(BF16), NT)


def keep_kernel(keep_ref, gate_ref, w_ref, out_ref):
    yl = lax.axis_index("yl")
    out_ref[...] = product(keep_ref[...], gate_ref[...], w_ref[...], yl)


def keep_product(keep, gate, w):
    return pl.pallas_call(
        keep_kernel,
        out_shape=jax.ShapeDtypeStruct((ROWS * COLS, WIDE), F32),
        compiler_params=params(),
        cost_estimate=cost(0.5),
        name="keep_product",
    )(keep, gate, w)


def table_kernel(parts_ref, bias_ref):
    for h in range(H):
        bias_ref[h] = sum(parts_ref[n * H + h].astype(F32) for n in range(8))


def table_sum(parts):
    return pl.pallas_call(
        table_kernel,
        out_shape=jax.ShapeDtypeStruct((H, COLS, COLS), F32),
        compiler_params=params(),
        cost_estimate=cost(0.3),
        name="table_sum",
    )(parts)


def output_kernel(kept_ref, recv_ref, gate_ref, w_ref, out_ref):
    yl = lax.axis_index("yl")
    other = product(recv_ref[...], gate_ref[...], w_ref[...], 1 - yl)
    out_ref[...] = (kept_ref[...] + other).astype(BF16).reshape(ROWS, COLS, WIDE)


def output(kept, recv, gate, w):
    return pl.pallas_call(
        output_kernel,
        out_shape=BLOCK,
        compiler_params=params(),
        cost_estimate=cost(0.5),
        name="output",
    )(kept, recv, gate, w)


def shift(value, step):
    return lax.ppermute(value, "z", [(z, (z + step) % RING) for z in range(RING)])


def swap(value, axis):
    return lax.ppermute(value, axis, [(0, 1), (1, 0)])


def added(a, b):
    return (a.astype(F32) + b.astype(F32)).astype(BF16)


def body(pair, w_qkvg, w_out, bias, chain_lengths, d_pair_out):
    peers = ("yh", "x", "yl")
    oth = swap(bias, "core")
    mine, other, lift = project(chain_lengths, pair, d_pair_out, w_qkvg, w_out)
    recv = swap(other, "yl")
    wanted = want(bias, oth)
    everything = lax.all_to_all(wanted, peers, 0, 0, tiled=True)
    kv, q, da, qt, dat = pack(mine, recv, wanted)
    kvs = [kv] + [None] * (RING - 1)
    kvs[1] = shift(kv, -1)
    kvs[7] = shift(kv, 1)
    kvs[2] = shift(kvs[1], -1)
    kvs[6] = shift(kvs[7], 1)
    kvs[3] = shift(kvs[2], -1)
    bias_near, bias_far, bias_late = bias_tables(lift, everything)
    e_near, *state = early(NEAR, q, da, bias_near, kvs, ())
    near_top = state[-1]
    kvs[4] = shift(join(kvs[3], near_top), -1)
    kvs[5] = shift(kvs[6], 1)
    e_far, *state = early(FAR, q, da, bias_far, kvs, state)
    u, dot, factor, near_factor, d4, d5, t_late = turn(
        q, da, qt, dat, bias_late, near_top, state, kvs
    )
    up = shift(d4, 1)
    down = shift(d5, -1)
    u, far, t_far = backward(FAR, d4, da, qt, dat, (u, dot, factor), e_far, kvs, 2.5)
    sent = added(up, far[3])
    up = shift(sent, 1)
    down = shift(added(down, far[6]), -1)
    u, near, t_near = backward(NEAR, sent, da, qt, dat, (u, dot, near_factor), e_near, kvs, 3.0)
    keep_table, send_table = split_tables(t_near, t_far, t_late)
    recv_table = swap(send_table, "core")
    sent3 = added(up, near[2])
    up = shift(sent3, 1)
    down = shift(added(down, near[7]), -1)
    up, summed = relay(up, near[1], keep_table, recv_table)
    up = shift(up, 1)
    parts = lax.all_to_all(summed.reshape(16, COLS, COLS), peers, 0, 0, tiled=True)
    gmine, gother = slopes(sent3, pair, d_pair_out, w_qkvg, w_out)
    first, second = gather_parts(u, near[0], down)
    keep, send = finish(first, second, up)
    recv = swap(send, "yl")
    kept = keep_product(keep, gmine, w_qkvg)
    return output(kept, recv, gother, w_qkvg), table_sum(parts)


def solution(mesh):
    split = Mesh(mesh.devices.reshape(2, 4, 2, 2, RING), ("yh", "x", "core", "yl", "z"))
    row, col = ("yh", "x", "core"), ("yl", "z")
    in_specs = (P(row, col, None), P(), P(), P(None, col, row), P(), P(row, col, None))
    out_specs = (P(row, col, None), P(None, col, row))
    return jax.shard_map(body, mesh=split, in_specs=in_specs, out_specs=out_specs, check_vma=False)
```

```python
import functools
import math

import jax
import jax.numpy as jnp
from jax import lax
from jax.experimental import pallas as pl
from jax.experimental.pallas import tpu as pltpu
from jax.sharding import Mesh, PartitionSpec as P

H = 2
DH = 32
CHAINS = 8
SCALE = 1.0 / math.sqrt(DH)
MASKED_SCORE = -1e30
F32 = jnp.float32
BF16 = jnp.bfloat16

ROWS = 6
COLS = 96
RING = 8
HALF = RING * COLS
KEYS = 2 * HALF
WIDE = 128
NEAR = (0, 1, 7, 2, 6)
LATE = (3, 4, 5)
NC, NL = (2 * len(group) * COLS for group in (NEAR, LATE))


NT = (((1,), (1,)), ((), ()))
NN = (((1,), (0,)), ((), ()))
TN = (((0,), (0,)), ((), ()))


def mm(a, b, dims):
    return lax.dot_general(a, b, dims, preferred_element_type=F32)


def params(limit=32 << 20):
    return pltpu.CompilerParams(vmem_limit_bytes=limit)


def cost(us):
    return pl.CostEstimate(flops=0, bytes_accessed=int(us * 1e5), transcendentals=0)


def lanes(shape):
    return lax.broadcasted_iota(jnp.int32, shape, len(shape) - 1)


def head_weight(w, h):
    parts = [w[:, (part * H + h) * DH : (part * H + h + 1) * DH] for part in (1, 2, 0, 3)]
    return jnp.concatenate(parts, axis=1)


def project_kernel(
    len_hbm, pair_hbm, grad_hbm, w_hbm, wout_hbm,
    mine_ref, other_ref, lift_ref,
    len_s, pair_s, grad_s, w_s, wout_s, sem,
):
    yl = lax.axis_index("yl")
    pairs = (
        (len_hbm, len_s), (w_hbm, w_s), (wout_hbm, wout_s),
        (pair_hbm, pair_s), (grad_hbm, grad_s),
    )
    copies = [pltpu.make_async_copy(a, b, sem.at[n]) for n, (a, b) in enumerate(pairs)]
    for copy in copies:
        copy.start()
    copies[0].wait()
    for c in range(CHAINS):
        for half in range(2):
            position = lanes((1, COLS)) + half * COLS
            lift_ref[2 * c + half] = jnp.where(position < len_s[c], 0.0, MASKED_SCORE)
    for copy in copies[1:]:
        copy.wait()
    pair = pair_s[...].reshape(ROWS * COLS, WIDE)
    grad = grad_s[...].reshape(ROWS * COLS, WIDE)
    w = w_s[...]
    wout = wout_s[...]
    lane = lanes((ROWS * COLS, WIDE))
    for h in range(H):
        proj = mm(pair, head_weight(w, h), NN)
        rows = jnp.concatenate(
            [jnp.zeros((WIDE - DH, WIDE), BF16), wout[h * DH : (h + 1) * DH]], axis=0
        )
        d_out = mm(grad, rows, NT)
        gate = jax.nn.sigmoid(proj)
        payload = jnp.where(
            lane < 2 * DH, proj, jnp.where(lane < 3 * DH, proj * SCALE, d_out * gate)
        )
        payload = payload.astype(BF16).reshape(ROWS, COLS, WIDE)

        @pl.when(yl == h)
        def _():
            mine_ref[...] = payload

        @pl.when(yl != h)
        def _():
            other_ref[...] = payload


def project(chain_lengths, pair, grad, w, wout):
    shape = (ROWS, COLS, WIDE)
    arrays = (chain_lengths, pair, grad, w, wout)
    arrays = [pltpu.with_memory_space_constraint(array, pltpu.HBM) for array in arrays]
    return pl.pallas_call(
        project_kernel,
        in_specs=[pl.BlockSpec(memory_space=pltpu.HBM)] * 5,
        out_shape=[
            jax.ShapeDtypeStruct(shape, BF16),
            jax.ShapeDtypeStruct(shape, BF16),
            jax.ShapeDtypeStruct((2 * CHAINS, 1, COLS), F32),
        ],
        scratch_shapes=[
            pltpu.SMEM((CHAINS,), jnp.int32),
            pltpu.VMEM(shape, BF16),
            pltpu.VMEM(shape, BF16),
            pltpu.VMEM(w.shape, BF16),
            pltpu.VMEM(wout.shape, BF16),
            pltpu.SemaphoreType.DMA((5,)),
        ],
        compiler_params=params(),
        cost_estimate=cost(2.0),
        name="project",
    )(*arrays)


def slope_kernel(
    _, pair_hbm, grad_hbm, w_hbm, wout_hbm, gmine_ref, gother_ref, pair_s, grad_s, w_s, wout_s, sem
):
    yl = lax.axis_index("yl")
    pairs = ((w_hbm, w_s), (wout_hbm, wout_s), (pair_hbm, pair_s), (grad_hbm, grad_s))
    copies = [pltpu.make_async_copy(a, b, sem.at[n]) for n, (a, b) in enumerate(pairs)]
    for copy in copies:
        copy.start()
    for copy in copies:
        copy.wait()
    pair = pair_s[...].reshape(ROWS * COLS, WIDE)
    grad = grad_s[...].reshape(ROWS * COLS, WIDE)
    zeros = jnp.zeros((WIDE - DH, WIDE), BF16)
    for h in range(H):
        gate = jax.nn.sigmoid(mm(pair, head_weight(w_s[...], h), NN))
        rows = jnp.concatenate([zeros, wout_s[h * DH : (h + 1) * DH]], axis=0)
        g = mm(grad, rows, NT) * gate * (1.0 - gate)

        @pl.when(yl == h)
        def _():
            gmine_ref[...] = g.reshape(ROWS, COLS, WIDE)

        @pl.when(yl != h)
        def _():
            gother_ref[...] = g.reshape(ROWS, COLS, WIDE)


def slopes(after, pair, grad, w, wout):
    shape = (ROWS, COLS, WIDE)
    arrays = [pltpu.with_memory_space_constraint(array, pltpu.HBM) for array in (pair, grad, w, wout)]
    return pl.pallas_call(
        slope_kernel,
        in_specs=[pl.BlockSpec(memory_space=pl.ANY)] + [pl.BlockSpec(memory_space=pltpu.HBM)] * 4,
        out_shape=[jax.ShapeDtypeStruct(shape, F32)] * 2,
        scratch_shapes=[
            pltpu.VMEM(shape, BF16),
            pltpu.VMEM(shape, BF16),
            pltpu.VMEM(w.shape, BF16),
            pltpu.VMEM(wout.shape, BF16),
            pltpu.SemaphoreType.DMA((4,)),
        ],
        compiler_params=params(),
        cost_estimate=cost(2.0),
        name="slopes",
    )(after, *arrays)


def pack_kernel(mine_ref, recv_ref, _, kv_ref, q_ref, da_ref, qt_ref, dat_ref):
    yl = lax.axis_index("yl")
    lane = lanes((COLS, WIDE))

    def write(i, a, b):
        a, b = a.astype(F32), b.astype(F32)
        kv_ref[i] = jnp.where(lane < 2 * DH, a, pltpu.roll(b, 2 * DH, 1)).astype(BF16)
        for part, x in enumerate((a, b)):
            y = pltpu.roll(x, 2 * DH, 1)
            rows = slice(part * COLS, (part + 1) * COLS)
            q_ref[i, rows] = jnp.where(lane < DH, y, 0.0).astype(BF16)
            da_ref[i, rows] = jnp.where((lane >= DH) & (lane < 2 * DH), y, 0.0).astype(BF16)
        turned = jnp.concatenate([a, b], axis=0).T
        qt_ref[i] = turned[2 * DH : 3 * DH].astype(BF16)
        dat_ref[i] = turned[3 * DH :].astype(BF16)

    for i in range(ROWS):

        @pl.when(yl == 0)
        def _():
            write(i, mine_ref[i], recv_ref[i])

        @pl.when(yl != 0)
        def _():
            write(i, recv_ref[i], mine_ref[i])


BLOCK = jax.ShapeDtypeStruct((ROWS, COLS, WIDE), BF16)
STATE = jax.ShapeDtypeStruct((ROWS, 2 * COLS, WIDE), F32)


def pack(mine, recv, after):
    both = jax.ShapeDtypeStruct((ROWS, 2 * COLS, WIDE), BF16)
    turned = jax.ShapeDtypeStruct((ROWS, DH, 2 * COLS), BF16)
    return pl.pallas_call(
        pack_kernel,
        in_specs=[pl.BlockSpec(memory_space=pltpu.VMEM)] * 2 + [pl.BlockSpec(memory_space=pl.ANY)],
        out_shape=[BLOCK, both, both, turned, turned],
        compiler_params=params(),
        cost_estimate=cost(0.6),
        name="pack",
    )(mine, recv, after)


EXCHANGE = jax.ShapeDtypeStruct((16, 2, COLS, COLS), BF16)


def want_kernel(own_ref, oth_ref, out_ref):
    core = lax.axis_index("core")
    for h in range(H):
        for n in range(8):
            out_ref[n * H + h, core] = own_ref[h]
            out_ref[n * H + h, 1 - core] = oth_ref[h]


def want(own, oth):
    return pl.pallas_call(
        want_kernel,
        out_shape=EXCHANGE,
        compiler_params=params(),
        cost_estimate=cost(0.4),
        name="want",
    )(own, oth)


def bias_kernel(lift_ref, all_ref, near_ref, late_ref):
    z = lax.axis_index("z")
    for group, out_ref in ((NEAR, near_ref), (LATE, late_ref)):
        for n, r in enumerate(group):
            at = lax.rem(z + r, RING)
            x, odd = at // 2, lax.rem(at, 2)
            for yh in range(2):
                start = (yh * len(group) + n) * COLS
                lift = lift_ref[yh * CHAINS + at]
                for yl in range(2):
                    rows = slice(yl * COLS, (yl + 1) * COLS)
                    block = all_ref[(yh * 4 + x) * 2 + yl, odd].astype(F32)
                    out_ref[rows, start : start + COLS] = block + lift


def bias_tables(lift, everything):
    return pl.pallas_call(
        bias_kernel,
        out_shape=[
            jax.ShapeDtypeStruct((2 * COLS, NC), F32),
            jax.ShapeDtypeStruct((2 * COLS, NL), F32),
        ],
        compiler_params=params(),
        cost_estimate=cost(0.5),
        name="bias_tables",
    )(lift, everything)


def join_kernel(block_ref, _, out_ref):
    out_ref[...] = block_ref[...]


def join(block, after):
    return pl.pallas_call(
        join_kernel,
        in_specs=[pl.BlockSpec(memory_space=pltpu.VMEM), pl.BlockSpec(memory_space=pl.ANY)],
        out_shape=BLOCK,
        compiler_params=params(),
        cost_estimate=cost(0.2),
        name="join",
    )(block, after)


def stack(refs, i):
    one = jnp.concatenate([ref[i] for ref in refs], axis=0)
    moved = pltpu.roll(one.astype(F32), 2 * DH, 1).astype(BF16)
    return jnp.concatenate([one, moved], axis=0)


def key_gradients(qt, dat, low, p_low, dkv_refs, i):
    dk = mm(qt, low, NN)
    dv = mm(dat, p_low, NN)
    half = dk.shape[1] // 2
    dkv = jnp.concatenate([dk[:, :half], dv[:, :half], dk[:, half:], dv[:, half:]], axis=0).T
    for n, ref in enumerate(dkv_refs):
        ref[i] = dkv[n * COLS : (n + 1) * COLS].astype(BF16)


def wide(value):
    return jnp.broadcast_to(value, (2 * COLS, WIDE))


def across(value, like):
    width = like.shape[1]
    return jnp.concatenate([value] * pl.cdiv(width, WIDE), axis=1)[:, :width]


def add_row(table_ref, i, value):
    if i == 0:
        table_ref[...] = value
    else:
        table_ref[...] += value


def staged(first, second, third):
    held = first(0)
    for i in range(ROWS):
        done = second(i, *held)
        if i + 1 < ROWS:
            following = first(i + 1)
        third(i, *done)
        held = following


def early_kernel(q_ref, da_ref, bias_ref, *refs):
    n = len(NEAR)
    kv_refs, (e_ref, acc_ref, total_ref, mass_ref, top_ref) = refs[:n], refs[n:]

    def scores(i):
        kv = stack(kv_refs, i)
        return kv, mm(q_ref[i], kv, NT) + bias_ref[...], mm(da_ref[i], kv, NT)

    def weigh(i, kv, s, w):
        top = jnp.max(s, axis=1, keepdims=True)
        e = jnp.exp(s - top)
        low = e.astype(BF16)
        e_ref[i] = low
        total_ref[i] = wide(jnp.sum(e, axis=1, keepdims=True))
        mass_ref[i] = wide(jnp.sum(e * w, axis=1, keepdims=True))
        top_ref[i] = wide(top)
        return kv, low

    def gather(i, kv, low):
        acc_ref[i] = mm(low, kv, NN)

    staged(scores, weigh, gather)


def early(q, da, bias, kvs):
    return pl.pallas_call(
        early_kernel,
        out_shape=[jax.ShapeDtypeStruct((ROWS, 2 * COLS, NC), BF16)] + [STATE] * 4,
        compiler_params=params(),
        cost_estimate=cost(4.0),
        name="early",
    )(q, da, bias, *[kvs[r] for r in NEAR])


def turn_kernel(
    q_ref, da_ref, qt_ref, dat_ref, bias_ref, acc_ref, total_ref, mass_ref, top_ref, *refs
):
    n = len(LATE)
    kv_refs, (u_ref, dot_ref, factor_ref) = refs[:n], refs[n : n + 3]
    dkv_refs, table_ref = refs[n + 3 : 2 * n + 3], refs[-1]
    lane = lanes((2 * COLS, WIDE))

    def scores(i):
        kv = stack(kv_refs, i)
        return kv, mm(q_ref[i], kv, NT) + bias_ref[...], mm(da_ref[i], kv, NT)

    def weigh(i, kv, s, w):
        old = top_ref[i]
        top = jnp.maximum(jnp.max(s, axis=1, keepdims=True), old)
        fade = jnp.exp(old - top)
        e = jnp.exp(s - across(top, s))
        inverse = 1.0 / (jnp.sum(e, axis=1, keepdims=True) + total_ref[i] * fade)
        factor = fade * inverse
        dot = (jnp.sum(e * w, axis=1, keepdims=True) + mass_ref[i] * fade) * inverse
        factor_ref[i] = factor
        dot_ref[i] = dot
        p = e * across(inverse, e)
        d = p * (w - across(dot, p))
        add_row(table_ref, i, d)
        return kv, p.astype(BF16), d.astype(BF16), factor

    def gather(i, kv, p_low, low, factor):
        key_gradients(qt_ref[i], dat_ref[i], low, p_low, dkv_refs, i)
        acc = mm(p_low, kv, NN) + acc_ref[i] * factor
        u_ref[i] = jnp.where(lane < DH, mm(low, kv, NN), acc)

    staged(scores, weigh, gather)


def turn(q, da, qt, dat, bias, state, kvs):
    return pl.pallas_call(
        turn_kernel,
        out_shape=[STATE] * 3
        + [BLOCK] * len(LATE)
        + [jax.ShapeDtypeStruct((2 * COLS, NL), F32)],
        compiler_params=params(),
        cost_estimate=cost(3.0),
        name="turn",
    )(q, da, qt, dat, bias, *state, *[kvs[r] for r in LATE])


def backward_kernel(
    group, _, da_ref, qt_ref, dat_ref, part_ref, dot_ref, factor_ref, e_ref, *refs
):
    n = len(group)
    kv_refs, u_ref, dkv_refs, table_ref = refs[:n], refs[n], refs[n + 1 : 2 * n + 1], refs[2 * n + 1]
    lane = lanes((2 * COLS, WIDE))

    def scores(i):
        kv = stack(kv_refs, i)
        return kv, mm(da_ref[i], kv, NT)

    def weigh(i, kv, w):
        p = e_ref[i].astype(F32)
        p = p * across(factor_ref[i], p)
        d = p * (w - across(dot_ref[i], p))
        add_row(table_ref, i, d)
        return kv, p.astype(BF16), d.astype(BF16)

    def gather(i, kv, p_low, low):
        u = part_ref[i]
        u_ref[i] = jnp.where(lane < DH, u + mm(low, kv, NN), u)
        key_gradients(qt_ref[i], dat_ref[i], low, p_low, dkv_refs, i)

    staged(scores, weigh, gather)


def backward(group, after, da, qt, dat, state, e, kvs, time):
    n = len(group)
    out = pl.pallas_call(
        functools.partial(backward_kernel, group),
        in_specs=[pl.BlockSpec(memory_space=pl.ANY)]
        + [pl.BlockSpec(memory_space=pltpu.VMEM)] * (7 + n),
        out_shape=[STATE]
        + [BLOCK] * n
        + [jax.ShapeDtypeStruct((2 * COLS, 2 * n * COLS), F32)],
        compiler_params=params(),
        cost_estimate=cost(time),
        name="backward",
    )(after, da, qt, dat, *state, e, *[kvs[r] for r in group])
    return out[0], dict(zip(group, out[1 : n + 1])), out[-1]


def split_kernel(near_ref, late_ref, keep_ref, send_ref):
    core = lax.axis_index("core")
    z = lax.axis_index("z")

    def write(even_ref, odd_ref):
        for group, table in ((NEAR, near_ref), (LATE, late_ref)):
            for m, r in enumerate(group):
                ref = odd_ref if r % 2 else even_ref
                x = lax.rem(z + r, RING) // 2
                for yh in range(2):
                    start = (yh * len(group) + m) * COLS
                    for yl in range(2):
                        piece = table[yl * COLS : (yl + 1) * COLS, start : start + COLS]
                        ref[yh, x, yl] = piece.astype(ref.dtype)

    @pl.when(lax.rem(z + core, 2) == 0)
    def _():
        write(keep_ref, send_ref)

    @pl.when(lax.rem(z + core, 2) != 0)
    def _():
        write(send_ref, keep_ref)


def split_tables(near, late):
    blocks = (2, 4, 2, COLS, COLS)
    return pl.pallas_call(
        split_kernel,
        out_shape=[jax.ShapeDtypeStruct(blocks, F32), jax.ShapeDtypeStruct(blocks, BF16)],
        compiler_params=params(),
        cost_estimate=cost(1.0),
        name="split_tables",
    )(near, late)


def relay_kernel(
    up_ref, near_ref, down_ref, far_ref, keep_ref, recv_ref, up_out, down_out, summed_ref
):
    up_out[...] = (up_ref[...].astype(F32) + near_ref[...].astype(F32)).astype(BF16)
    down_out[...] = (down_ref[...].astype(F32) + far_ref[...].astype(F32)).astype(BF16)
    summed_ref[...] = (keep_ref[...] + recv_ref[...].astype(F32)).astype(BF16)


def relay(up, near, down, far, keep, recv):
    return pl.pallas_call(
        relay_kernel,
        out_shape=[BLOCK, BLOCK, jax.ShapeDtypeStruct(keep.shape, BF16)],
        compiler_params=params(),
        cost_estimate=cost(0.8),
        name="relay",
    )(up, near, down, far, keep, recv)


def gather_kernel(u_ref, a_ref, b_ref, near_ref, far_ref):
    lane = lanes((COLS, WIDE))
    lane2 = lanes((2 * COLS, WIDE))
    for i in range(ROWS):
        dkv = a_ref[i].astype(F32) + b_ref[i].astype(F32)
        u = jnp.where(lane2 < DH, u_ref[i] * SCALE, u_ref[i])
        u = pltpu.roll(u, 2 * DH, 1)
        near_ref[i] = jnp.where(lane < 2 * DH, dkv, u[:COLS])
        far_ref[i] = jnp.where(lane < 2 * DH, pltpu.roll(dkv, 2 * DH, 1), u[COLS:])


def gather_parts(u, a, b):
    shape = jax.ShapeDtypeStruct((ROWS, COLS, WIDE), F32)
    return pl.pallas_call(
        gather_kernel,
        out_shape=[shape, shape],
        compiler_params=params(),
        cost_estimate=cost(0.5),
        name="gather_parts",
    )(u, a, b)


def finish_kernel(first_ref, second_ref, last_ref, keep_ref, send_ref):
    yl = lax.axis_index("yl")
    lane = lanes((COLS, WIDE))

    def write(first_out, second_out):
        for i in range(ROWS):
            last = last_ref[i].astype(F32)
            first = first_ref[i] + jnp.where(lane < 2 * DH, last, 0.0)
            second = second_ref[i] + jnp.where(lane < 2 * DH, pltpu.roll(last, 2 * DH, 1), 0.0)
            first_out[i] = first.astype(first_out.dtype)
            second_out[i] = second.astype(second_out.dtype)

    @pl.when(yl == 0)
    def _():
        write(keep_ref, send_ref)

    @pl.when(yl != 0)
    def _():
        write(send_ref, keep_ref)


def finish(first, second, last):
    shape = (ROWS, COLS, WIDE)
    return pl.pallas_call(
        finish_kernel,
        out_shape=[jax.ShapeDtypeStruct(shape, F32), jax.ShapeDtypeStruct(shape, BF16)],
        compiler_params=params(),
        cost_estimate=cost(0.8),
        name="finish",
    )(first, second, last)


def product(value, gate, w, h):
    flat = (ROWS * COLS, WIDE)
    value = value.reshape(flat).astype(F32)
    value = jnp.where(lanes(flat) < 3 * DH, value, value * gate.reshape(flat)).astype(BF16)
    weight = jnp.where(h == 0, head_weight(w, 0).astype(F32), head_weight(w, 1).astype(F32))
    return mm(value, weight.astype(BF16), NT)


def keep_kernel(keep_ref, gate_ref, w_ref, out_ref):
    yl = lax.axis_index("yl")
    out_ref[...] = product(keep_ref[...], gate_ref[...], w_ref[...], yl)


def keep_product(keep, gate, w):
    return pl.pallas_call(
        keep_kernel,
        out_shape=jax.ShapeDtypeStruct((ROWS * COLS, WIDE), F32),
        compiler_params=params(),
        cost_estimate=cost(0.5),
        name="keep_product",
    )(keep, gate, w)


def table_kernel(parts_ref, bias_ref):
    for h in range(H):
        bias_ref[h] = sum(parts_ref[n * H + h].astype(F32) for n in range(8))


def table_sum(parts):
    return pl.pallas_call(
        table_kernel,
        out_shape=jax.ShapeDtypeStruct((H, COLS, COLS), F32),
        compiler_params=params(),
        cost_estimate=cost(0.3),
        name="table_sum",
    )(parts)


def output_kernel(kept_ref, recv_ref, gate_ref, w_ref, out_ref):
    yl = lax.axis_index("yl")
    other = product(recv_ref[...], gate_ref[...], w_ref[...], 1 - yl)
    out_ref[...] = (kept_ref[...] + other).astype(BF16).reshape(ROWS, COLS, WIDE)


def output(kept, recv, gate, w):
    return pl.pallas_call(
        output_kernel,
        out_shape=BLOCK,
        compiler_params=params(),
        cost_estimate=cost(0.5),
        name="output",
    )(kept, recv, gate, w)


def shift(value, step):
    return lax.ppermute(value, "z", [(z, (z + step) % RING) for z in range(RING)])


def swap(value, axis):
    return lax.ppermute(value, axis, [(0, 1), (1, 0)])


def added(*parts):
    return sum(part.astype(F32) for part in parts).astype(BF16)


def body(pair, w_qkvg, w_out, bias, chain_lengths, d_pair_out):
    peers = ("yh", "x", "yl")
    oth = swap(bias, "core")
    mine, other, lift = project(chain_lengths, pair, d_pair_out, w_qkvg, w_out)
    recv = swap(other, "yl")
    wanted = want(bias, oth)
    everything = lax.all_to_all(wanted, peers, 0, 0, tiled=True)
    kv, q, da, qt, dat = pack(mine, recv, wanted)
    kvs = [kv] + [None] * (RING - 1)
    kvs[1] = shift(kv, -1)
    kvs[7] = shift(kv, 1)
    kvs[2] = shift(kvs[1], -1)
    kvs[6] = shift(kvs[7], 1)
    kvs[3] = shift(kvs[2], -1)
    kvs[4] = shift(kvs[2], -2)
    kvs[5] = shift(kvs[6], 1)
    bias_near, bias_late = bias_tables(lift, everything)
    e, *state = early(q, da, bias_near, kvs)
    u, dot, factor, d3, d4, d5, t_late = turn(q, da, qt, dat, bias_late, state, kvs)
    up, far, down = shift(d3, 1), shift(d4, 2), shift(d5, -1)
    u, near, t_near = backward(NEAR, d4, da, qt, dat, (u, dot, factor), e, kvs, 3.0)
    keep_table, send_table = split_tables(t_near, t_late)
    recv_table = swap(send_table, "core")
    sent = added(up, far, near[2])
    up = shift(sent, 1)
    down = shift(added(down, near[6]), -1)
    up, down, summed = relay(up, near[1], down, near[7], keep_table, recv_table)
    gmine, gother = slopes(up, pair, d_pair_out, w_qkvg, w_out)
    up, down = shift(up, 1), shift(down, -1)
    parts = lax.all_to_all(summed.reshape(16, COLS, COLS), peers, 0, 0, tiled=True)
    first, second = gather_parts(u, near[0], down)
    keep, send = finish(first, second, up)
    recv = swap(send, "yl")
    kept = keep_product(keep, gmine, w_qkvg)
    return output(kept, recv, gother, w_qkvg), table_sum(parts)


def solution(mesh):
    split = Mesh(mesh.devices.reshape(2, 4, 2, 2, RING), ("yh", "x", "core", "yl", "z"))
    row, col = ("yh", "x", "core"), ("yl", "z")
    in_specs = (P(row, col, None), P(), P(), P(None, col, row), P(), P(row, col, None))
    out_specs = (P(row, col, None), P(None, col, row))
    return jax.shard_map(body, mesh=split, in_specs=in_specs, out_specs=out_specs, check_vma=False)
```

```python
import functools
import math

import jax
import jax.numpy as jnp
from jax import lax
from jax.experimental import pallas as pl
from jax.experimental.pallas import tpu as pltpu
from jax.sharding import Mesh, PartitionSpec as P

H = 2
DH = 32
CHAINS = 8
SCALE = 1.0 / math.sqrt(DH)
MASKED_SCORE = -1e30
F32 = jnp.float32
BF16 = jnp.bfloat16

ROWS = 6
COLS = 96
RING = 8
HALF = RING * COLS
KEYS = 2 * HALF
WIDE = 128
NEAR = (0, 1, 7, 2, 6)
LATE = (3, 4, 5)
NC, NL = (2 * len(group) * COLS for group in (NEAR, LATE))


NT = (((1,), (1,)), ((), ()))
NN = (((1,), (0,)), ((), ()))
TN = (((0,), (0,)), ((), ()))


def mm(a, b, dims):
    return lax.dot_general(a, b, dims, preferred_element_type=F32)


def params(limit=32 << 20):
    return pltpu.CompilerParams(vmem_limit_bytes=limit)


def cost(us):
    return pl.CostEstimate(flops=0, bytes_accessed=int(us * 1e5), transcendentals=0)


def lanes(shape):
    return lax.broadcasted_iota(jnp.int32, shape, len(shape) - 1)


def head_weight(w, h):
    parts = [w[:, (part * H + h) * DH : (part * H + h + 1) * DH] for part in (1, 2, 0, 3)]
    return jnp.concatenate(parts, axis=1)


def project_kernel(
    len_hbm, bias_hbm, pair_hbm, grad_hbm, w_hbm, wout_hbm,
    mine_ref, other_ref, lift_ref, bias_ref,
    len_s, pair_s, grad_s, w_s, wout_s, sem,
):
    yl = lax.axis_index("yl")
    pairs = (
        (len_hbm, len_s), (w_hbm, w_s), (wout_hbm, wout_s),
        (pair_hbm, pair_s), (grad_hbm, grad_s), (bias_hbm, bias_ref),
    )
    copies = [pltpu.make_async_copy(a, b, sem.at[n]) for n, (a, b) in enumerate(pairs)]
    for copy in copies:
        copy.start()
    copies[0].wait()
    for c in range(CHAINS):
        for half in range(2):
            position = lanes((1, COLS)) + half * COLS
            lift_ref[2 * c + half] = jnp.where(position < len_s[c], 0.0, MASKED_SCORE)
    for copy in copies[1:]:
        copy.wait()
    pair = pair_s[...].reshape(ROWS * COLS, WIDE)
    grad = grad_s[...].reshape(ROWS * COLS, WIDE)
    w = w_s[...]
    wout = wout_s[...]
    lane = lanes((ROWS * COLS, WIDE))
    for h in range(H):
        proj = mm(pair, head_weight(w, h), NN)
        rows = jnp.concatenate(
            [jnp.zeros((WIDE - DH, WIDE), BF16), wout[h * DH : (h + 1) * DH]], axis=0
        )
        d_out = mm(grad, rows, NT)
        gate = jax.nn.sigmoid(proj)
        payload = jnp.where(
            lane < 2 * DH, proj, jnp.where(lane < 3 * DH, proj * SCALE, d_out * gate)
        )
        payload = payload.astype(BF16).reshape(ROWS, COLS, WIDE)

        @pl.when(yl == h)
        def _():
            mine_ref[...] = payload

        @pl.when(yl != h)
        def _():
            other_ref[...] = payload


def project(chain_lengths, bias, pair, grad, w, wout):
    shape = (ROWS, COLS, WIDE)
    arrays = (chain_lengths, bias, pair, grad, w, wout)
    arrays = [pltpu.with_memory_space_constraint(array, pltpu.HBM) for array in arrays]
    return pl.pallas_call(
        project_kernel,
        in_specs=[pl.BlockSpec(memory_space=pltpu.HBM)] * 6,
        out_shape=[
            jax.ShapeDtypeStruct(shape, BF16),
            jax.ShapeDtypeStruct(shape, BF16),
            jax.ShapeDtypeStruct((2 * CHAINS, 1, COLS), F32),
            jax.ShapeDtypeStruct(bias.shape, BF16),
        ],
        scratch_shapes=[
            pltpu.SMEM((CHAINS,), jnp.int32),
            pltpu.VMEM(shape, BF16),
            pltpu.VMEM(shape, BF16),
            pltpu.VMEM(w.shape, BF16),
            pltpu.VMEM(wout.shape, BF16),
            pltpu.SemaphoreType.DMA((6,)),
        ],
        compiler_params=params(),
        cost_estimate=cost(2.0),
        name="project",
    )(*arrays)


def slope_kernel(
    _, pair_hbm, grad_hbm, w_hbm, wout_hbm, gmine_ref, gother_ref, pair_s, grad_s, w_s, wout_s, sem
):
    yl = lax.axis_index("yl")
    pairs = ((w_hbm, w_s), (wout_hbm, wout_s), (pair_hbm, pair_s), (grad_hbm, grad_s))
    copies = [pltpu.make_async_copy(a, b, sem.at[n]) for n, (a, b) in enumerate(pairs)]
    for copy in copies:
        copy.start()
    for copy in copies:
        copy.wait()
    pair = pair_s[...].reshape(ROWS * COLS, WIDE)
    grad = grad_s[...].reshape(ROWS * COLS, WIDE)
    zeros = jnp.zeros((WIDE - DH, WIDE), BF16)
    for h in range(H):
        gate = jax.nn.sigmoid(mm(pair, head_weight(w_s[...], h), NN))
        rows = jnp.concatenate([zeros, wout_s[h * DH : (h + 1) * DH]], axis=0)
        g = mm(grad, rows, NT) * gate * (1.0 - gate)

        @pl.when(yl == h)
        def _():
            gmine_ref[...] = g.reshape(ROWS, COLS, WIDE)

        @pl.when(yl != h)
        def _():
            gother_ref[...] = g.reshape(ROWS, COLS, WIDE)


def slopes(after, pair, grad, w, wout):
    shape = (ROWS, COLS, WIDE)
    arrays = [pltpu.with_memory_space_constraint(array, pltpu.HBM) for array in (pair, grad, w, wout)]
    return pl.pallas_call(
        slope_kernel,
        in_specs=[pl.BlockSpec(memory_space=pl.ANY)] + [pl.BlockSpec(memory_space=pltpu.HBM)] * 4,
        out_shape=[jax.ShapeDtypeStruct(shape, F32)] * 2,
        scratch_shapes=[
            pltpu.VMEM(shape, BF16),
            pltpu.VMEM(shape, BF16),
            pltpu.VMEM(w.shape, BF16),
            pltpu.VMEM(wout.shape, BF16),
            pltpu.SemaphoreType.DMA((4,)),
        ],
        compiler_params=params(),
        cost_estimate=cost(2.0),
        name="slopes",
    )(after, *arrays)


def pack_kernel(mine_ref, recv_ref, _, kv_ref, q_ref, da_ref, qt_ref, dat_ref):
    yl = lax.axis_index("yl")
    lane = lanes((COLS, WIDE))

    def write(i, a, b):
        a, b = a.astype(F32), b.astype(F32)
        kv_ref[i] = jnp.where(lane < 2 * DH, a, pltpu.roll(b, 2 * DH, 1)).astype(BF16)
        for part, x in enumerate((a, b)):
            y = pltpu.roll(x, 2 * DH, 1)
            rows = slice(part * COLS, (part + 1) * COLS)
            q_ref[i, rows] = jnp.where(lane < DH, y, 0.0).astype(BF16)
            da_ref[i, rows] = jnp.where((lane >= DH) & (lane < 2 * DH), y, 0.0).astype(BF16)
        turned = jnp.concatenate([a, b], axis=0).T
        qt_ref[i] = turned[2 * DH : 3 * DH].astype(BF16)
        dat_ref[i] = turned[3 * DH :].astype(BF16)

    for i in range(ROWS):

        @pl.when(yl == 0)
        def _():
            write(i, mine_ref[i], recv_ref[i])

        @pl.when(yl != 0)
        def _():
            write(i, recv_ref[i], mine_ref[i])


BLOCK = jax.ShapeDtypeStruct((ROWS, COLS, WIDE), BF16)
STATE = jax.ShapeDtypeStruct((ROWS, 2 * COLS, WIDE), F32)


def pack(mine, recv, after):
    both = jax.ShapeDtypeStruct((ROWS, 2 * COLS, WIDE), BF16)
    turned = jax.ShapeDtypeStruct((ROWS, DH, 2 * COLS), BF16)
    return pl.pallas_call(
        pack_kernel,
        in_specs=[pl.BlockSpec(memory_space=pltpu.VMEM)] * 2 + [pl.BlockSpec(memory_space=pl.ANY)],
        out_shape=[BLOCK, both, both, turned, turned],
        compiler_params=params(),
        cost_estimate=cost(0.6),
        name="pack",
    )(mine, recv, after)


EXCHANGE = jax.ShapeDtypeStruct((16, 2, COLS, COLS), BF16)


def want_kernel(own_ref, oth_ref, out_ref):
    core = lax.axis_index("core")
    for h in range(H):
        for n in range(8):
            out_ref[n * H + h, core] = own_ref[h]
            out_ref[n * H + h, 1 - core] = oth_ref[h]


def want(own, oth):
    return pl.pallas_call(
        want_kernel,
        out_shape=EXCHANGE,
        compiler_params=params(),
        cost_estimate=cost(0.4),
        name="want",
    )(own, oth)


def bias_kernel(lift_ref, all_ref, near_ref, late_ref):
    z = lax.axis_index("z")
    for group, out_ref in ((NEAR, near_ref), (LATE, late_ref)):
        for n, r in enumerate(group):
            at = lax.rem(z + r, RING)
            x, odd = at // 2, lax.rem(at, 2)
            for yh in range(2):
                start = (yh * len(group) + n) * COLS
                lift = lift_ref[yh * CHAINS + at]
                for yl in range(2):
                    rows = slice(yl * COLS, (yl + 1) * COLS)
                    block = all_ref[(yh * 4 + x) * 2 + yl, odd].astype(F32)
                    out_ref[rows, start : start + COLS] = block + lift


def bias_tables(lift, everything):
    return pl.pallas_call(
        bias_kernel,
        out_shape=[
            jax.ShapeDtypeStruct((2 * COLS, NC), F32),
            jax.ShapeDtypeStruct((2 * COLS, NL), F32),
        ],
        compiler_params=params(),
        cost_estimate=cost(0.5),
        name="bias_tables",
    )(lift, everything)


def join_kernel(block_ref, _, out_ref):
    out_ref[...] = block_ref[...]


def join(block, after):
    return pl.pallas_call(
        join_kernel,
        in_specs=[pl.BlockSpec(memory_space=pltpu.VMEM), pl.BlockSpec(memory_space=pl.ANY)],
        out_shape=BLOCK,
        compiler_params=params(),
        cost_estimate=cost(0.2),
        name="join",
    )(block, after)


def stack(refs, i):
    one = jnp.concatenate([ref[i] for ref in refs], axis=0)
    moved = pltpu.roll(one.astype(F32), 2 * DH, 1).astype(BF16)
    return jnp.concatenate([one, moved], axis=0)


def key_gradients(qt, dat, low, p_low, dkv_refs, i):
    dk = mm(qt, low, NN)
    dv = mm(dat, p_low, NN)
    half = dk.shape[1] // 2
    dkv = jnp.concatenate([dk[:, :half], dv[:, :half], dk[:, half:], dv[:, half:]], axis=0).T
    for n, ref in enumerate(dkv_refs):
        ref[i] = dkv[n * COLS : (n + 1) * COLS].astype(BF16)


def wide(value):
    return jnp.broadcast_to(value, (2 * COLS, WIDE))


def across(value, like):
    width = like.shape[1]
    return jnp.concatenate([value] * pl.cdiv(width, WIDE), axis=1)[:, :width]


def add_row(table_ref, i, value):
    if i == 0:
        table_ref[...] = value
    else:
        table_ref[...] += value


def staged(first, second, third):
    held = first(0)
    for i in range(ROWS):
        done = second(i, *held)
        if i + 1 < ROWS:
            following = first(i + 1)
        third(i, *done)
        held = following


def early_kernel(q_ref, da_ref, bias_ref, *refs):
    n = len(NEAR)
    kv_refs, (e_ref, acc_ref, total_ref, mass_ref, top_ref) = refs[:n], refs[n:]

    def scores(i):
        kv = stack(kv_refs, i)
        return kv, mm(q_ref[i], kv, NT) + bias_ref[...], mm(da_ref[i], kv, NT)

    def weigh(i, kv, s, w):
        top = jnp.max(s, axis=1, keepdims=True)
        e = jnp.exp(s - top)
        low = e.astype(BF16)
        e_ref[i] = low
        total_ref[i] = wide(jnp.sum(e, axis=1, keepdims=True))
        mass_ref[i] = wide(jnp.sum(e * w, axis=1, keepdims=True))
        top_ref[i] = wide(top)
        return kv, low

    def gather(i, kv, low):
        acc_ref[i] = mm(low, kv, NN)

    staged(scores, weigh, gather)


def early(q, da, bias, kvs):
    return pl.pallas_call(
        early_kernel,
        out_shape=[jax.ShapeDtypeStruct((ROWS, 2 * COLS, NC), BF16)] + [STATE] * 4,
        compiler_params=params(),
        cost_estimate=cost(4.0),
        name="early",
    )(q, da, bias, *[kvs[r] for r in NEAR])


def turn_kernel(
    q_ref, da_ref, qt_ref, dat_ref, bias_ref, acc_ref, total_ref, mass_ref, top_ref, *refs
):
    n = len(LATE)
    kv_refs, (u_ref, dot_ref, factor_ref) = refs[:n], refs[n : n + 3]
    dkv_refs, table_ref = refs[n + 3 : 2 * n + 3], refs[-1]
    lane = lanes((2 * COLS, WIDE))

    def scores(i):
        kv = stack(kv_refs, i)
        return kv, mm(q_ref[i], kv, NT) + bias_ref[...], mm(da_ref[i], kv, NT)

    def weigh(i, kv, s, w):
        old = top_ref[i]
        top = jnp.maximum(jnp.max(s, axis=1, keepdims=True), old)
        fade = jnp.exp(old - top)
        e = jnp.exp(s - across(top, s))
        inverse = 1.0 / (jnp.sum(e, axis=1, keepdims=True) + total_ref[i] * fade)
        factor = fade * inverse
        dot = (jnp.sum(e * w, axis=1, keepdims=True) + mass_ref[i] * fade) * inverse
        factor_ref[i] = factor
        dot_ref[i] = dot
        p = e * across(inverse, e)
        d = p * (w - across(dot, p))
        add_row(table_ref, i, d)
        return kv, p.astype(BF16), d.astype(BF16), factor

    def gather(i, kv, p_low, low, factor):
        key_gradients(qt_ref[i], dat_ref[i], low, p_low, dkv_refs, i)
        acc = mm(p_low, kv, NN) + acc_ref[i] * factor
        u_ref[i] = jnp.where(lane < DH, mm(low, kv, NN), acc)

    staged(scores, weigh, gather)


def turn(q, da, qt, dat, bias, state, kvs):
    return pl.pallas_call(
        turn_kernel,
        out_shape=[STATE] * 3
        + [BLOCK] * len(LATE)
        + [jax.ShapeDtypeStruct((2 * COLS, NL), F32)],
        compiler_params=params(),
        cost_estimate=cost(3.0),
        name="turn",
    )(q, da, qt, dat, bias, *state, *[kvs[r] for r in LATE])


def backward_kernel(
    group, _, da_ref, qt_ref, dat_ref, part_ref, dot_ref, factor_ref, e_ref, *refs
):
    n = len(group)
    kv_refs, u_ref, dkv_refs, table_ref = refs[:n], refs[n], refs[n + 1 : 2 * n + 1], refs[2 * n + 1]
    lane = lanes((2 * COLS, WIDE))

    def scores(i):
        kv = stack(kv_refs, i)
        return kv, mm(da_ref[i], kv, NT)

    def weigh(i, kv, w):
        p = e_ref[i].astype(F32)
        p = p * across(factor_ref[i], p)
        d = p * (w - across(dot_ref[i], p))
        add_row(table_ref, i, d)
        return kv, p.astype(BF16), d.astype(BF16)

    def gather(i, kv, p_low, low):
        u = part_ref[i]
        u_ref[i] = jnp.where(lane < DH, u + mm(low, kv, NN), u)
        key_gradients(qt_ref[i], dat_ref[i], low, p_low, dkv_refs, i)

    staged(scores, weigh, gather)


def backward(group, after, da, qt, dat, state, e, kvs, time):
    n = len(group)
    out = pl.pallas_call(
        functools.partial(backward_kernel, group),
        in_specs=[pl.BlockSpec(memory_space=pl.ANY)]
        + [pl.BlockSpec(memory_space=pltpu.VMEM)] * (7 + n),
        out_shape=[STATE]
        + [BLOCK] * n
        + [jax.ShapeDtypeStruct((2 * COLS, 2 * n * COLS), F32)],
        compiler_params=params(),
        cost_estimate=cost(time),
        name="backward",
    )(after, da, qt, dat, *state, e, *[kvs[r] for r in group])
    return out[0], dict(zip(group, out[1 : n + 1])), out[-1]


def split_kernel(near_ref, late_ref, keep_ref, send_ref):
    core = lax.axis_index("core")
    z = lax.axis_index("z")

    def write(even_ref, odd_ref):
        for group, table in ((NEAR, near_ref), (LATE, late_ref)):
            for m, r in enumerate(group):
                ref = odd_ref if r % 2 else even_ref
                x = lax.rem(z + r, RING) // 2
                for yh in range(2):
                    start = (yh * len(group) + m) * COLS
                    for yl in range(2):
                        piece = table[yl * COLS : (yl + 1) * COLS, start : start + COLS]
                        ref[yh, x, yl] = piece.astype(ref.dtype)

    @pl.when(lax.rem(z + core, 2) == 0)
    def _():
        write(keep_ref, send_ref)

    @pl.when(lax.rem(z + core, 2) != 0)
    def _():
        write(send_ref, keep_ref)


def split_tables(near, late):
    blocks = (2, 4, 2, COLS, COLS)
    return pl.pallas_call(
        split_kernel,
        out_shape=[jax.ShapeDtypeStruct(blocks, F32), jax.ShapeDtypeStruct(blocks, BF16)],
        compiler_params=params(),
        cost_estimate=cost(1.0),
        name="split_tables",
    )(near, late)


def relay_kernel(
    up_ref, near_ref, down_ref, far_ref, keep_ref, recv_ref, up_out, down_out, summed_ref
):
    up_out[...] = (up_ref[...].astype(F32) + near_ref[...].astype(F32)).astype(BF16)
    down_out[...] = (down_ref[...].astype(F32) + far_ref[...].astype(F32)).astype(BF16)
    summed_ref[...] = (keep_ref[...] + recv_ref[...].astype(F32)).astype(BF16)


def relay(up, near, down, far, keep, recv):
    return pl.pallas_call(
        relay_kernel,
        out_shape=[BLOCK, BLOCK, jax.ShapeDtypeStruct(keep.shape, BF16)],
        compiler_params=params(),
        cost_estimate=cost(0.8),
        name="relay",
    )(up, near, down, far, keep, recv)


def gather_kernel(u_ref, a_ref, b_ref, c_ref, near_ref, far_ref):
    lane = lanes((COLS, WIDE))
    lane2 = lanes((2 * COLS, WIDE))
    for i in range(ROWS):
        dkv = a_ref[i].astype(F32) + b_ref[i].astype(F32) + c_ref[i].astype(F32)
        u = jnp.where(lane2 < DH, u_ref[i] * SCALE, u_ref[i])
        u = pltpu.roll(u, 2 * DH, 1)
        near_ref[i] = jnp.where(lane < 2 * DH, dkv, u[:COLS])
        far_ref[i] = jnp.where(lane < 2 * DH, pltpu.roll(dkv, 2 * DH, 1), u[COLS:])


def gather_parts(u, a, b, c):
    shape = jax.ShapeDtypeStruct((ROWS, COLS, WIDE), F32)
    return pl.pallas_call(
        gather_kernel,
        out_shape=[shape, shape],
        compiler_params=params(),
        cost_estimate=cost(0.5),
        name="gather_parts",
    )(u, a, b, c)


def finish_kernel(first_ref, second_ref, last_ref, keep_ref, send_ref):
    yl = lax.axis_index("yl")
    lane = lanes((COLS, WIDE))

    def write(first_out, second_out):
        for i in range(ROWS):
            last = last_ref[i].astype(F32)
            first = first_ref[i] + jnp.where(lane < 2 * DH, last, 0.0)
            second = second_ref[i] + jnp.where(lane < 2 * DH, pltpu.roll(last, 2 * DH, 1), 0.0)
            first_out[i] = first.astype(first_out.dtype)
            second_out[i] = second.astype(second_out.dtype)

    @pl.when(yl == 0)
    def _():
        write(keep_ref, send_ref)

    @pl.when(yl != 0)
    def _():
        write(send_ref, keep_ref)


def finish(first, second, last):
    shape = (ROWS, COLS, WIDE)
    return pl.pallas_call(
        finish_kernel,
        out_shape=[jax.ShapeDtypeStruct(shape, F32), jax.ShapeDtypeStruct(shape, BF16)],
        compiler_params=params(),
        cost_estimate=cost(0.8),
        name="finish",
    )(first, second, last)


def product(value, gate, w, h):
    flat = (ROWS * COLS, WIDE)
    value = value.reshape(flat).astype(F32)
    value = jnp.where(lanes(flat) < 3 * DH, value, value * gate.reshape(flat)).astype(BF16)
    weight = jnp.where(h == 0, head_weight(w, 0).astype(F32), head_weight(w, 1).astype(F32))
    return mm(value, weight.astype(BF16), NT)


def keep_kernel(keep_ref, gate_ref, w_ref, out_ref):
    yl = lax.axis_index("yl")
    out_ref[...] = product(keep_ref[...], gate_ref[...], w_ref[...], yl)


def keep_product(keep, gate, w):
    return pl.pallas_call(
        keep_kernel,
        out_shape=jax.ShapeDtypeStruct((ROWS * COLS, WIDE), F32),
        compiler_params=params(),
        cost_estimate=cost(0.5),
        name="keep_product",
    )(keep, gate, w)


def table_kernel(parts_ref, bias_ref):
    for h in range(H):
        bias_ref[h] = sum(parts_ref[n * H + h].astype(F32) for n in range(8))


def table_sum(parts):
    return pl.pallas_call(
        table_kernel,
        out_shape=jax.ShapeDtypeStruct((H, COLS, COLS), F32),
        compiler_params=params(),
        cost_estimate=cost(0.3),
        name="table_sum",
    )(parts)


def output_kernel(kept_ref, recv_ref, gate_ref, w_ref, out_ref):
    yl = lax.axis_index("yl")
    other = product(recv_ref[...], gate_ref[...], w_ref[...], 1 - yl)
    out_ref[...] = (kept_ref[...] + other).astype(BF16).reshape(ROWS, COLS, WIDE)


def output(kept, recv, gate, w):
    return pl.pallas_call(
        output_kernel,
        out_shape=BLOCK,
        compiler_params=params(),
        cost_estimate=cost(0.5),
        name="output",
    )(kept, recv, gate, w)


def shift(value, step):
    return lax.ppermute(value, "z", [(z, (z + step) % RING) for z in range(RING)])


def swap(value, axis):
    return lax.ppermute(value, axis, [(0, 1), (1, 0)])


def added(*parts):
    return sum(part.astype(F32) for part in parts).astype(BF16)


def body(pair, w_qkvg, w_out, bias, chain_lengths, d_pair_out):
    peers = ("yh", "x", "yl")
    oth = swap(bias, "core")
    mine, other, lift, bias = project(chain_lengths, bias, pair, d_pair_out, w_qkvg, w_out)
    recv = swap(other, "yl")
    wanted = want(bias, oth)
    everything = lax.all_to_all(wanted, peers, 0, 0, tiled=True)
    kv, q, da, qt, dat = pack(mine, recv, wanted)
    kvs = [kv] + [None] * (RING - 1)
    kvs[2] = shift(kv, -2)
    kvs[7] = shift(kv, 1)
    kvs[1] = shift(kv, -1)
    kvs[3] = shift(kvs[2], -1)
    kvs[6] = shift(kvs[7], 1)
    kvs[4] = shift(kvs[3], -1)
    kvs[5] = shift(kvs[6], 1)
    bias_near, bias_late = bias_tables(lift, everything)
    e, *state = early(q, da, bias_near, kvs)
    u, dot, factor, *late, t_late = turn(q, da, qt, dat, bias_late, state, kvs)
    late = dict(zip(LATE, late))
    up, down = shift(late[4], 1), shift(late[5], -1)
    u, near, t_near = backward(NEAR, late[4], da, qt, dat, (u, dot, factor), e, kvs, 3.0)
    parts = {**near, **late}
    keep_table, send_table = split_tables(t_near, t_late)
    recv_table = swap(send_table, "core")
    up = shift(added(up, parts[3]), 1)
    down = shift(added(down, parts[6]), -1)
    step = shift(parts[1], 1)
    up, down, summed = relay(up, parts[2], down, parts[7], keep_table, recv_table)
    up, down = shift(up, 2), shift(down, -1)
    tables = lax.all_to_all(summed.reshape(16, COLS, COLS), peers, 0, 0, tiled=True)
    gmine, gother = slopes(step, pair, d_pair_out, w_qkvg, w_out)
    first, second = gather_parts(u, parts[0], step, down)
    keep, send = finish(first, second, up)
    recv = swap(send, "yl")
    kept = keep_product(keep, gmine, w_qkvg)
    return output(kept, recv, gother, w_qkvg), table_sum(tables)


def solution(mesh):
    split = Mesh(mesh.devices.reshape(2, 4, 2, 2, RING), ("yh", "x", "core", "yl", "z"))
    row, col = ("yh", "x", "core"), ("yl", "z")
    in_specs = (P(row, col, None), P(), P(), P(None, col, row), P(), P(row, col, None))
    out_specs = (P(row, col, None), P(None, col, row))
    return jax.shard_map(body, mesh=split, in_specs=in_specs, out_specs=out_specs, check_vma=False)
```

```python
import functools
import math

import jax
import jax.numpy as jnp
from jax import lax
from jax.experimental import pallas as pl
from jax.experimental.pallas import tpu as pltpu
from jax.sharding import Mesh, PartitionSpec as P

H = 2
DH = 32
CHAINS = 8
SCALE = 1.0 / math.sqrt(DH)
MASKED_SCORE = -1e30
F32 = jnp.float32
BF16 = jnp.bfloat16

ROWS = 6
COLS = 96
RING = 8
HALF = RING * COLS
KEYS = 2 * HALF
WIDE = 128
NEAR = (0, 1, 7, 2, 6)
LATE = (3, 4, 5)
NC, NL = (2 * len(group) * COLS for group in (NEAR, LATE))


NT = (((1,), (1,)), ((), ()))
NN = (((1,), (0,)), ((), ()))
TN = (((0,), (0,)), ((), ()))


def mm(a, b, dims):
    return lax.dot_general(a, b, dims, preferred_element_type=F32)


def params(limit=32 << 20):
    return pltpu.CompilerParams(vmem_limit_bytes=limit)


def cost(us):
    return pl.CostEstimate(flops=0, bytes_accessed=int(us * 1e5), transcendentals=0)


def lanes(shape):
    return lax.broadcasted_iota(jnp.int32, shape, len(shape) - 1)


def head_weight(w, h):
    parts = [w[:, (part * H + h) * DH : (part * H + h + 1) * DH] for part in (1, 2, 0, 3)]
    return jnp.concatenate(parts, axis=1)


def project_kernel(
    len_hbm, bias_hbm, pair_hbm, grad_hbm, w_hbm, wout_hbm,
    mine_ref, other_ref, lift_ref, bias_ref,
    len_s, pair_s, grad_s, w_s, wout_s, sem,
):
    yl = lax.axis_index("yl")
    pairs = (
        (len_hbm, len_s), (w_hbm, w_s), (wout_hbm, wout_s),
        (pair_hbm, pair_s), (grad_hbm, grad_s), (bias_hbm, bias_ref),
    )
    copies = [pltpu.make_async_copy(a, b, sem.at[n]) for n, (a, b) in enumerate(pairs)]
    for copy in copies:
        copy.start()
    copies[0].wait()
    for c in range(CHAINS):
        for half in range(2):
            position = lanes((1, COLS)) + half * COLS
            lift_ref[2 * c + half] = jnp.where(position < len_s[c], 0.0, MASKED_SCORE)
    for copy in copies[1:]:
        copy.wait()
    pair = pair_s[...].reshape(ROWS * COLS, WIDE)
    grad = grad_s[...].reshape(ROWS * COLS, WIDE)
    w = w_s[...]
    wout = wout_s[...]
    lane = lanes((ROWS * COLS, WIDE))
    for h in range(H):
        proj = mm(pair, head_weight(w, h), NN)
        rows = jnp.concatenate(
            [jnp.zeros((WIDE - DH, WIDE), BF16), wout[h * DH : (h + 1) * DH]], axis=0
        )
        d_out = mm(grad, rows, NT)
        gate = jax.nn.sigmoid(proj)
        payload = jnp.where(
            lane < 2 * DH, proj, jnp.where(lane < 3 * DH, proj * SCALE, d_out * gate)
        )
        payload = payload.astype(BF16).reshape(ROWS, COLS, WIDE)

        @pl.when(yl == h)
        def _():
            mine_ref[...] = payload

        @pl.when(yl != h)
        def _():
            other_ref[...] = payload


def project(chain_lengths, bias, pair, grad, w, wout):
    shape = (ROWS, COLS, WIDE)
    arrays = (chain_lengths, bias, pair, grad, w, wout)
    arrays = [pltpu.with_memory_space_constraint(array, pltpu.HBM) for array in arrays]
    return pl.pallas_call(
        project_kernel,
        in_specs=[pl.BlockSpec(memory_space=pltpu.HBM)] * 6,
        out_shape=[
            jax.ShapeDtypeStruct(shape, BF16),
            jax.ShapeDtypeStruct(shape, BF16),
            jax.ShapeDtypeStruct((2 * CHAINS, 1, COLS), F32),
            jax.ShapeDtypeStruct(bias.shape, BF16),
        ],
        scratch_shapes=[
            pltpu.SMEM((CHAINS,), jnp.int32),
            pltpu.VMEM(shape, BF16),
            pltpu.VMEM(shape, BF16),
            pltpu.VMEM(w.shape, BF16),
            pltpu.VMEM(wout.shape, BF16),
            pltpu.SemaphoreType.DMA((6,)),
        ],
        compiler_params=params(),
        cost_estimate=cost(2.0),
        name="project",
    )(*arrays)


def slope_kernel(
    _, pair_hbm, grad_hbm, w_hbm, wout_hbm, gmine_ref, gother_ref, pair_s, grad_s, w_s, wout_s, sem
):
    yl = lax.axis_index("yl")
    pairs = ((w_hbm, w_s), (wout_hbm, wout_s), (pair_hbm, pair_s), (grad_hbm, grad_s))
    copies = [pltpu.make_async_copy(a, b, sem.at[n]) for n, (a, b) in enumerate(pairs)]
    for copy in copies:
        copy.start()
    for copy in copies:
        copy.wait()
    pair = pair_s[...].reshape(ROWS * COLS, WIDE)
    grad = grad_s[...].reshape(ROWS * COLS, WIDE)
    zeros = jnp.zeros((WIDE - DH, WIDE), BF16)
    for h in range(H):
        gate = jax.nn.sigmoid(mm(pair, head_weight(w_s[...], h), NN))
        rows = jnp.concatenate([zeros, wout_s[h * DH : (h + 1) * DH]], axis=0)
        g = mm(grad, rows, NT) * gate * (1.0 - gate)

        @pl.when(yl == h)
        def _():
            gmine_ref[...] = g.reshape(ROWS, COLS, WIDE)

        @pl.when(yl != h)
        def _():
            gother_ref[...] = g.reshape(ROWS, COLS, WIDE)


def slopes(after, pair, grad, w, wout):
    shape = (ROWS, COLS, WIDE)
    arrays = [pltpu.with_memory_space_constraint(array, pltpu.HBM) for array in (pair, grad, w, wout)]
    return pl.pallas_call(
        slope_kernel,
        in_specs=[pl.BlockSpec(memory_space=pl.ANY)] + [pl.BlockSpec(memory_space=pltpu.HBM)] * 4,
        out_shape=[jax.ShapeDtypeStruct(shape, F32)] * 2,
        scratch_shapes=[
            pltpu.VMEM(shape, BF16),
            pltpu.VMEM(shape, BF16),
            pltpu.VMEM(w.shape, BF16),
            pltpu.VMEM(wout.shape, BF16),
            pltpu.SemaphoreType.DMA((4,)),
        ],
        compiler_params=params(),
        cost_estimate=cost(2.0),
        name="slopes",
    )(after, *arrays)


def pack_kernel(mine_ref, recv_ref, _, kv_ref, q_ref, da_ref, qt_ref, dat_ref):
    yl = lax.axis_index("yl")
    lane = lanes((COLS, WIDE))

    def write(i, a, b):
        a, b = a.astype(F32), b.astype(F32)
        kv_ref[i] = jnp.where(lane < 2 * DH, a, pltpu.roll(b, 2 * DH, 1)).astype(BF16)
        for part, x in enumerate((a, b)):
            y = pltpu.roll(x, 2 * DH, 1)
            rows = slice(part * COLS, (part + 1) * COLS)
            q_ref[i, rows] = jnp.where(lane < DH, y, 0.0).astype(BF16)
            da_ref[i, rows] = jnp.where((lane >= DH) & (lane < 2 * DH), y, 0.0).astype(BF16)
        turned = jnp.concatenate([a, b], axis=0).T
        qt_ref[i] = turned[2 * DH : 3 * DH].astype(BF16)
        dat_ref[i] = turned[3 * DH :].astype(BF16)

    for i in range(ROWS):

        @pl.when(yl == 0)
        def _():
            write(i, mine_ref[i], recv_ref[i])

        @pl.when(yl != 0)
        def _():
            write(i, recv_ref[i], mine_ref[i])


BLOCK = jax.ShapeDtypeStruct((ROWS, COLS, WIDE), BF16)
STATE = jax.ShapeDtypeStruct((ROWS, 2 * COLS, WIDE), F32)


def pack(mine, recv, after):
    both = jax.ShapeDtypeStruct((ROWS, 2 * COLS, WIDE), BF16)
    turned = jax.ShapeDtypeStruct((ROWS, DH, 2 * COLS), BF16)
    return pl.pallas_call(
        pack_kernel,
        in_specs=[pl.BlockSpec(memory_space=pltpu.VMEM)] * 2 + [pl.BlockSpec(memory_space=pl.ANY)],
        out_shape=[BLOCK, both, both, turned, turned],
        compiler_params=params(),
        cost_estimate=cost(0.6),
        name="pack",
    )(mine, recv, after)


EXCHANGE = jax.ShapeDtypeStruct((16, 2, COLS, COLS), BF16)


def want_kernel(own_ref, oth_ref, out_ref):
    core = lax.axis_index("core")
    for h in range(H):
        for n in range(8):
            out_ref[n * H + h, core] = own_ref[h]
            out_ref[n * H + h, 1 - core] = oth_ref[h]


def want(own, oth):
    return pl.pallas_call(
        want_kernel,
        out_shape=EXCHANGE,
        compiler_params=params(),
        cost_estimate=cost(0.4),
        name="want",
    )(own, oth)


def bias_kernel(lift_ref, all_ref, near_ref, late_ref):
    z = lax.axis_index("z")
    for group, out_ref in ((NEAR, near_ref), (LATE, late_ref)):
        for n, r in enumerate(group):
            at = lax.rem(z + r, RING)
            x, odd = at // 2, lax.rem(at, 2)
            for yh in range(2):
                start = (yh * len(group) + n) * COLS
                lift = lift_ref[yh * CHAINS + at]
                for yl in range(2):
                    rows = slice(yl * COLS, (yl + 1) * COLS)
                    block = all_ref[(yh * 4 + x) * 2 + yl, odd].astype(F32)
                    out_ref[rows, start : start + COLS] = block + lift


def bias_tables(lift, everything):
    return pl.pallas_call(
        bias_kernel,
        out_shape=[
            jax.ShapeDtypeStruct((2 * COLS, NC), F32),
            jax.ShapeDtypeStruct((2 * COLS, NL), F32),
        ],
        compiler_params=params(),
        cost_estimate=cost(0.5),
        name="bias_tables",
    )(lift, everything)


def join_kernel(block_ref, _, out_ref):
    out_ref[...] = block_ref[...]


def join(block, after):
    return pl.pallas_call(
        join_kernel,
        in_specs=[pl.BlockSpec(memory_space=pltpu.VMEM), pl.BlockSpec(memory_space=pl.ANY)],
        out_shape=BLOCK,
        compiler_params=params(),
        cost_estimate=cost(0.2),
        name="join",
    )(block, after)


def stack(refs, i):
    one = jnp.concatenate([ref[i] for ref in refs], axis=0)
    moved = pltpu.roll(one.astype(F32), 2 * DH, 1).astype(BF16)
    return jnp.concatenate([one, moved], axis=0)


def key_gradients(qt, dat, low, p_low, dkv_refs, i):
    dk = mm(qt, low, NN)
    dv = mm(dat, p_low, NN)
    half = dk.shape[1] // 2
    dkv = jnp.concatenate([dk[:, :half], dv[:, :half], dk[:, half:], dv[:, half:]], axis=0).T
    for n, ref in enumerate(dkv_refs):
        ref[i] = dkv[n * COLS : (n + 1) * COLS].astype(BF16)


def wide(value):
    return jnp.broadcast_to(value, (2 * COLS, WIDE))


def across(value, like):
    width = like.shape[1]
    return jnp.concatenate([value] * pl.cdiv(width, WIDE), axis=1)[:, :width]


def add_row(table_ref, i, value):
    if i == 0:
        table_ref[...] = value
    else:
        table_ref[...] += value


def staged(first, second, third):
    held = first(0)
    for i in range(ROWS):
        done = second(i, *held)
        if i + 1 < ROWS:
            following = first(i + 1)
        third(i, *done)
        held = following


def early_kernel(q_ref, da_ref, bias_ref, *refs):
    n = len(NEAR)
    kv_refs, (e_ref, acc_ref, total_ref, mass_ref, top_ref) = refs[:n], refs[n:]

    def scores(i):
        kv = stack(kv_refs, i)
        return kv, mm(q_ref[i], kv, NT) + bias_ref[...], mm(da_ref[i], kv, NT)

    def weigh(i, kv, s, w):
        top = jnp.max(s, axis=1, keepdims=True)
        e = jnp.exp(s - top)
        low = e.astype(BF16)
        e_ref[i] = low
        total_ref[i] = wide(jnp.sum(e, axis=1, keepdims=True))
        mass_ref[i] = wide(jnp.sum(e * w, axis=1, keepdims=True))
        top_ref[i] = wide(top)
        return kv, low

    def gather(i, kv, low):
        acc_ref[i] = mm(low, kv, NN)

    staged(scores, weigh, gather)


def early(q, da, bias, kvs):
    return pl.pallas_call(
        early_kernel,
        out_shape=[jax.ShapeDtypeStruct((ROWS, 2 * COLS, NC), BF16)] + [STATE] * 4,
        compiler_params=params(),
        cost_estimate=cost(4.0),
        name="early",
    )(q, da, bias, *[kvs[r] for r in NEAR])


def turn_kernel(
    q_ref, da_ref, qt_ref, dat_ref, bias_ref, acc_ref, total_ref, mass_ref, top_ref, *refs
):
    n = len(LATE)
    kv_refs, (u_ref, dot_ref, factor_ref) = refs[:n], refs[n : n + 3]
    dkv_refs, table_ref = refs[n + 3 : 2 * n + 3], refs[-1]
    lane = lanes((2 * COLS, WIDE))

    def scores(i):
        kv = stack(kv_refs, i)
        return kv, mm(q_ref[i], kv, NT) + bias_ref[...], mm(da_ref[i], kv, NT)

    def weigh(i, kv, s, w):
        old = top_ref[i]
        top = jnp.maximum(jnp.max(s, axis=1, keepdims=True), old)
        fade = jnp.exp(old - top)
        e = jnp.exp(s - across(top, s))
        inverse = 1.0 / (jnp.sum(e, axis=1, keepdims=True) + total_ref[i] * fade)
        factor = fade * inverse
        dot = (jnp.sum(e * w, axis=1, keepdims=True) + mass_ref[i] * fade) * inverse
        factor_ref[i] = factor
        dot_ref[i] = dot
        p = e * across(inverse, e)
        d = p * (w - across(dot, p))
        add_row(table_ref, i, d)
        return kv, p.astype(BF16), d.astype(BF16), factor

    def gather(i, kv, p_low, low, factor):
        key_gradients(qt_ref[i], dat_ref[i], low, p_low, dkv_refs, i)
        acc = mm(p_low, kv, NN) + acc_ref[i] * factor
        u_ref[i] = jnp.where(lane < DH, mm(low, kv, NN), acc)

    staged(scores, weigh, gather)


def turn(q, da, qt, dat, bias, state, kvs):
    return pl.pallas_call(
        turn_kernel,
        out_shape=[STATE] * 3
        + [BLOCK] * len(LATE)
        + [jax.ShapeDtypeStruct((2 * COLS, NL), F32)],
        compiler_params=params(),
        cost_estimate=cost(3.0),
        name="turn",
    )(q, da, qt, dat, bias, *state, *[kvs[r] for r in LATE])


def backward_kernel(
    group, _, da_ref, qt_ref, dat_ref, part_ref, dot_ref, factor_ref, e_ref, *refs
):
    n = len(group)
    kv_refs, u_ref, dkv_refs, table_ref = refs[:n], refs[n], refs[n + 1 : 2 * n + 1], refs[2 * n + 1]
    lane = lanes((2 * COLS, WIDE))

    def scores(i):
        kv = stack(kv_refs, i)
        return kv, mm(da_ref[i], kv, NT)

    def weigh(i, kv, w):
        p = e_ref[i].astype(F32)
        p = p * across(factor_ref[i], p)
        d = p * (w - across(dot_ref[i], p))
        add_row(table_ref, i, d)
        return kv, p.astype(BF16), d.astype(BF16)

    def gather(i, kv, p_low, low):
        u = part_ref[i]
        u_ref[i] = jnp.where(lane < DH, u + mm(low, kv, NN), u)
        key_gradients(qt_ref[i], dat_ref[i], low, p_low, dkv_refs, i)

    staged(scores, weigh, gather)


def backward(group, after, da, qt, dat, state, e, kvs, time):
    n = len(group)
    out = pl.pallas_call(
        functools.partial(backward_kernel, group),
        in_specs=[pl.BlockSpec(memory_space=pl.ANY)]
        + [pl.BlockSpec(memory_space=pltpu.VMEM)] * (7 + n),
        out_shape=[STATE]
        + [BLOCK] * n
        + [jax.ShapeDtypeStruct((2 * COLS, 2 * n * COLS), F32)],
        compiler_params=params(),
        cost_estimate=cost(time),
        name="backward",
    )(after, da, qt, dat, *state, e, *[kvs[r] for r in group])
    return out[0], dict(zip(group, out[1 : n + 1])), out[-1]


def split_kernel(near_ref, late_ref, keep_ref, send_ref):
    core = lax.axis_index("core")
    z = lax.axis_index("z")

    def write(even_ref, odd_ref):
        for group, table in ((NEAR, near_ref), (LATE, late_ref)):
            for m, r in enumerate(group):
                ref = odd_ref if r % 2 else even_ref
                x = lax.rem(z + r, RING) // 2
                for yh in range(2):
                    start = (yh * len(group) + m) * COLS
                    for yl in range(2):
                        piece = table[yl * COLS : (yl + 1) * COLS, start : start + COLS]
                        ref[yh, x, yl] = piece.astype(ref.dtype)

    @pl.when(lax.rem(z + core, 2) == 0)
    def _():
        write(keep_ref, send_ref)

    @pl.when(lax.rem(z + core, 2) != 0)
    def _():
        write(send_ref, keep_ref)


def split_tables(near, late):
    blocks = (2, 4, 2, COLS, COLS)
    return pl.pallas_call(
        split_kernel,
        out_shape=[jax.ShapeDtypeStruct(blocks, F32), jax.ShapeDtypeStruct(blocks, BF16)],
        compiler_params=params(),
        cost_estimate=cost(1.0),
        name="split_tables",
    )(near, late)


def relay_kernel(
    down_ref, far_ref, keep_ref, recv_ref, down_out, summed_ref
):
    down_out[...] = (down_ref[...].astype(F32) + far_ref[...].astype(F32)).astype(BF16)
    summed_ref[...] = (keep_ref[...] + recv_ref[...].astype(F32)).astype(BF16)


def relay(down, far, keep, recv):
    return pl.pallas_call(
        relay_kernel,
        out_shape=[BLOCK, jax.ShapeDtypeStruct(keep.shape, BF16)],
        compiler_params=params(),
        cost_estimate=cost(0.8),
        name="relay",
    )(down, far, keep, recv)


def gather_kernel(u_ref, a_ref, b_ref, c_ref, near_ref, far_ref):
    lane = lanes((COLS, WIDE))
    lane2 = lanes((2 * COLS, WIDE))
    for i in range(ROWS):
        dkv = a_ref[i].astype(F32) + b_ref[i].astype(F32) + c_ref[i].astype(F32)
        u = jnp.where(lane2 < DH, u_ref[i] * SCALE, u_ref[i])
        u = pltpu.roll(u, 2 * DH, 1)
        near_ref[i] = jnp.where(lane < 2 * DH, dkv, u[:COLS])
        far_ref[i] = jnp.where(lane < 2 * DH, pltpu.roll(dkv, 2 * DH, 1), u[COLS:])


def gather_parts(u, a, b, c):
    shape = jax.ShapeDtypeStruct((ROWS, COLS, WIDE), F32)
    return pl.pallas_call(
        gather_kernel,
        out_shape=[shape, shape],
        compiler_params=params(),
        cost_estimate=cost(0.5),
        name="gather_parts",
    )(u, a, b, c)


def finish_kernel(first_ref, second_ref, last_ref, keep_ref, send_ref):
    yl = lax.axis_index("yl")
    lane = lanes((COLS, WIDE))

    def write(first_out, second_out):
        for i in range(ROWS):
            last = last_ref[i].astype(F32)
            first = first_ref[i] + jnp.where(lane < 2 * DH, last, 0.0)
            second = second_ref[i] + jnp.where(lane < 2 * DH, pltpu.roll(last, 2 * DH, 1), 0.0)
            first_out[i] = first.astype(first_out.dtype)
            second_out[i] = second.astype(second_out.dtype)

    @pl.when(yl == 0)
    def _():
        write(keep_ref, send_ref)

    @pl.when(yl != 0)
    def _():
        write(send_ref, keep_ref)


def finish(first, second, last):
    shape = (ROWS, COLS, WIDE)
    return pl.pallas_call(
        finish_kernel,
        out_shape=[jax.ShapeDtypeStruct(shape, F32), jax.ShapeDtypeStruct(shape, BF16)],
        compiler_params=params(),
        cost_estimate=cost(0.8),
        name="finish",
    )(first, second, last)


def product(value, gate, w, h):
    flat = (ROWS * COLS, WIDE)
    value = value.reshape(flat).astype(F32)
    value = jnp.where(lanes(flat) < 3 * DH, value, value * gate.reshape(flat)).astype(BF16)
    weight = jnp.where(h == 0, head_weight(w, 0).astype(F32), head_weight(w, 1).astype(F32))
    return mm(value, weight.astype(BF16), NT)


def keep_kernel(keep_ref, gate_ref, w_ref, out_ref):
    yl = lax.axis_index("yl")
    out_ref[...] = product(keep_ref[...], gate_ref[...], w_ref[...], yl)


def keep_product(keep, gate, w):
    return pl.pallas_call(
        keep_kernel,
        out_shape=jax.ShapeDtypeStruct((ROWS * COLS, WIDE), F32),
        compiler_params=params(),
        cost_estimate=cost(0.5),
        name="keep_product",
    )(keep, gate, w)


def table_kernel(parts_ref, bias_ref):
    for h in range(H):
        bias_ref[h] = sum(parts_ref[n * H + h].astype(F32) for n in range(8))


def table_sum(parts):
    return pl.pallas_call(
        table_kernel,
        out_shape=jax.ShapeDtypeStruct((H, COLS, COLS), F32),
        compiler_params=params(),
        cost_estimate=cost(0.3),
        name="table_sum",
    )(parts)


def output_kernel(kept_ref, recv_ref, gate_ref, w_ref, out_ref):
    yl = lax.axis_index("yl")
    other = product(recv_ref[...], gate_ref[...], w_ref[...], 1 - yl)
    out_ref[...] = (kept_ref[...] + other).astype(BF16).reshape(ROWS, COLS, WIDE)


def output(kept, recv, gate, w):
    return pl.pallas_call(
        output_kernel,
        out_shape=BLOCK,
        compiler_params=params(),
        cost_estimate=cost(0.5),
        name="output",
    )(kept, recv, gate, w)


def shift(value, step):
    return lax.ppermute(value, "z", [(z, (z + step) % RING) for z in range(RING)])


def swap(value, axis):
    return lax.ppermute(value, axis, [(0, 1), (1, 0)])


def added(*parts):
    return sum(part.astype(F32) for part in parts).astype(BF16)


def body(pair, w_qkvg, w_out, bias, chain_lengths, d_pair_out):
    peers = ("yh", "x", "yl")
    oth = swap(bias, "core")
    mine, other, lift, bias = project(chain_lengths, bias, pair, d_pair_out, w_qkvg, w_out)
    recv = swap(other, "yl")
    wanted = want(bias, oth)
    everything = lax.all_to_all(wanted, peers, 0, 0, tiled=True)
    kv, q, da, qt, dat = pack(mine, recv, wanted)
    kvs = [kv] + [None] * (RING - 1)
    kvs[2] = shift(kv, -2)
    kvs[7] = shift(kv, 1)
    kvs[1] = shift(kv, -1)
    kvs[3] = shift(kvs[2], -1)
    kvs[6] = shift(kvs[7], 1)
    kvs[4] = shift(kvs[3], -1)
    kvs[5] = shift(kvs[6], 1)
    bias_near, bias_late = bias_tables(lift, everything)
    e, *state = early(q, da, bias_near, kvs)
    u, dot, factor, *late, t_late = turn(q, da, qt, dat, bias_late, state, kvs)
    late = dict(zip(LATE, late))
    up = shift(late[4], 1)
    u, near, t_near = backward(NEAR, late[4], da, qt, dat, (u, dot, factor), e, kvs, 3.0)
    parts = {**near, **late}
    down = shift(join(late[5], t_near), -1)
    keep_table, send_table = split_tables(t_near, t_late)
    recv_table = swap(send_table, "core")
    up = shift(added(up, parts[3]), 1)
    down = shift(added(down, parts[6]), -1)
    step = shift(parts[1], 1)
    up = shift(added(up, parts[2]), 2)
    down, summed = relay(down, parts[7], keep_table, recv_table)
    down = shift(down, -1)
    tables = lax.all_to_all(summed.reshape(16, COLS, COLS), peers, 0, 0, tiled=True)
    gmine, gother = slopes(step, pair, d_pair_out, w_qkvg, w_out)
    first, second = gather_parts(u, parts[0], step, down)
    keep, send = finish(first, second, up)
    recv = swap(send, "yl")
    kept = keep_product(keep, gmine, w_qkvg)
    return output(kept, recv, gother, w_qkvg), table_sum(tables)


def solution(mesh):
    split = Mesh(mesh.devices.reshape(2, 4, 2, 2, RING), ("yh", "x", "core", "yl", "z"))
    row, col = ("yh", "x", "core"), ("yl", "z")
    in_specs = (P(row, col, None), P(), P(), P(None, col, row), P(), P(row, col, None))
    out_specs = (P(row, col, None), P(None, col, row))
    return jax.shard_map(body, mesh=split, in_specs=in_specs, out_specs=out_specs, check_vma=False)
```

```python
import functools
import math

import jax
import jax.numpy as jnp
from jax import lax
from jax.experimental import pallas as pl
from jax.experimental.pallas import tpu as pltpu
from jax.sharding import Mesh, PartitionSpec as P

H = 2
DH = 32
CHAINS = 8
SCALE = 1.0 / math.sqrt(DH)
MASKED_SCORE = -1e30
F32 = jnp.float32
BF16 = jnp.bfloat16

ROWS = 6
COLS = 96
RING = 8
HALF = RING * COLS
KEYS = 2 * HALF
WIDE = 128
NEAR = (0, 1, 7, 2, 6)
LATE = (3, 4, 5)
NC, NL = (2 * len(group) * COLS for group in (NEAR, LATE))


NT = (((1,), (1,)), ((), ()))
NN = (((1,), (0,)), ((), ()))
TN = (((0,), (0,)), ((), ()))


def mm(a, b, dims):
    return lax.dot_general(a, b, dims, preferred_element_type=F32)


def params(limit=32 << 20):
    return pltpu.CompilerParams(vmem_limit_bytes=limit)


def cost(us):
    return pl.CostEstimate(flops=0, bytes_accessed=int(us * 1e5), transcendentals=0)


def lanes(shape):
    return lax.broadcasted_iota(jnp.int32, shape, len(shape) - 1)


def head_weight(w, h):
    parts = [w[:, (part * H + h) * DH : (part * H + h + 1) * DH] for part in (1, 2, 0, 3)]
    return jnp.concatenate(parts, axis=1)


def project_kernel(
    len_hbm, bias_hbm, pair_hbm, grad_hbm, w_hbm, wout_hbm,
    mine_ref, other_ref, lift_ref, bias_ref,
    len_s, pair_s, grad_s, w_s, wout_s, sem,
):
    yl = lax.axis_index("yl")
    pairs = (
        (len_hbm, len_s), (w_hbm, w_s), (wout_hbm, wout_s),
        (pair_hbm, pair_s), (grad_hbm, grad_s), (bias_hbm, bias_ref),
    )
    copies = [pltpu.make_async_copy(a, b, sem.at[n]) for n, (a, b) in enumerate(pairs)]
    for copy in copies:
        copy.start()
    copies[0].wait()
    for c in range(CHAINS):
        for half in range(2):
            position = lanes((1, COLS)) + half * COLS
            lift_ref[2 * c + half] = jnp.where(position < len_s[c], 0.0, MASKED_SCORE)
    for copy in copies[1:]:
        copy.wait()
    pair = pair_s[...].reshape(ROWS * COLS, WIDE)
    grad = grad_s[...].reshape(ROWS * COLS, WIDE)
    w = w_s[...]
    wout = wout_s[...]
    lane = lanes((ROWS * COLS, WIDE))
    for h in range(H):
        proj = mm(pair, head_weight(w, h), NN)
        rows = jnp.concatenate(
            [jnp.zeros((WIDE - DH, WIDE), BF16), wout[h * DH : (h + 1) * DH]], axis=0
        )
        d_out = mm(grad, rows, NT)
        gate = jax.nn.sigmoid(proj)
        payload = jnp.where(
            lane < 2 * DH, proj, jnp.where(lane < 3 * DH, proj * SCALE, d_out * gate)
        )
        payload = payload.astype(BF16).reshape(ROWS, COLS, WIDE)

        @pl.when(yl == h)
        def _():
            mine_ref[...] = payload

        @pl.when(yl != h)
        def _():
            other_ref[...] = payload


def project(chain_lengths, bias, pair, grad, w, wout):
    shape = (ROWS, COLS, WIDE)
    arrays = (chain_lengths, bias, pair, grad, w, wout)
    arrays = [pltpu.with_memory_space_constraint(array, pltpu.HBM) for array in arrays]
    return pl.pallas_call(
        project_kernel,
        in_specs=[pl.BlockSpec(memory_space=pltpu.HBM)] * 6,
        out_shape=[
            jax.ShapeDtypeStruct(shape, BF16),
            jax.ShapeDtypeStruct(shape, BF16),
            jax.ShapeDtypeStruct((2 * CHAINS, 1, COLS), F32),
            jax.ShapeDtypeStruct(bias.shape, BF16),
        ],
        scratch_shapes=[
            pltpu.SMEM((CHAINS,), jnp.int32),
            pltpu.VMEM(shape, BF16),
            pltpu.VMEM(shape, BF16),
            pltpu.VMEM(w.shape, BF16),
            pltpu.VMEM(wout.shape, BF16),
            pltpu.SemaphoreType.DMA((6,)),
        ],
        compiler_params=params(),
        cost_estimate=cost(2.0),
        name="project",
    )(*arrays)


def slope_kernel(
    _, pair_hbm, grad_hbm, w_hbm, wout_hbm, gmine_ref, gother_ref, pair_s, grad_s, w_s, wout_s, sem
):
    yl = lax.axis_index("yl")
    pairs = ((w_hbm, w_s), (wout_hbm, wout_s), (pair_hbm, pair_s), (grad_hbm, grad_s))
    copies = [pltpu.make_async_copy(a, b, sem.at[n]) for n, (a, b) in enumerate(pairs)]
    for copy in copies:
        copy.start()
    for copy in copies:
        copy.wait()
    pair = pair_s[...].reshape(ROWS * COLS, WIDE)
    grad = grad_s[...].reshape(ROWS * COLS, WIDE)
    zeros = jnp.zeros((WIDE - DH, WIDE), BF16)
    for h in range(H):
        gate = jax.nn.sigmoid(mm(pair, head_weight(w_s[...], h), NN))
        rows = jnp.concatenate([zeros, wout_s[h * DH : (h + 1) * DH]], axis=0)
        g = mm(grad, rows, NT) * gate * (1.0 - gate)

        @pl.when(yl == h)
        def _():
            gmine_ref[...] = g.reshape(ROWS, COLS, WIDE)

        @pl.when(yl != h)
        def _():
            gother_ref[...] = g.reshape(ROWS, COLS, WIDE)


def slopes(after, pair, grad, w, wout):
    shape = (ROWS, COLS, WIDE)
    arrays = [pltpu.with_memory_space_constraint(array, pltpu.HBM) for array in (pair, grad, w, wout)]
    return pl.pallas_call(
        slope_kernel,
        in_specs=[pl.BlockSpec(memory_space=pl.ANY)] + [pl.BlockSpec(memory_space=pltpu.HBM)] * 4,
        out_shape=[jax.ShapeDtypeStruct(shape, F32)] * 2,
        scratch_shapes=[
            pltpu.VMEM(shape, BF16),
            pltpu.VMEM(shape, BF16),
            pltpu.VMEM(w.shape, BF16),
            pltpu.VMEM(wout.shape, BF16),
            pltpu.SemaphoreType.DMA((4,)),
        ],
        compiler_params=params(),
        cost_estimate=cost(2.0),
        name="slopes",
    )(after, *arrays)


def pack_kernel(mine_ref, recv_ref, _, kv_ref, q_ref, da_ref, qt_ref, dat_ref):
    yl = lax.axis_index("yl")
    lane = lanes((COLS, WIDE))

    def write(i, a, b):
        a, b = a.astype(F32), b.astype(F32)
        kv_ref[i] = jnp.where(lane < 2 * DH, a, pltpu.roll(b, 2 * DH, 1)).astype(BF16)
        for part, x in enumerate((a, b)):
            y = pltpu.roll(x, 2 * DH, 1)
            rows = slice(part * COLS, (part + 1) * COLS)
            q_ref[i, rows] = jnp.where(lane < DH, y, 0.0).astype(BF16)
            da_ref[i, rows] = jnp.where((lane >= DH) & (lane < 2 * DH), y, 0.0).astype(BF16)
        turned = jnp.concatenate([a, b], axis=0).T
        qt_ref[i] = turned[2 * DH : 3 * DH].astype(BF16)
        dat_ref[i] = turned[3 * DH :].astype(BF16)

    for i in range(ROWS):

        @pl.when(yl == 0)
        def _():
            write(i, mine_ref[i], recv_ref[i])

        @pl.when(yl != 0)
        def _():
            write(i, recv_ref[i], mine_ref[i])


BLOCK = jax.ShapeDtypeStruct((ROWS, COLS, WIDE), BF16)
STATE = jax.ShapeDtypeStruct((ROWS, 2 * COLS, WIDE), F32)


def pack(mine, recv, after):
    both = jax.ShapeDtypeStruct((ROWS, 2 * COLS, WIDE), BF16)
    turned = jax.ShapeDtypeStruct((ROWS, DH, 2 * COLS), BF16)
    return pl.pallas_call(
        pack_kernel,
        in_specs=[pl.BlockSpec(memory_space=pltpu.VMEM)] * 2 + [pl.BlockSpec(memory_space=pl.ANY)],
        out_shape=[BLOCK, both, both, turned, turned],
        compiler_params=params(),
        cost_estimate=cost(0.6),
        name="pack",
    )(mine, recv, after)


EXCHANGE = jax.ShapeDtypeStruct((16, 2, COLS, COLS), BF16)


def want_kernel(own_ref, oth_ref, out_ref):
    core = lax.axis_index("core")
    for h in range(H):
        for n in range(8):
            out_ref[n * H + h, core] = own_ref[h]
            out_ref[n * H + h, 1 - core] = oth_ref[h]


def want(own, oth):
    return pl.pallas_call(
        want_kernel,
        out_shape=EXCHANGE,
        compiler_params=params(),
        cost_estimate=cost(0.4),
        name="want",
    )(own, oth)


def bias_kernel(lift_ref, all_ref, near_ref, late_ref):
    z = lax.axis_index("z")
    for group, out_ref in ((NEAR, near_ref), (LATE, late_ref)):
        for n, r in enumerate(group):
            at = lax.rem(z + r, RING)
            x, odd = at // 2, lax.rem(at, 2)
            for yh in range(2):
                start = (yh * len(group) + n) * COLS
                lift = lift_ref[yh * CHAINS + at]
                for yl in range(2):
                    rows = slice(yl * COLS, (yl + 1) * COLS)
                    block = all_ref[(yh * 4 + x) * 2 + yl, odd].astype(F32)
                    out_ref[rows, start : start + COLS] = block + lift


def bias_tables(lift, everything):
    return pl.pallas_call(
        bias_kernel,
        out_shape=[
            jax.ShapeDtypeStruct((2 * COLS, NC), F32),
            jax.ShapeDtypeStruct((2 * COLS, NL), F32),
        ],
        compiler_params=params(),
        cost_estimate=cost(0.5),
        name="bias_tables",
    )(lift, everything)


def join_kernel(block_ref, _, out_ref):
    out_ref[...] = block_ref[...]


def join(block, after):
    return pl.pallas_call(
        join_kernel,
        in_specs=[pl.BlockSpec(memory_space=pltpu.VMEM), pl.BlockSpec(memory_space=pl.ANY)],
        out_shape=BLOCK,
        compiler_params=params(),
        cost_estimate=cost(0.2),
        name="join",
    )(block, after)


def stack(refs, i):
    one = jnp.concatenate([ref[i] for ref in refs], axis=0)
    moved = pltpu.roll(one.astype(F32), 2 * DH, 1).astype(BF16)
    return jnp.concatenate([one, moved], axis=0)


def key_gradients(qt, dat, low, p_low, dkv_refs, i):
    dk = mm(qt, low, NN)
    dv = mm(dat, p_low, NN)
    half = dk.shape[1] // 2
    dkv = jnp.concatenate([dk[:, :half], dv[:, :half], dk[:, half:], dv[:, half:]], axis=0).T
    for n, ref in enumerate(dkv_refs):
        ref[i] = dkv[n * COLS : (n + 1) * COLS].astype(BF16)


def wide(value):
    return jnp.broadcast_to(value, (2 * COLS, WIDE))


def across(value, like):
    width = like.shape[1]
    return jnp.concatenate([value] * pl.cdiv(width, WIDE), axis=1)[:, :width]


def add_row(table_ref, i, value):
    if i == 0:
        table_ref[...] = value
    else:
        table_ref[...] += value


def staged(first, second, third):
    held = first(0)
    for i in range(ROWS):
        done = second(i, *held)
        if i + 1 < ROWS:
            following = first(i + 1)
        third(i, *done)
        held = following


def early_kernel(q_ref, da_ref, bias_ref, *refs):
    n = len(NEAR)
    kv_refs, (e_ref, acc_ref, total_ref, mass_ref, top_ref) = refs[:n], refs[n:]

    def scores(i):
        kv = stack(kv_refs, i)
        return kv, mm(q_ref[i], kv, NT) + bias_ref[...], mm(da_ref[i], kv, NT)

    def weigh(i, kv, s, w):
        top = jnp.max(s, axis=1, keepdims=True)
        e = jnp.exp(s - top)
        low = e.astype(BF16)
        e_ref[i] = low
        total_ref[i] = wide(jnp.sum(e, axis=1, keepdims=True))
        mass_ref[i] = wide(jnp.sum(e * w, axis=1, keepdims=True))
        top_ref[i] = wide(top)
        return kv, low

    def gather(i, kv, low):
        acc_ref[i] = mm(low, kv, NN)

    staged(scores, weigh, gather)


def early(q, da, bias, kvs):
    return pl.pallas_call(
        early_kernel,
        out_shape=[jax.ShapeDtypeStruct((ROWS, 2 * COLS, NC), BF16)] + [STATE] * 4,
        compiler_params=params(),
        cost_estimate=cost(4.0),
        name="early",
    )(q, da, bias, *[kvs[r] for r in NEAR])


def turn_kernel(
    q_ref, da_ref, qt_ref, dat_ref, bias_ref, acc_ref, total_ref, mass_ref, top_ref, *refs
):
    n = len(LATE)
    kv_refs, (u_ref, dot_ref, factor_ref) = refs[:n], refs[n : n + 3]
    dkv_refs, table_ref = refs[n + 3 : 2 * n + 3], refs[-1]
    lane = lanes((2 * COLS, WIDE))

    def scores(i):
        kv = stack(kv_refs, i)
        return kv, mm(q_ref[i], kv, NT) + bias_ref[...], mm(da_ref[i], kv, NT)

    def weigh(i, kv, s, w):
        old = top_ref[i]
        top = jnp.maximum(jnp.max(s, axis=1, keepdims=True), old)
        fade = jnp.exp(old - top)
        e = jnp.exp(s - across(top, s))
        inverse = 1.0 / (jnp.sum(e, axis=1, keepdims=True) + total_ref[i] * fade)
        factor = fade * inverse
        dot = (jnp.sum(e * w, axis=1, keepdims=True) + mass_ref[i] * fade) * inverse
        factor_ref[i] = factor
        dot_ref[i] = dot
        p = e * across(inverse, e)
        d = p * (w - across(dot, p))
        add_row(table_ref, i, d)
        return kv, p.astype(BF16), d.astype(BF16), factor

    def gather(i, kv, p_low, low, factor):
        key_gradients(qt_ref[i], dat_ref[i], low, p_low, dkv_refs, i)
        acc = mm(p_low, kv, NN) + acc_ref[i] * factor
        u_ref[i] = jnp.where(lane < DH, mm(low, kv, NN), acc)

    staged(scores, weigh, gather)


def turn(q, da, qt, dat, bias, state, kvs):
    return pl.pallas_call(
        turn_kernel,
        out_shape=[STATE] * 3
        + [BLOCK] * len(LATE)
        + [jax.ShapeDtypeStruct((2 * COLS, NL), F32)],
        compiler_params=params(),
        cost_estimate=cost(3.0),
        name="turn",
    )(q, da, qt, dat, bias, *state, *[kvs[r] for r in LATE])


def backward_kernel(
    group, _, da_ref, qt_ref, dat_ref, part_ref, dot_ref, factor_ref, e_ref, *refs
):
    n = len(group)
    kv_refs, u_ref, dkv_refs, table_ref = refs[:n], refs[n], refs[n + 1 : 2 * n + 1], refs[2 * n + 1]
    lane = lanes((2 * COLS, WIDE))

    def scores(i):
        kv = stack(kv_refs, i)
        return kv, mm(da_ref[i], kv, NT)

    def weigh(i, kv, w):
        p = e_ref[i].astype(F32)
        p = p * across(factor_ref[i], p)
        d = p * (w - across(dot_ref[i], p))
        add_row(table_ref, i, d)
        return kv, p.astype(BF16), d.astype(BF16)

    def gather(i, kv, p_low, low):
        u = part_ref[i]
        u_ref[i] = jnp.where(lane < DH, u + mm(low, kv, NN), u)
        key_gradients(qt_ref[i], dat_ref[i], low, p_low, dkv_refs, i)

    staged(scores, weigh, gather)


def backward(group, after, da, qt, dat, state, e, kvs, time):
    n = len(group)
    out = pl.pallas_call(
        functools.partial(backward_kernel, group),
        in_specs=[pl.BlockSpec(memory_space=pl.ANY)]
        + [pl.BlockSpec(memory_space=pltpu.VMEM)] * (7 + n),
        out_shape=[STATE]
        + [BLOCK] * n
        + [jax.ShapeDtypeStruct((2 * COLS, 2 * n * COLS), F32)],
        compiler_params=params(),
        cost_estimate=cost(time),
        name="backward",
    )(after, da, qt, dat, *state, e, *[kvs[r] for r in group])
    return out[0], dict(zip(group, out[1 : n + 1])), out[-1]


def split_kernel(near_ref, late_ref, keep_ref, send_ref):
    core = lax.axis_index("core")
    z = lax.axis_index("z")

    def write(even_ref, odd_ref):
        for group, table in ((NEAR, near_ref), (LATE, late_ref)):
            for m, r in enumerate(group):
                ref = odd_ref if r % 2 else even_ref
                x = lax.rem(z + r, RING) // 2
                for yh in range(2):
                    start = (yh * len(group) + m) * COLS
                    for yl in range(2):
                        piece = table[yl * COLS : (yl + 1) * COLS, start : start + COLS]
                        ref[yh, x, yl] = piece.astype(ref.dtype)

    @pl.when(lax.rem(z + core, 2) == 0)
    def _():
        write(keep_ref, send_ref)

    @pl.when(lax.rem(z + core, 2) != 0)
    def _():
        write(send_ref, keep_ref)


def split_tables(near, late):
    blocks = (2, 4, 2, COLS, COLS)
    return pl.pallas_call(
        split_kernel,
        out_shape=[jax.ShapeDtypeStruct(blocks, F32), jax.ShapeDtypeStruct(blocks, BF16)],
        compiler_params=params(),
        cost_estimate=cost(1.0),
        name="split_tables",
    )(near, late)


def relay_kernel(
    down_ref, far_ref, keep_ref, recv_ref, down_out, summed_ref
):
    down_out[...] = (down_ref[...].astype(F32) + far_ref[...].astype(F32)).astype(BF16)
    summed_ref[...] = (keep_ref[...] + recv_ref[...].astype(F32)).astype(BF16)


def relay(down, far, keep, recv):
    return pl.pallas_call(
        relay_kernel,
        out_shape=[BLOCK, jax.ShapeDtypeStruct(keep.shape, BF16)],
        compiler_params=params(),
        cost_estimate=cost(0.8),
        name="relay",
    )(down, far, keep, recv)


def gather_kernel(u_ref, a_ref, b_ref, c_ref, near_ref, far_ref):
    lane = lanes((COLS, WIDE))
    lane2 = lanes((2 * COLS, WIDE))
    for i in range(ROWS):
        dkv = a_ref[i].astype(F32) + b_ref[i].astype(F32) + c_ref[i].astype(F32)
        u = jnp.where(lane2 < DH, u_ref[i] * SCALE, u_ref[i])
        u = pltpu.roll(u, 2 * DH, 1)
        near_ref[i] = jnp.where(lane < 2 * DH, dkv, u[:COLS])
        far_ref[i] = jnp.where(lane < 2 * DH, pltpu.roll(dkv, 2 * DH, 1), u[COLS:])


def gather_parts(u, a, b, c):
    shape = jax.ShapeDtypeStruct((ROWS, COLS, WIDE), F32)
    return pl.pallas_call(
        gather_kernel,
        out_shape=[shape, shape],
        compiler_params=params(),
        cost_estimate=cost(0.5),
        name="gather_parts",
    )(u, a, b, c)


def finish_kernel(first_ref, second_ref, last_ref, keep_ref, send_ref):
    yl = lax.axis_index("yl")
    lane = lanes((COLS, WIDE))

    def write(first_out, second_out):
        for i in range(ROWS):
            last = last_ref[i].astype(F32)
            first = first_ref[i] + jnp.where(lane < 2 * DH, last, 0.0)
            second = second_ref[i] + jnp.where(lane < 2 * DH, pltpu.roll(last, 2 * DH, 1), 0.0)
            first_out[i] = first.astype(first_out.dtype)
            second_out[i] = second.astype(second_out.dtype)

    @pl.when(yl == 0)
    def _():
        write(keep_ref, send_ref)

    @pl.when(yl != 0)
    def _():
        write(send_ref, keep_ref)


def finish(first, second, last):
    shape = (ROWS, COLS, WIDE)
    return pl.pallas_call(
        finish_kernel,
        out_shape=[jax.ShapeDtypeStruct(shape, F32), jax.ShapeDtypeStruct(shape, BF16)],
        compiler_params=params(),
        cost_estimate=cost(0.8),
        name="finish",
    )(first, second, last)


def product(value, gate, w, h):
    flat = (ROWS * COLS, WIDE)
    value = value.reshape(flat).astype(F32)
    value = jnp.where(lanes(flat) < 3 * DH, value, value * gate.reshape(flat)).astype(BF16)
    weight = jnp.where(h == 0, head_weight(w, 0).astype(F32), head_weight(w, 1).astype(F32))
    return mm(value, weight.astype(BF16), NT)


def keep_kernel(keep_ref, gate_ref, w_ref, out_ref):
    yl = lax.axis_index("yl")
    out_ref[...] = product(keep_ref[...], gate_ref[...], w_ref[...], yl)


def keep_product(keep, gate, w):
    return pl.pallas_call(
        keep_kernel,
        out_shape=jax.ShapeDtypeStruct((ROWS * COLS, WIDE), F32),
        compiler_params=params(),
        cost_estimate=cost(0.5),
        name="keep_product",
    )(keep, gate, w)


def output_kernel(kept_ref, recv_ref, gate_ref, w_ref, parts_ref, out_ref, bias_ref):
    yl = lax.axis_index("yl")
    for h in range(H):
        bias_ref[h] = sum(parts_ref[n * H + h].astype(F32) for n in range(8))
    other = product(recv_ref[...], gate_ref[...], w_ref[...], 1 - yl)
    out_ref[...] = (kept_ref[...] + other).astype(BF16).reshape(ROWS, COLS, WIDE)


def output(kept, recv, gate, w, parts):
    return pl.pallas_call(
        output_kernel,
        out_shape=[BLOCK, jax.ShapeDtypeStruct((H, COLS, COLS), F32)],
        compiler_params=params(),
        cost_estimate=cost(0.5),
        name="output",
    )(kept, recv, gate, w, parts)


def shift(value, step):
    return lax.ppermute(value, "z", [(z, (z + step) % RING) for z in range(RING)])


def swap(value, axis):
    return lax.ppermute(value, axis, [(0, 1), (1, 0)])


def added(*parts):
    return sum(part.astype(F32) for part in parts).astype(BF16)


def body(pair, w_qkvg, w_out, bias, chain_lengths, d_pair_out):
    peers = ("yh", "x", "yl")
    oth = swap(bias, "core")
    mine, other, lift, bias = project(chain_lengths, bias, pair, d_pair_out, w_qkvg, w_out)
    recv = swap(other, "yl")
    wanted = want(bias, oth)
    everything = lax.all_to_all(wanted, peers, 0, 0, tiled=True)
    kv, q, da, qt, dat = pack(mine, recv, wanted)
    kvs = [kv] + [None] * (RING - 1)
    kvs[2] = shift(kv, -2)
    kvs[7] = shift(kv, 1)
    kvs[1] = shift(kv, -1)
    kvs[3] = shift(kvs[2], -1)
    kvs[6] = shift(kvs[7], 1)
    kvs[4] = shift(kvs[3], -1)
    kvs[5] = shift(kvs[6], 1)
    bias_near, bias_late = bias_tables(lift, everything)
    e, *state = early(q, da, bias_near, kvs)
    u, dot, factor, *late, t_late = turn(q, da, qt, dat, bias_late, state, kvs)
    late = dict(zip(LATE, late))
    up = shift(late[4], 1)
    u, near, t_near = backward(NEAR, late[4], da, qt, dat, (u, dot, factor), e, kvs, 3.0)
    parts = {**near, **late}
    down = shift(join(late[5], t_near), -1)
    keep_table, send_table = split_tables(t_near, t_late)
    recv_table = swap(send_table, "core")
    up = shift(added(up, parts[3]), 1)
    down = shift(added(down, parts[6]), -1)
    step = shift(parts[1], 1)
    up = shift(added(up, parts[2]), 2)
    down, summed = relay(down, parts[7], keep_table, recv_table)
    down = shift(down, -1)
    tables = lax.all_to_all(summed.reshape(16, COLS, COLS), peers, 0, 0, tiled=True)
    gmine, gother = slopes(step, pair, d_pair_out, w_qkvg, w_out)
    first, second = gather_parts(u, parts[0], step, down)
    keep, send = finish(first, second, up)
    recv = swap(send, "yl")
    kept = keep_product(keep, gmine, w_qkvg)
    return output(kept, recv, gother, w_qkvg, tables)


def solution(mesh):
    split = Mesh(mesh.devices.reshape(2, 4, 2, 2, RING), ("yh", "x", "core", "yl", "z"))
    row, col = ("yh", "x", "core"), ("yl", "z")
    in_specs = (P(row, col, None), P(), P(), P(None, col, row), P(), P(row, col, None))
    out_specs = (P(row, col, None), P(None, col, row))
    return jax.shard_map(body, mesh=split, in_specs=in_specs, out_specs=out_specs, check_vma=False)
```
